32 devices in a mesh: ctx: 2 (over y), row: 8 (over z, x), col: 2 (over core).
Axes of the slice: x: 2, y: 2, z: 4, core: 2. Of those that a mesh axis runs over, the one named last changes fastest.
Arguments:
- context_map: bfloat16 [128, 512, 256], P(('ctx', 'row'), 'col'), parts along dimension 0, may hold values from -6 to 6
- norm_gains: float32 [3, 256], replicated, may hold values from 0.25 to 1.75
- conv_biases: float32 [3, 256], replicated, may hold values from -3 to 3
- conv_weights: bfloat16 [3, 3, 3, 256, 256], replicated, may hold values from -0.125 to 0.125
Outputs:
- refined: bfloat16 [128, 512, 256], P(('ctx', 'row'), 'col'), parts along dimension 0
The draws below stay inside these ranges and needn't reach their ends.
There are 2 independent parts, one for each index of `ctx`. The reference program is written for one: setup_inputs(seed, part) draws one part's arguments, and reference() takes and returns one part's arrays. A program takes and returns all parts, laid end to end along the dimension named above; an argument that names none is the same for every part. Nothing has to cross between parts.
All inputs are finite; a program needn't handle non-finite values.
Results may differ from the reference program's by a relative error of at most 0.0052.
Values may be sent and summed in bfloat16 or wider, within the bound.
No kernel may reach another device: no remote copies, remote signals or barrier semaphores. Data moves between devices by JAX's collectives and lax.ppermute only.
A program may use at most 64 MiB of HBM per device.

```python
import jax
import jax.numpy as jnp
from jax import lax

C = 256
H = 64
W = 512


def block_levels(key, dims, shards, low, top_value):
    gain, own = 1.0, jax.random.fold_in(key, 6)
    for axis_at, shards_of in shards:
        heights = jnp.exp(jax.random.uniform(jax.random.fold_in(own, axis_at), (shards_of,), jnp.float32, low / len(shards), top_value / len(shards)))
        gain = gain * jnp.repeat(heights, dims[axis_at] // shards_of).reshape([-1 if axis == axis_at else 1 for axis in range(len(dims))])
    return gain


def gaussian(rng, dims, spread, bound, split=(), dtype=jnp.bfloat16):
    level = block_levels(rng, dims, split, -0.22, 0.18) if split else 1.0
    array = jax.random.normal(rng, dims, jnp.float32) * spread * level
    return jnp.minimum(jnp.maximum(array, -bound), bound).astype(dtype)


def setup_inputs(seed: int = 0, part: int = 0) -> dict:
    key_list = jax.random.split(jax.random.key(seed), 5)
    part_splits = jax.random.split(jax.random.fold_in(key_list[4], part), 5)
    context_map = gaussian(part_splits[0], (H, W, C), 1.0, 6.0, ((0, 8), (1, 2)))
    norm_gains = jnp.clip(1.0 + 0.15 * jax.random.normal(key_list[1], (3, C), jnp.float32), 0.25, 1.75)
    conv_biases = gaussian(key_list[2], (3, C), 0.5, 3.0, (), jnp.float32)
    conv_weights = gaussian(key_list[3], (3, 3, 3, C, C), (9 * C) ** -0.5, 0.125)
    return dict(context_map=context_map, norm_gains=norm_gains, conv_biases=conv_biases, conv_weights=conv_weights)


def one_layer(current, weight, gain_row, bias_row, dilation):
    values = current.astype(jnp.float32)
    centred = values - lax.optimization_barrier(jnp.mean(values, axis=-1, keepdims=True))
    variance = lax.optimization_barrier(jnp.mean(centred * centred, axis=-1, keepdims=True))
    normed = (centred * lax.rsqrt(variance + 1e-05) * gain_row).astype(jnp.bfloat16)
    normed = lax.optimization_barrier(normed)
    response = lax.conv_general_dilated(normed.astype(jnp.float32)[None], weight.astype(jnp.float32), (1, 1), ((dilation, dilation), (dilation, dilation)), rhs_dilation=(dilation, dilation), dimension_numbers=('NHWC', 'HWIO', 'NHWC'), precision=lax.Precision.HIGHEST)[0]
    return (values + jnp.maximum(response + bias_row, 0.0)).astype(jnp.bfloat16)

def reference(context_map, norm_gains, conv_biases, conv_weights):
    current = context_map
    for position, dilation in ((0, 4), (1, 32), (2, 64)):
        current = one_layer(current, conv_weights[position], norm_gains[position], conv_biases[position], dilation)
    return current
```

```python
import functools

import jax
import jax.numpy as jnp
from jax import lax
from jax.experimental import pallas as pl
from jax.experimental.pallas import tpu as pltpu
from jax.sharding import PartitionSpec as P

epsilon = 1e-05
dilations = (4, 32, 64)
lane_pad = 16
vmem_limit = 40 * 1024 * 1024


def extended(x, sides, width):
    for axis, dim in sides:
        size, length = (lax.axis_size(axis), x.shape[dim])
        up = [(i, (i + 1) % size) for i in range(size - 1)]
        down = [(j, i) for i, j in up]
        last = lax.slice_in_dim(x, length - width, length, axis=dim)
        first = lax.slice_in_dim(x, 0, width, axis=dim)
        before = lax.ppermute(last, axis, up)
        after = lax.ppermute(first, axis, down)
        x = jnp.concatenate([before, x, after], axis=dim)
    return x


def normalize(current, gain_row):
    values = current.astype(jnp.float32)
    centred = values - jnp.mean(values, axis=-1, keepdims=True)
    variance = jnp.mean(centred * centred, axis=-1, keepdims=True)
    return (centred * lax.rsqrt(variance + epsilon) * gain_row).astype(jnp.bfloat16)


def convolve(padded, kernel, row_step, col_step, out_rows, out_cols):
    channels = padded.shape[2]
    tap_list = []
    for tap_row in range(3):
        for tap_col in range(3):
            tap_list.append(
                lax.slice(
                    padded,
                    (tap_row * row_step, tap_col * col_step, 0),
                    (tap_row * row_step + out_rows, tap_col * col_step + out_cols, channels),
                )
            )
    stacked = jnp.concatenate(tap_list, axis=2).reshape(out_rows * out_cols, 9 * channels)
    product = jnp.dot(
        stacked, kernel.reshape(9 * channels, kernel.shape[3]), preferred_element_type=jnp.float32
    )
    return product.reshape(out_rows, out_cols, kernel.shape[3])


def update(current, response, bias_row):
    return (current.astype(jnp.float32) + jnp.maximum(response + bias_row, 0.0)).astype(
        jnp.bfloat16
    )


def by_classes(context_map, norm_gains, conv_biases, conv_weights):
    tile_rows, tile_cols, channels = context_map.shape
    normed = normalize(context_map, norm_gains[0])
    padded = extended(normed, (("row", 0), ("col", 1)), 4)
    current = update(
        context_map, convolve(padded, conv_weights[0], 4, 4, tile_rows, tile_cols), conv_biases[0]
    )
    class_count = lax.axis_size("row") // tile_rows
    sub_cols = tile_cols // class_count
    outgoing = (
        current.reshape(tile_rows, sub_cols, class_count, channels)
        .transpose(0, 2, 1, 3)
        .reshape(tile_rows * class_count, sub_cols, channels)
    )
    grouped = lax.all_to_all(outgoing, "row", split_axis=0, concat_axis=0, tiled=True)
    sub_rows = grouped.shape[0]
    for position, dilation in ((1, 32), (2, 64)):
        normed = normalize(grouped, norm_gains[position])
        row_gap = dilation // tile_rows
        col_gap = dilation // class_count
        with_sides = extended(normed, (("col", 1),), col_gap)
        padded = jnp.pad(with_sides, ((row_gap, row_gap), (0, 0), (0, 0)))
        response = convolve(padded, conv_weights[position], row_gap, col_gap, sub_rows, sub_cols)
        grouped = update(grouped, response, conv_biases[position])
    returned = lax.all_to_all(grouped, "row", split_axis=0, concat_axis=0, tiled=True)
    return (
        returned.reshape(tile_rows, class_count, sub_cols, channels)
        .transpose(0, 2, 1, 3)
        .reshape(tile_rows, tile_cols, channels)
    )


def vmem_spec():
    return pl.BlockSpec(memory_space=pltpu.VMEM)


def smem_spec():
    return pl.BlockSpec(memory_space=pltpu.SMEM)


def kernel_call(body, out_shape, in_specs, scratch, flops, bytes_accessed):
    return pl.pallas_call(
        body,
        out_shape=out_shape,
        in_specs=in_specs,
        out_specs=jax.tree.map(lambda _: vmem_spec(), out_shape),
        scratch_shapes=scratch,
        compiler_params=pltpu.CompilerParams(vmem_limit_bytes=vmem_limit),
        cost_estimate=pl.CostEstimate(
            flops=flops, bytes_accessed=bytes_accessed, transcendentals=0
        ),
    )


def place(core, at_zero, at_one):
    return pl.multiple_of(jnp.where(core == 0, at_zero, at_one), lane_pad)


def first_layer_kernel(
    segments, zero_at, out_at, rows, width, core_ref, x_ref, gain_ref, bias_ref, w_ref, *rest
):
    parts, (next_ref, normed_ref, window, taps) = rest[:-4], rest[-4:]
    refs = (x_ref,) + tuple(parts)
    core = core_ref[0]
    half = rows // 2
    channels = x_ref.shape[2]
    gain = gain_ref[0:1, :]
    for which, source_row, window_row, count, source, target, columns in segments:
        src, dst = place(core, *source), place(core, *target)
        for r in range(count):
            window[window_row + r, pl.ds(dst, columns), :] = normalize(
                refs[which][source_row + r, pl.ds(src, columns), :], gain
            )
    if zero_at is not None:
        dst = place(core, *zero_at)
        for r in range(2 * rows):
            window[r, pl.ds(dst, lane_pad), :] = jnp.zeros((lane_pad, channels), jnp.bfloat16)
    step = dilations[0]
    for b in range(3):
        first = lane_pad + (b - 1) * step
        for r in range(2 * rows):
            taps[b, r] = window[r, first : first + width, :]
    stacked = jnp.concatenate(
        [
            taps[b, a * half : a * half + rows].reshape(rows * width, channels)
            for a in range(3)
            for b in range(3)
        ],
        axis=1,
    )
    response = jnp.dot(
        stacked, w_ref[...].reshape(9 * channels, channels), preferred_element_type=jnp.float32
    )
    out_col = place(core, *out_at)
    current = x_ref[:, pl.ds(out_col, width), :].reshape(rows * width, channels)
    result = update(current, response, bias_ref[0:1, :])
    next_ref[...] = result.reshape(rows, width, channels)
    normed_ref[...] = normalize(result, gain_ref[1:2, :]).reshape(rows, width, channels)


def first_layer(core, x, gains, biases, weights, parts, segments, zero_at, out_at, width):
    rows, _, channels = x.shape
    out = jax.ShapeDtypeStruct((rows, width, channels), x.dtype)
    cells = rows * width
    body = functools.partial(first_layer_kernel, segments, zero_at, out_at, rows, width)
    return kernel_call(
        body,
        (out, out),
        [smem_spec()] + [vmem_spec()] * (4 + len(parts)),
        [
            pltpu.VMEM((2 * rows, width + 2 * lane_pad, channels), x.dtype),
            pltpu.VMEM((3, 2 * rows, width, channels), x.dtype),
        ],
        18 * cells * channels * channels,
        9 * channels * channels * 2,
    )(core, x, gains, biases, weights, *parts)


def second_layer_kernel(
    strip,
    core_ref,
    gain_ref,
    bias_ref,
    w_ref,
    wx_ref,
    near_ref,
    mid_ref,
    far_ref,
    cnear_ref,
    cfar_ref,
    side_ref,
    near1_ref,
    mid1_ref,
    far1_ref,
    lows_ref,
    highs_ref,
    nlows_ref,
    nhighs_ref,
    acc_ref,
    mids_ref,
    own,
    other,
    x1,
):
    core = core_ref[0]
    step = dilations[1]
    rows, mid, channels = mid_ref.shape
    cols = 2 * strip + mid
    near_at, far_at = (cols - strip, 0), (0, cols - strip)
    dst = place(core, step + near_at[0], step + near_at[1])
    own[:, pl.ds(dst, strip), :] = near_ref[...]
    other[:, pl.ds(dst, strip), :] = cnear_ref[...]
    dst = place(core, *near_at)
    x1[:, pl.ds(dst, strip), :] = near1_ref[...]
    dst = place(core, step + far_at[0], step + far_at[1])
    own[:, pl.ds(dst, strip), :] = far_ref[...]
    other[:, pl.ds(dst, strip), :] = cfar_ref[...]
    dst = place(core, *far_at)
    x1[:, pl.ds(dst, strip), :] = far1_ref[...]
    own[:, step + strip : step + strip + mid, :] = mid_ref[...]
    other[:, step + strip : step + strip + mid, :] = jnp.zeros((rows, mid, channels), own.dtype)
    x1[:, strip : strip + mid, :] = mid1_ref[...]
    dst = place(core, step + cols, 0)
    own[:, pl.ds(dst, step), :] = side_ref[0:rows]
    other[:, pl.ds(dst, step), :] = side_ref[rows : 2 * rows]
    dst = place(core, 0, step + cols)
    own[:, pl.ds(dst, step), :] = jnp.zeros((rows, step, channels), own.dtype)
    other[:, pl.ds(dst, step), :] = jnp.zeros((rows, step, channels), own.dtype)
    edge = strip - step
    w_own = w_ref[...].reshape(3 * channels, channels)
    w_other = wx_ref[...].reshape(3 * channels, channels)
    weights = jnp.concatenate([w_own, w_other], axis=0)
    for first, width in ((0, edge), (edge, mid + 2 * step), (cols - edge, edge)):
        stacked = jnp.concatenate(
            [
                ref[:, first + b * step : first + b * step + width, :].reshape(
                    rows * width, channels
                )
                for ref in (own, other)
                for b in range(3)
            ],
            axis=1,
        )
        response = jnp.dot(stacked, weights, preferred_element_type=jnp.float32)
        current = x1[:, first : first + width, :]
        if first == edge:
            acc_ref[...] = response.reshape(rows, width, channels)
            mids_ref[...] = current
        else:
            result = update(
                current.reshape(rows * width, channels), response, bias_ref[1:2, :]
            )
            normed = normalize(result, gain_ref[2:3, :])
            result_ref, out_ref = (lows_ref, nlows_ref) if first == 0 else (highs_ref, nhighs_ref)
            result_ref[...] = result.reshape(rows, width, channels)
            out_ref[...] = normed.reshape(rows, width, channels)


def last_kernel(
    core_ref,
    gain_ref,
    bias_ref,
    wx_ref,
    w_ref,
    cmid_ref,
    acc_ref,
    mids_ref,
    lows_ref,
    highs_ref,
    nlows_ref,
    nhighs_ref,
    side_ref,
    out_ref,
    other,
    normed,
    x2,
):
    core = core_ref[0]
    rows, mid, channels = cmid_ref.shape
    edge = nlows_ref.shape[1]
    step, reach = dilations[1], dilations[2]
    width = mid + 2 * step
    cols = 2 * edge + width
    blank = jnp.zeros((rows, 2 * step, channels), other.dtype)
    other[:, 0 : 2 * step, :] = blank
    other[:, 2 * step + mid : 4 * step + mid, :] = blank
    other[:, 2 * step : 2 * step + mid, :] = cmid_ref[...]
    stacked = jnp.concatenate(
        [
            other[:, b * step : b * step + width, :].reshape(rows * width, channels)
            for b in range(3)
        ],
        axis=1,
    )
    response = acc_ref[...].reshape(rows * width, channels) + jnp.dot(
        stacked, wx_ref[...].reshape(3 * channels, channels), preferred_element_type=jnp.float32
    )
    result = update(
        mids_ref[...].reshape(rows * width, channels), response, bias_ref[1:2, :]
    )
    x2[:, 0:edge, :] = lows_ref[...]
    x2[:, edge : edge + width, :] = result.reshape(rows, width, channels)
    x2[:, edge + width : cols, :] = highs_ref[...]
    normed[:, reach : reach + edge, :] = nlows_ref[...]
    normed[:, reach + edge : reach + edge + width, :] = normalize(
        result, gain_ref[2:3, :]
    ).reshape(rows, width, channels)
    normed[:, reach + edge + width : reach + cols, :] = nhighs_ref[...]
    dst = place(core, reach + cols, 0)
    normed[:, pl.ds(dst, reach), :] = side_ref[...]
    dst = place(core, 0, reach + cols)
    normed[:, pl.ds(dst, reach), :] = jnp.zeros((rows, reach, channels), normed.dtype)
    stacked = jnp.concatenate(
        [
            normed[:, b * reach : b * reach + cols, :].reshape(rows * cols, channels)
            for b in range(3)
        ],
        axis=1,
    )
    response = jnp.dot(
        stacked, w_ref[...].reshape(3 * channels, channels), preferred_element_type=jnp.float32
    )
    out_ref[...] = update(
        x2[...].reshape(rows * cols, channels), response, bias_ref[2:3, :]
    ).reshape(rows, cols, channels)


def by_halves(context_map, norm_gains, conv_biases, conv_weights):
    rows, cols, channels = context_map.shape
    size = lax.axis_size("row")
    half = rows // 2
    strip = dilations[1] + dilations[2]
    mid = cols - 2 * strip
    pad = lane_pad
    core = lax.axis_index("col")
    upper_half = lax.axis_index("row") < size // 2
    core_array = jnp.full((1,), core, jnp.int32)
    swap = [(0, 1), (1, 0)]
    partner = [(i, (i + size // 2) % size) for i in range(size)]
    down = [(i, i + 1) for i in range(size - 1)]
    up = [(j, i) for i, j in down]

    def columns(x, at_zero, at_one, width):
        return lax.dynamic_slice_in_dim(x, jnp.where(core == 0, at_zero, at_one), width, axis=1)

    def halos(at_zero, at_one, width):
        part = columns(context_map, at_zero, at_one, width)
        return (
            lax.ppermute(part[rows - half :], "row", down),
            lax.ppermute(part[:half], "row", up),
        )

    wide = strip + pad
    near_at, far_at = (cols - strip, 0), (0, cols - strip)
    above_near, below_near = halos(cols - wide, 0, wide)
    above_far, below_far = halos(0, cols - wide, wide)
    above_mid, below_mid = halos(wide, wide, cols - 2 * wide)

    rim = jnp.concatenate(
        [
            columns(above_near, wide - pad, 0, pad),
            columns(context_map, cols - pad, 0, pad),
            columns(below_near, wide - pad, 0, pad),
        ],
        axis=0,
    )
    rim = lax.ppermute(rim, "col", swap)

    params = (norm_gains, conv_biases, conv_weights[0])
    near_segments = (
        (0, 0, half, rows, (cols - wide, 0), (0, pad), wide),
        (1, 0, 0, half, (0, 0), (0, pad), wide),
        (2, 0, half + rows, half, (0, 0), (0, pad), wide),
        (3, 0, 0, 2 * rows, (0, 0), (wide, 0), pad),
    )
    near1, near_n = first_layer(
        core_array, context_map, *params, (above_near, below_near, rim), near_segments, None,
        near_at, strip,
    )
    cross_near = lax.ppermute(near_n, "row", partner)
    far_segments = (
        (0, 0, half, rows, (0, cols - wide), (pad, 0), wide),
        (1, 0, 0, half, (0, 0), (pad, 0), wide),
        (2, 0, half + rows, half, (0, 0), (pad, 0), wide),
    )
    far1, far_n = first_layer(
        core_array, context_map, *params, (above_far, below_far), far_segments,
        (0, wide), far_at, strip,
    )
    cross_far = lax.ppermute(far_n, "row", partner)
    mid_segments = (
        (0, 0, half, rows, (strip - pad, strip - pad), (0, 0), mid + 2 * pad),
        (1, 0, 0, half, (0, 0), (2 * pad, 2 * pad), mid - 2 * pad),
        (2, 0, half + rows, half, (0, 0), (2 * pad, 2 * pad), mid - 2 * pad),
        (3, 0, 0, half, (wide - 2 * pad, 0), (0, mid), 2 * pad),
        (4, 0, half + rows, half, (wide - 2 * pad, 0), (0, mid), 2 * pad),
        (5, 0, 0, half, (0, wide - 2 * pad), (mid, 0), 2 * pad),
        (6, 0, half + rows, half, (0, wide - 2 * pad), (mid, 0), 2 * pad),
    )
    mid1, mid_n = first_layer(
        core_array, context_map, *params,
        (above_mid, below_mid, above_far, below_far, above_near, below_near), mid_segments,
        None, (strip, strip), mid,
    )
    cross_mid = lax.ppermute(mid_n, "row", partner)

    step, reach = dilations[1], dilations[2]
    side = jnp.concatenate(
        [columns(near_n, strip - step, 0, step), columns(cross_near, strip - step, 0, step)], axis=0
    )
    side = lax.ppermute(side, "col", swap)
    toward = lax.dynamic_index_in_dim(
        conv_weights[1], jnp.where(upper_half, 2, 0), axis=0, keepdims=False
    )
    edge = strip - step
    wider = mid + 2 * step
    kind = context_map.dtype
    edge_shape = jax.ShapeDtypeStruct((rows, edge, channels), kind)
    lows, highs, n_lows, n_highs, acc, mids = kernel_call(
        functools.partial(second_layer_kernel, strip),
        (
            edge_shape,
            edge_shape,
            edge_shape,
            edge_shape,
            jax.ShapeDtypeStruct((rows, wider, channels), jnp.float32),
            jax.ShapeDtypeStruct((rows, wider, channels), kind),
        ),
        [smem_spec()] + [vmem_spec()] * 13,
        [
            pltpu.VMEM((rows, cols + 2 * step, channels), kind),
            pltpu.VMEM((rows, cols + 2 * step, channels), kind),
            pltpu.VMEM((rows, cols, channels), kind),
        ],
        12 * rows * cols * channels * channels,
        6 * channels * channels * 2,
    )(
        core_array, norm_gains, conv_biases, conv_weights[1, 1], toward, near_n, mid_n, far_n,
        cross_near, cross_far, side, near1, mid1, far1,
    )
    last_side = lax.ppermute(jnp.where(core == 0, n_highs, n_lows), "col", swap)
    return kernel_call(
        last_kernel,
        jax.ShapeDtypeStruct(context_map.shape, kind),
        [smem_spec()] + [vmem_spec()] * 12,
        [
            pltpu.VMEM((rows, mid + 4 * step, channels), kind),
            pltpu.VMEM((rows, cols + 2 * reach, channels), kind),
            pltpu.VMEM((rows, cols, channels), kind),
        ],
        8 * rows * cols * channels * channels,
        3 * channels * channels * 2,
    )(
        core_array, norm_gains, conv_biases, toward, conv_weights[2, 1], cross_mid, acc, mids, lows,
        highs, n_lows, n_highs, last_side,
    )


def shards(context_map, *params):
    rows, cols, _ = context_map.shape
    map_rows = lax.axis_size("row") * rows
    strip = dilations[1] + dilations[2]
    if (
        map_rows == 2 * dilations[1]
        and map_rows <= dilations[2]
        and rows == 2 * dilations[0]
        and dilations[1] % rows == 0
        and lax.axis_size("col") == 2
        and cols >= 2 * strip + 3 * lane_pad
        and cols % lane_pad == 0
    ):
        return by_halves(context_map, *params)
    return by_classes(context_map, *params)


def solution(mesh):
    return jax.shard_map(
        shards,
        mesh=mesh,
        in_specs=(P(("ctx", "row"), "col", None), P(), P(), P()),
        out_specs=P(("ctx", "row"), "col", None),
        check_vma=False,
    )
```

```python
import functools

import jax
import jax.numpy as jnp
from jax import lax
from jax.experimental import pallas as pl
from jax.experimental.pallas import tpu as pltpu
from jax.sharding import PartitionSpec as P

epsilon = 1e-05
dilations = (4, 32, 64)
lane_pad = 16
vmem_limit = 40 * 1024 * 1024


def extended(x, sides, width):
    for axis, dim in sides:
        size, length = (lax.axis_size(axis), x.shape[dim])
        up = [(i, (i + 1) % size) for i in range(size - 1)]
        down = [(j, i) for i, j in up]
        last = lax.slice_in_dim(x, length - width, length, axis=dim)
        first = lax.slice_in_dim(x, 0, width, axis=dim)
        before = lax.ppermute(last, axis, up)
        after = lax.ppermute(first, axis, down)
        x = jnp.concatenate([before, x, after], axis=dim)
    return x


def normalize(current, gain_row):
    values = current.astype(jnp.float32)
    centred = values - jnp.mean(values, axis=-1, keepdims=True)
    variance = jnp.mean(centred * centred, axis=-1, keepdims=True)
    return (centred * lax.rsqrt(variance + epsilon) * gain_row).astype(jnp.bfloat16)


def convolve(padded, kernel, row_step, col_step, out_rows, out_cols):
    channels = padded.shape[2]
    tap_list = []
    for tap_row in range(3):
        for tap_col in range(3):
            tap_list.append(
                lax.slice(
                    padded,
                    (tap_row * row_step, tap_col * col_step, 0),
                    (tap_row * row_step + out_rows, tap_col * col_step + out_cols, channels),
                )
            )
    stacked = jnp.concatenate(tap_list, axis=2).reshape(out_rows * out_cols, 9 * channels)
    product = jnp.dot(
        stacked, kernel.reshape(9 * channels, kernel.shape[3]), preferred_element_type=jnp.float32
    )
    return product.reshape(out_rows, out_cols, kernel.shape[3])


def update(current, response, bias_row):
    return (current.astype(jnp.float32) + jnp.maximum(response + bias_row, 0.0)).astype(
        jnp.bfloat16
    )


def by_classes(context_map, norm_gains, conv_biases, conv_weights):
    tile_rows, tile_cols, channels = context_map.shape
    normed = normalize(context_map, norm_gains[0])
    padded = extended(normed, (("row", 0), ("col", 1)), 4)
    current = update(
        context_map, convolve(padded, conv_weights[0], 4, 4, tile_rows, tile_cols), conv_biases[0]
    )
    class_count = lax.axis_size("row") // tile_rows
    sub_cols = tile_cols // class_count
    outgoing = (
        current.reshape(tile_rows, sub_cols, class_count, channels)
        .transpose(0, 2, 1, 3)
        .reshape(tile_rows * class_count, sub_cols, channels)
    )
    grouped = lax.all_to_all(outgoing, "row", split_axis=0, concat_axis=0, tiled=True)
    sub_rows = grouped.shape[0]
    for position, dilation in ((1, 32), (2, 64)):
        normed = normalize(grouped, norm_gains[position])
        row_gap = dilation // tile_rows
        col_gap = dilation // class_count
        with_sides = extended(normed, (("col", 1),), col_gap)
        padded = jnp.pad(with_sides, ((row_gap, row_gap), (0, 0), (0, 0)))
        response = convolve(padded, conv_weights[position], row_gap, col_gap, sub_rows, sub_cols)
        grouped = update(grouped, response, conv_biases[position])
    returned = lax.all_to_all(grouped, "row", split_axis=0, concat_axis=0, tiled=True)
    return (
        returned.reshape(tile_rows, class_count, sub_cols, channels)
        .transpose(0, 2, 1, 3)
        .reshape(tile_rows, tile_cols, channels)
    )


def vmem_spec():
    return pl.BlockSpec(memory_space=pltpu.VMEM)


def smem_spec():
    return pl.BlockSpec(memory_space=pltpu.SMEM)


def kernel_call(body, out_shape, in_specs, scratch, flops, bytes_accessed):
    return pl.pallas_call(
        body,
        out_shape=out_shape,
        in_specs=in_specs,
        out_specs=jax.tree.map(lambda _: vmem_spec(), out_shape),
        scratch_shapes=scratch,
        compiler_params=pltpu.CompilerParams(vmem_limit_bytes=vmem_limit),
        cost_estimate=pl.CostEstimate(
            flops=flops, bytes_accessed=bytes_accessed, transcendentals=0
        ),
    )


def place(core, at_zero, at_one):
    return pl.multiple_of(jnp.where(core == 0, at_zero, at_one), lane_pad)


def guarded(flag_ref, condition, action):
    if condition is None:
        action()
    else:
        number, value = condition
        pl.when(flag_ref[number] == value)(action)


def copy_kernel(moves, inputs, flag_ref, *refs):
    sources, targets, sems = refs[:inputs], refs[inputs:-1], refs[-1]

    def descriptor(at):
        _, which, row, count, column, width, target, target_row = moves[at]
        return pltpu.make_async_copy(
            sources[which].at[pl.ds(row, count), pl.ds(place(flag_ref[0], *column), width)],
            targets[target].at[pl.ds(target_row, count)],
            sems.at[at],
        )

    for at, move in enumerate(moves):
        guarded(flag_ref, move[0], lambda at=at: descriptor(at).start())
    for at, move in enumerate(moves):
        guarded(flag_ref, move[0], lambda at=at: descriptor(at).wait())


def copies(flags, arrays, moves):
    channels, kind = arrays[0].shape[2], arrays[0].dtype
    shapes = {}
    for _, _, _, count, _, width, target, target_row in moves:
        height = max(target_row + count, shapes.get(target, (0, 0))[0])
        shapes[target] = (height, width)
    out = tuple(
        jax.ShapeDtypeStruct(shapes[target] + (channels,), kind) for target in range(len(shapes))
    )
    volume = sum(2 * height * width * channels * 2 for height, width in shapes.values())
    return pl.pallas_call(
        functools.partial(copy_kernel, moves, len(arrays)),
        out_shape=out,
        in_specs=[smem_spec()] + [pl.BlockSpec(memory_space=pl.ANY)] * len(arrays),
        out_specs=tuple(pl.BlockSpec(memory_space=pl.ANY) for _ in out),
        scratch_shapes=[pltpu.SemaphoreType.DMA((len(moves),))],
        cost_estimate=pl.CostEstimate(flops=0, bytes_accessed=volume, transcendentals=0),
    )(flags, *arrays)


def first_layer_kernel(segments, out_at, rows, width, flag_ref, gain_ref, bias_ref, w_ref, *rest):
    parts, (next_ref, normed_ref, window, taps) = rest[:-4], rest[-4:]
    core = flag_ref[0]
    half = rows // 2
    channels = window.shape[2]
    gain = gain_ref[0:1, :]

    def fill(which, source_row, window_row, count, source, target, columns):
        src, dst = place(core, *source), place(core, *target)
        for r in range(count):
            if which is None:
                values = jnp.zeros((columns, channels), window.dtype)
            else:
                values = normalize(
                    parts[which][source_row + r, pl.ds(src, columns), :], gain
                )
            window[window_row + r, pl.ds(dst, columns), :] = values

    for segment in segments:
        guarded(flag_ref, segment[0], functools.partial(fill, *segment[1:]))
    step = dilations[0]
    for b in range(3):
        first = lane_pad + (b - 1) * step
        for r in range(2 * rows):
            taps[b, r] = window[r, first : first + width, :]
    stacked = jnp.concatenate(
        [
            taps[b, a * half : a * half + rows].reshape(rows * width, channels)
            for a in range(3)
            for b in range(3)
        ],
        axis=1,
    )
    response = jnp.dot(
        stacked, w_ref[...].reshape(9 * channels, channels), preferred_element_type=jnp.float32
    )
    out_col = place(core, *out_at)
    current = parts[0][:, pl.ds(out_col, width), :].reshape(rows * width, channels)
    result = update(current, response, bias_ref[0:1, :])
    next_ref[...] = result.reshape(rows, width, channels)
    normed_ref[...] = normalize(result, gain_ref[1:2, :]).reshape(rows, width, channels)


def first_layer(flags, params, parts, segments, out_at, width):
    rows, _, channels = parts[0].shape
    kind = parts[0].dtype
    out = jax.ShapeDtypeStruct((rows, width, channels), kind)
    cells = rows * width
    return kernel_call(
        functools.partial(first_layer_kernel, segments, out_at, rows, width),
        (out, out),
        [smem_spec()] + [vmem_spec()] * (3 + len(parts)),
        [
            pltpu.VMEM((2 * rows, width + 2 * lane_pad, channels), kind),
            pltpu.VMEM((3, 2 * rows, width, channels), kind),
        ],
        18 * cells * channels * channels,
        9 * channels * channels * 2,
    )(flags, *params, *parts)


def second_layer_kernel(
    strip,
    flag_ref,
    gain_ref,
    bias_ref,
    w_ref,
    wx_ref,
    near_ref,
    mid_ref,
    far_ref,
    cnear_ref,
    cfar_ref,
    side_ref,
    near1_ref,
    mid1_ref,
    far1_ref,
    lows_ref,
    highs_ref,
    nlows_ref,
    nhighs_ref,
    nside_ref,
    acc_ref,
    mids_ref,
    own,
    other,
    x1,
):
    core = flag_ref[0]
    step = dilations[1]
    rows, mid, channels = mid_ref.shape
    cols = 2 * strip + mid
    near_at, far_at = (cols - strip, 0), (0, cols - strip)
    dst = place(core, step + near_at[0], step + near_at[1])
    own[:, pl.ds(dst, strip), :] = near_ref[...]
    other[:, pl.ds(dst, strip), :] = cnear_ref[...]
    dst = place(core, *near_at)
    x1[:, pl.ds(dst, strip), :] = near1_ref[...]
    dst = place(core, step + far_at[0], step + far_at[1])
    own[:, pl.ds(dst, strip), :] = far_ref[...]
    other[:, pl.ds(dst, strip), :] = cfar_ref[...]
    dst = place(core, *far_at)
    x1[:, pl.ds(dst, strip), :] = far1_ref[...]
    own[:, step + strip : step + strip + mid, :] = mid_ref[...]
    other[:, step + strip : step + strip + mid, :] = jnp.zeros((rows, mid, channels), own.dtype)
    x1[:, strip : strip + mid, :] = mid1_ref[...]
    dst = place(core, step + cols, 0)
    own[:, pl.ds(dst, step), :] = side_ref[0:rows]
    other[:, pl.ds(dst, step), :] = side_ref[rows : 2 * rows]
    dst = place(core, 0, step + cols)
    own[:, pl.ds(dst, step), :] = jnp.zeros((rows, step, channels), own.dtype)
    other[:, pl.ds(dst, step), :] = jnp.zeros((rows, step, channels), own.dtype)
    edge = strip - step
    w_own = w_ref[...].reshape(3 * channels, channels)
    w_other = wx_ref[...].reshape(3 * channels, channels)
    weights = jnp.concatenate([w_own, w_other], axis=0)
    for first, width in ((0, edge), (edge, mid + 2 * step), (cols - edge, edge)):
        stacked = jnp.concatenate(
            [
                ref[:, first + b * step : first + b * step + width, :].reshape(
                    rows * width, channels
                )
                for ref in (own, other)
                for b in range(3)
            ],
            axis=1,
        )
        response = jnp.dot(stacked, weights, preferred_element_type=jnp.float32)
        current = x1[:, first : first + width, :]
        if first == edge:
            acc_ref[...] = response.reshape(rows, width, channels)
            mids_ref[...] = current
        else:
            result = update(
                current.reshape(rows * width, channels), response, bias_ref[1:2, :]
            )
            normed = normalize(result, gain_ref[2:3, :])
            result_ref, out_ref = (lows_ref, nlows_ref) if first == 0 else (highs_ref, nhighs_ref)
            result_ref[...] = result.reshape(rows, width, channels)
            out_ref[...] = normed.reshape(rows, width, channels)
            near_core = 1 if first == 0 else 0

            def give(normed=normed, width=width):
                nside_ref[...] = normed.reshape(rows, width, channels)

            pl.when(core == near_core)(give)


def last_kernel(
    flag_ref,
    gain_ref,
    bias_ref,
    wx_ref,
    w_ref,
    cmid_ref,
    acc_ref,
    mids_ref,
    lows_ref,
    highs_ref,
    nlows_ref,
    nhighs_ref,
    side_ref,
    out_ref,
    other,
    normed,
    x2,
):
    core = flag_ref[0]
    rows, mid, channels = cmid_ref.shape
    edge = nlows_ref.shape[1]
    step, reach = dilations[1], dilations[2]
    width = mid + 2 * step
    cols = 2 * edge + width
    blank = jnp.zeros((rows, 2 * step, channels), other.dtype)
    other[:, 0 : 2 * step, :] = blank
    other[:, 2 * step + mid : 4 * step + mid, :] = blank
    other[:, 2 * step : 2 * step + mid, :] = cmid_ref[...]
    stacked = jnp.concatenate(
        [
            other[:, b * step : b * step + width, :].reshape(rows * width, channels)
            for b in range(3)
        ],
        axis=1,
    )
    response = acc_ref[...].reshape(rows * width, channels) + jnp.dot(
        stacked, wx_ref[...].reshape(3 * channels, channels), preferred_element_type=jnp.float32
    )
    result = update(
        mids_ref[...].reshape(rows * width, channels), response, bias_ref[1:2, :]
    )
    x2[:, 0:edge, :] = lows_ref[...]
    x2[:, edge : edge + width, :] = result.reshape(rows, width, channels)
    x2[:, edge + width : cols, :] = highs_ref[...]
    normed[:, reach : reach + edge, :] = nlows_ref[...]
    normed[:, reach + edge : reach + edge + width, :] = normalize(
        result, gain_ref[2:3, :]
    ).reshape(rows, width, channels)
    normed[:, reach + edge + width : reach + cols, :] = nhighs_ref[...]
    dst = place(core, reach + cols, 0)
    normed[:, pl.ds(dst, reach), :] = side_ref[...]
    dst = place(core, 0, reach + cols)
    normed[:, pl.ds(dst, reach), :] = jnp.zeros((rows, reach, channels), normed.dtype)
    stacked = jnp.concatenate(
        [
            normed[:, b * reach : b * reach + cols, :].reshape(rows * cols, channels)
            for b in range(3)
        ],
        axis=1,
    )
    response = jnp.dot(
        stacked, w_ref[...].reshape(3 * channels, channels), preferred_element_type=jnp.float32
    )
    out_ref[...] = update(
        x2[...].reshape(rows * cols, channels), response, bias_ref[2:3, :]
    ).reshape(rows, cols, channels)


def by_halves(context_map, norm_gains, conv_biases, conv_weights):
    rows, cols, channels = context_map.shape
    kind = context_map.dtype
    size = lax.axis_size("row")
    group = size // 2
    half = rows // 2
    step, reach = dilations[1], dilations[2]
    strip = step + reach
    mid = cols - 2 * strip
    pad = lane_pad
    wide = strip + pad
    core, row = lax.axis_index("col"), lax.axis_index("row")
    upper_half = row < group
    flags = jnp.stack([core, row == group - 1, row == group]).astype(jnp.int32)
    last_above, first_below = (1, 1), (2, 1)
    swap = [(0, 1), (1, 0)]
    partner = [(i, (i + group) % size) for i in range(size)]
    down = [(i, i + 1) for i in range(size - 1)]
    up = [(j, i) for i, j in down]
    within_down = [(i, j) for i, j in down if j != group]
    within_up = [(j, i) for i, j in within_down]
    ring_down = [(i, i // group * group + (i + 1) % group) for i in range(size)]
    ring_up = [(j, i) for i, j in ring_down]

    near_at, far_at = (cols - strip, 0), (0, cols - strip)
    near_wide_at, far_wide_at = (cols - wide, 0), (0, cols - wide)
    mid_halo_at, far_halo_at = (strip - pad, wide), (0, cols - strip + pad)
    far_halo = strip - pad
    raw, near_low, near_high, mid_low, mid_high, far_low, far_high = copies(
        flags,
        (context_map,),
        (
            (None, 0, 0, rows, far_wide_at, wide, 0, 0),
            (None, 0, half, half, near_wide_at, wide, 1, 0),
            (None, 0, 0, half, near_wide_at, wide, 2, 0),
            (None, 0, half, half, mid_halo_at, mid, 3, 0),
            (None, 0, 0, half, mid_halo_at, mid, 4, 0),
            (None, 0, half, half, far_halo_at, far_halo, 5, 0),
            (None, 0, 0, half, far_halo_at, far_halo, 6, 0),
        ),
    )
    raw = lax.ppermute(raw, "row", partner)
    above_near = lax.ppermute(near_low, "row", down)
    below_near = lax.ppermute(near_high, "row", up)
    above_mid = lax.ppermute(mid_low, "row", down)
    below_mid = lax.ppermute(mid_high, "row", up)
    above_far = lax.ppermute(far_low, "row", within_down)
    below_far = lax.ppermute(far_high, "row", within_up)

    params = (norm_gains, conv_biases, conv_weights[0])
    (rim,) = copies(
        flags,
        (context_map, above_near, below_near),
        (
            (None, 1, 0, half, (wide - pad, 0), pad, 0, 0),
            (None, 0, 0, rows, (cols - pad, 0), pad, 0, half),
            (None, 2, 0, half, (wide - pad, 0), pad, 0, half + rows),
        ),
    )
    rim = lax.ppermute(rim, "col", swap)
    near_segments = (
        (None, 0, 0, half, rows, near_wide_at, (0, pad), wide),
        (None, 1, 0, 0, half, (0, 0), (0, pad), wide),
        (None, 2, 0, half + rows, half, (0, 0), (0, pad), wide),
        (None, 3, 0, 0, 2 * rows, (0, 0), (wide, 0), pad),
    )
    near1, near_n = first_layer(
        flags, params, (context_map, above_near, below_near, rim), near_segments, near_at, strip
    )
    cross_near = lax.ppermute(near_n, "row", partner)
    mid_segments = (
        (None, 0, 0, half, rows, (strip - pad, strip - pad), (0, 0), mid + 2 * pad),
        (None, 1, 0, 0, half, (0, 0), (0, 2 * pad), mid),
        (None, 2, 0, half + rows, half, (0, 0), (0, 2 * pad), mid),
        (None, 3, 0, 0, half, (0, wide - 2 * pad), (mid, 0), 2 * pad),
        (None, 4, 0, half + rows, half, (0, wide - 2 * pad), (mid, 0), 2 * pad),
    )
    mid1, mid_n = first_layer(
        flags, params, (context_map, above_mid, below_mid, above_near, below_near), mid_segments,
        (strip, strip), mid,
    )
    cross_mid = lax.ppermute(mid_n, "row", partner)

    ring_low, ring_high = copies(
        flags,
        (context_map, raw),
        (
            ((1, 1), 0, half, half, far_wide_at, wide, 0, 0),
            ((1, 0), 1, half, half, (0, 0), wide, 0, 0),
            ((2, 1), 0, 0, half, far_wide_at, wide, 1, 0),
            ((2, 0), 1, 0, half, (0, 0), wide, 1, 0),
        ),
    )
    ring_above = lax.ppermute(ring_low, "row", ring_down)
    ring_below = lax.ppermute(ring_high, "row", ring_up)
    spare = (0, mid - 2 * pad)
    body_at, edge_at = (pad, 0), (0, wide)
    halo_at, inner_at = (pad, 2 * pad), (pad + far_halo, 0)
    far_segments = (
        (None, 0, 0, half, rows, far_wide_at, body_at, wide),
        (None, 1, 0, 0, half, (0, 0), halo_at, far_halo),
        (None, 2, 0, half + rows, half, (0, 0), halo_at, far_halo),
        (None, 3, 0, 0, half, spare, inner_at, 2 * pad),
        (None, 4, 0, half + rows, half, spare, inner_at, 2 * pad),
        (first_below, 5, 0, 0, half, (0, 0), body_at, wide),
        (last_above, 6, 0, half + rows, half, (0, 0), body_at, wide),
        (None, None, 0, 0, 2 * rows, (0, 0), edge_at, pad),
    )
    far1, far_n = first_layer(
        flags, params,
        (context_map, above_far, below_far, above_mid, below_mid, ring_above, ring_below),
        far_segments, far_at, strip,
    )
    partner_segments = (
        (None, 0, 0, half, rows, (0, 0), body_at, wide),
        (None, 1, 0, 0, half, (0, 0), body_at, wide),
        (None, 2, 0, half + rows, half, (0, 0), body_at, wide),
        (first_below, None, 0, 0, half, (0, 0), body_at, wide),
        (last_above, None, 0, half + rows, half, (0, 0), body_at, wide),
        (None, None, 0, 0, 2 * rows, (0, 0), edge_at, pad),
    )
    _, cross_far = first_layer(
        flags, params, (raw, ring_above, ring_below), partner_segments, (0, pad), strip
    )

    (side,) = copies(
        flags,
        (near_n, cross_near),
        (
            (None, 0, 0, rows, (strip - step, 0), step, 0, 0),
            (None, 1, 0, rows, (strip - step, 0), step, 0, rows),
        ),
    )
    side = lax.ppermute(side, "col", swap)
    toward = lax.dynamic_index_in_dim(
        conv_weights[1], jnp.where(upper_half, 2, 0), axis=0, keepdims=False
    )
    edge = strip - step
    wider = mid + 2 * step
    edge_shape = jax.ShapeDtypeStruct((rows, edge, channels), kind)
    lows, highs, n_lows, n_highs, n_side, acc, mids = kernel_call(
        functools.partial(second_layer_kernel, strip),
        (
            edge_shape,
            edge_shape,
            edge_shape,
            edge_shape,
            edge_shape,
            jax.ShapeDtypeStruct((rows, wider, channels), jnp.float32),
            jax.ShapeDtypeStruct((rows, wider, channels), kind),
        ),
        [smem_spec()] + [vmem_spec()] * 13,
        [
            pltpu.VMEM((rows, cols + 2 * step, channels), kind),
            pltpu.VMEM((rows, cols + 2 * step, channels), kind),
            pltpu.VMEM((rows, cols, channels), kind),
        ],
        12 * rows * cols * channels * channels,
        6 * channels * channels * 2,
    )(
        flags, norm_gains, conv_biases, conv_weights[1, 1], toward, near_n, mid_n, far_n,
        cross_near, cross_far, side, near1, mid1, far1,
    )
    last_side = lax.ppermute(n_side, "col", swap)
    return kernel_call(
        last_kernel,
        jax.ShapeDtypeStruct(context_map.shape, kind),
        [smem_spec()] + [vmem_spec()] * 12,
        [
            pltpu.VMEM((rows, mid + 4 * step, channels), kind),
            pltpu.VMEM((rows, cols + 2 * reach, channels), kind),
            pltpu.VMEM((rows, cols, channels), kind),
        ],
        8 * rows * cols * channels * channels,
        3 * channels * channels * 2,
    )(
        flags, norm_gains, conv_biases, toward, conv_weights[2, 1], cross_mid, acc, mids, lows,
        highs, n_lows, n_highs, last_side,
    )


def shards(context_map, *params):
    rows, cols, _ = context_map.shape
    map_rows = lax.axis_size("row") * rows
    strip = dilations[1] + dilations[2]
    if (
        map_rows == 2 * dilations[1]
        and map_rows <= dilations[2]
        and rows == 2 * dilations[0]
        and dilations[1] % rows == 0
        and lax.axis_size("col") == 2
        and cols >= 2 * strip + 3 * lane_pad
        and cols % lane_pad == 0
    ):
        return by_halves(context_map, *params)
    return by_classes(context_map, *params)


def solution(mesh):
    return jax.shard_map(
        shards,
        mesh=mesh,
        in_specs=(P(("ctx", "row"), "col", None), P(), P(), P()),
        out_specs=P(("ctx", "row"), "col", None),
        check_vma=False,
    )
```

```python
import functools

import jax
import jax.numpy as jnp
from jax import lax
from jax.experimental import pallas as pl
from jax.experimental.pallas import tpu as pltpu
from jax.sharding import PartitionSpec as P

epsilon = 1e-05
dilations = (4, 32, 64)
lane_pad = 16
vmem_limit = 40 * 1024 * 1024


def extended(x, sides, width):
    for axis, dim in sides:
        size, length = (lax.axis_size(axis), x.shape[dim])
        up = [(i, (i + 1) % size) for i in range(size - 1)]
        down = [(j, i) for i, j in up]
        last = lax.slice_in_dim(x, length - width, length, axis=dim)
        first = lax.slice_in_dim(x, 0, width, axis=dim)
        before = lax.ppermute(last, axis, up)
        after = lax.ppermute(first, axis, down)
        x = jnp.concatenate([before, x, after], axis=dim)
    return x


def normalize(current, gain_row):
    values = current.astype(jnp.float32)
    centred = values - jnp.mean(values, axis=-1, keepdims=True)
    variance = jnp.mean(centred * centred, axis=-1, keepdims=True)
    return (centred * lax.rsqrt(variance + epsilon) * gain_row).astype(jnp.bfloat16)


def convolve(padded, kernel, row_step, col_step, out_rows, out_cols):
    channels = padded.shape[2]
    tap_list = []
    for tap_row in range(3):
        for tap_col in range(3):
            tap_list.append(
                lax.slice(
                    padded,
                    (tap_row * row_step, tap_col * col_step, 0),
                    (tap_row * row_step + out_rows, tap_col * col_step + out_cols, channels),
                )
            )
    stacked = jnp.concatenate(tap_list, axis=2).reshape(out_rows * out_cols, 9 * channels)
    product = jnp.dot(
        stacked, kernel.reshape(9 * channels, kernel.shape[3]), preferred_element_type=jnp.float32
    )
    return product.reshape(out_rows, out_cols, kernel.shape[3])


def update(current, response, bias_row):
    return (current.astype(jnp.float32) + jnp.maximum(response + bias_row, 0.0)).astype(
        jnp.bfloat16
    )


def by_classes(context_map, norm_gains, conv_biases, conv_weights):
    tile_rows, tile_cols, channels = context_map.shape
    normed = normalize(context_map, norm_gains[0])
    padded = extended(normed, (("row", 0), ("col", 1)), 4)
    current = update(
        context_map, convolve(padded, conv_weights[0], 4, 4, tile_rows, tile_cols), conv_biases[0]
    )
    class_count = lax.axis_size("row") // tile_rows
    sub_cols = tile_cols // class_count
    outgoing = (
        current.reshape(tile_rows, sub_cols, class_count, channels)
        .transpose(0, 2, 1, 3)
        .reshape(tile_rows * class_count, sub_cols, channels)
    )
    grouped = lax.all_to_all(outgoing, "row", split_axis=0, concat_axis=0, tiled=True)
    sub_rows = grouped.shape[0]
    for position, dilation in ((1, 32), (2, 64)):
        normed = normalize(grouped, norm_gains[position])
        row_gap = dilation // tile_rows
        col_gap = dilation // class_count
        with_sides = extended(normed, (("col", 1),), col_gap)
        padded = jnp.pad(with_sides, ((row_gap, row_gap), (0, 0), (0, 0)))
        response = convolve(padded, conv_weights[position], row_gap, col_gap, sub_rows, sub_cols)
        grouped = update(grouped, response, conv_biases[position])
    returned = lax.all_to_all(grouped, "row", split_axis=0, concat_axis=0, tiled=True)
    return (
        returned.reshape(tile_rows, class_count, sub_cols, channels)
        .transpose(0, 2, 1, 3)
        .reshape(tile_rows, tile_cols, channels)
    )


def vmem_spec():
    return pl.BlockSpec(memory_space=pltpu.VMEM)


def smem_spec():
    return pl.BlockSpec(memory_space=pltpu.SMEM)


def any_spec():
    return pl.BlockSpec(memory_space=pl.ANY)


def kernel_call(body, out_shape, in_specs, scratch, flops, bytes_accessed):
    return pl.pallas_call(
        body,
        out_shape=out_shape,
        in_specs=in_specs,
        out_specs=jax.tree.map(lambda _: vmem_spec(), out_shape),
        scratch_shapes=scratch,
        compiler_params=pltpu.CompilerParams(vmem_limit_bytes=vmem_limit),
        cost_estimate=pl.CostEstimate(
            flops=flops, bytes_accessed=bytes_accessed, transcendentals=0
        ),
    )


def place(core, at_zero, at_one):
    return pl.multiple_of(jnp.where(core == 0, at_zero, at_one), lane_pad)


def guarded(flag_ref, condition, action):
    if condition is None:
        action()
    else:
        number, value = condition
        pl.when(flag_ref[number] == value)(action)


def copy_kernel(moves, inputs, flag_ref, *refs):
    sources, targets = refs[:inputs], refs[inputs:]

    def move(which, row, count, column, width, target, target_row):
        src = place(flag_ref[0], *column)
        for r in range(count):
            targets[target][target_row + r] = sources[which][row + r, pl.ds(src, width), :]

    for parts in moves:
        guarded(flag_ref, parts[0], functools.partial(move, *parts[1:]))


def copies(flags, arrays, moves):
    channels, kind = arrays[0].shape[2], arrays[0].dtype
    shapes = {}
    for _, _, _, count, _, width, target, target_row in moves:
        height = max(target_row + count, shapes.get(target, (0, 0))[0])
        shapes[target] = (height, width)
    out = tuple(
        jax.ShapeDtypeStruct(shapes[target] + (channels,), kind) for target in range(len(shapes))
    )
    volume = sum(2 * height * width * channels * 2 for height, width in shapes.values())
    return kernel_call(
        functools.partial(copy_kernel, moves, len(arrays)),
        out,
        [smem_spec()] + [vmem_spec()] * len(arrays),
        [],
        0,
        volume,
    )(flags, *arrays)


def first_layer_kernel(segments, out_at, rows, width, flag_ref, gain_ref, bias_ref, w_ref, *rest):
    parts, (next_ref, normed_ref, window, taps, weights, sem) = rest[:-6], rest[-6:]
    load = pltpu.make_async_copy(w_ref.at[0], weights, sem)
    load.start()
    core = flag_ref[0]
    half = rows // 2
    channels = window.shape[2]
    gain = gain_ref[0:1, :]

    def fill(which, source_row, window_row, count, source, target, columns):
        src, dst = place(core, *source), place(core, *target)
        for r in range(count):
            if which is None:
                values = jnp.zeros((columns, channels), window.dtype)
            else:
                values = normalize(
                    parts[which][source_row + r, pl.ds(src, columns), :], gain
                )
            window[window_row + r, pl.ds(dst, columns), :] = values

    for segment in segments:
        guarded(flag_ref, segment[0], functools.partial(fill, *segment[1:]))
    step = dilations[0]
    for b in range(3):
        first = lane_pad + (b - 1) * step
        for r in range(2 * rows):
            taps[b, r] = window[r, first : first + width, :]
    stacked = jnp.concatenate(
        [
            taps[b, a * half : a * half + rows].reshape(rows * width, channels)
            for a in range(3)
            for b in range(3)
        ],
        axis=1,
    )
    load.wait()
    response = jnp.dot(
        stacked, weights[...].reshape(9 * channels, channels), preferred_element_type=jnp.float32
    )
    out_col = place(core, *out_at)
    current = parts[0][:, pl.ds(out_col, width), :].reshape(rows * width, channels)
    result = update(current, response, bias_ref[0:1, :])
    next_ref[...] = result.reshape(rows, width, channels)
    normed_ref[...] = normalize(result, gain_ref[1:2, :]).reshape(rows, width, channels)


def first_layer(flags, params, parts, segments, out_at, width):
    rows, _, channels = parts[0].shape
    kind = parts[0].dtype
    out = jax.ShapeDtypeStruct((rows, width, channels), kind)
    cells = rows * width
    return kernel_call(
        functools.partial(first_layer_kernel, segments, out_at, rows, width),
        (out, out),
        [smem_spec(), vmem_spec(), vmem_spec(), any_spec()] + [vmem_spec()] * len(parts),
        [
            pltpu.VMEM((2 * rows, width + 2 * lane_pad, channels), kind),
            pltpu.VMEM((3, 2 * rows, width, channels), kind),
            pltpu.VMEM(params[2].shape[1:], kind),
            pltpu.SemaphoreType.DMA,
        ],
        18 * cells * channels * channels,
        9 * channels * channels * 2,
    )(flags, *params, *parts)


def second_layer_kernel(
    strip,
    flag_ref,
    gain_ref,
    bias_ref,
    w_ref,
    near_ref,
    mid_ref,
    far_ref,
    cnear_ref,
    cfar_ref,
    side_ref,
    near1_ref,
    mid1_ref,
    far1_ref,
    lows_ref,
    highs_ref,
    nlows_ref,
    nhighs_ref,
    nside_ref,
    acc_ref,
    mids_ref,
    own,
    other,
    x1,
    weights,
    sems,
):
    core = flag_ref[0]
    loads = (
        pltpu.make_async_copy(w_ref.at[1, 1], weights.at[0], sems.at[0]),
        pltpu.make_async_copy(w_ref.at[1, flag_ref[3]], weights.at[1], sems.at[1]),
    )
    for load in loads:
        load.start()
    step = dilations[1]
    rows, mid, channels = mid_ref.shape
    cols = 2 * strip + mid
    near_at, far_at = (cols - strip, 0), (0, cols - strip)
    dst = place(core, step + near_at[0], step + near_at[1])
    own[:, pl.ds(dst, strip), :] = near_ref[...]
    other[:, pl.ds(dst, strip), :] = cnear_ref[...]
    dst = place(core, *near_at)
    x1[:, pl.ds(dst, strip), :] = near1_ref[...]
    dst = place(core, step + far_at[0], step + far_at[1])
    own[:, pl.ds(dst, strip), :] = far_ref[...]
    other[:, pl.ds(dst, strip), :] = cfar_ref[...]
    dst = place(core, *far_at)
    x1[:, pl.ds(dst, strip), :] = far1_ref[...]
    own[:, step + strip : step + strip + mid, :] = mid_ref[...]
    other[:, step + strip : step + strip + mid, :] = jnp.zeros((rows, mid, channels), own.dtype)
    x1[:, strip : strip + mid, :] = mid1_ref[...]
    dst = place(core, step + cols, 0)
    own[:, pl.ds(dst, step), :] = side_ref[0:rows]
    other[:, pl.ds(dst, step), :] = side_ref[rows : 2 * rows]
    dst = place(core, 0, step + cols)
    own[:, pl.ds(dst, step), :] = jnp.zeros((rows, step, channels), own.dtype)
    other[:, pl.ds(dst, step), :] = jnp.zeros((rows, step, channels), own.dtype)
    edge = strip - step
    for load in loads:
        load.wait()
    for first, width in ((0, edge), (edge, mid + 2 * step), (cols - edge, edge)):
        stacked = jnp.concatenate(
            [
                ref[:, first + b * step : first + b * step + width, :].reshape(
                    rows * width, channels
                )
                for ref in (own, other)
                for b in range(3)
            ],
            axis=1,
        )
        response = jnp.dot(
            stacked,
            weights[...].reshape(6 * channels, channels),
            preferred_element_type=jnp.float32,
        )
        current = x1[:, first : first + width, :]
        if first == edge:
            acc_ref[...] = response.reshape(rows, width, channels)
            mids_ref[...] = current
        else:
            result = update(
                current.reshape(rows * width, channels), response, bias_ref[1:2, :]
            )
            normed = normalize(result, gain_ref[2:3, :])
            result_ref, out_ref = (lows_ref, nlows_ref) if first == 0 else (highs_ref, nhighs_ref)
            result_ref[...] = result.reshape(rows, width, channels)
            out_ref[...] = normed.reshape(rows, width, channels)
            near_core = 1 if first == 0 else 0

            def give(normed=normed, width=width):
                nside_ref[...] = normed.reshape(rows, width, channels)

            pl.when(core == near_core)(give)


def last_kernel(
    flag_ref,
    gain_ref,
    bias_ref,
    w_ref,
    cmid_ref,
    acc_ref,
    mids_ref,
    lows_ref,
    highs_ref,
    nlows_ref,
    nhighs_ref,
    side_ref,
    out_ref,
    other,
    normed,
    x2,
    weights,
    sems,
):
    core = flag_ref[0]
    loads = (
        pltpu.make_async_copy(w_ref.at[1, flag_ref[3]], weights.at[0], sems.at[0]),
        pltpu.make_async_copy(w_ref.at[2, 1], weights.at[1], sems.at[1]),
    )
    for load in loads:
        load.start()
    rows, mid, channels = cmid_ref.shape
    edge = nlows_ref.shape[1]
    step, reach = dilations[1], dilations[2]
    width = mid + 2 * step
    cols = 2 * edge + width
    blank = jnp.zeros((rows, 2 * step, channels), other.dtype)
    other[:, 0 : 2 * step, :] = blank
    other[:, 2 * step + mid : 4 * step + mid, :] = blank
    other[:, 2 * step : 2 * step + mid, :] = cmid_ref[...]
    stacked = jnp.concatenate(
        [
            other[:, b * step : b * step + width, :].reshape(rows * width, channels)
            for b in range(3)
        ],
        axis=1,
    )
    loads[0].wait()
    response = acc_ref[...].reshape(rows * width, channels) + jnp.dot(
        stacked, weights[0].reshape(3 * channels, channels), preferred_element_type=jnp.float32
    )
    result = update(
        mids_ref[...].reshape(rows * width, channels), response, bias_ref[1:2, :]
    )
    x2[:, 0:edge, :] = lows_ref[...]
    x2[:, edge : edge + width, :] = result.reshape(rows, width, channels)
    x2[:, edge + width : cols, :] = highs_ref[...]
    normed[:, reach : reach + edge, :] = nlows_ref[...]
    normed[:, reach + edge : reach + edge + width, :] = normalize(
        result, gain_ref[2:3, :]
    ).reshape(rows, width, channels)
    normed[:, reach + edge + width : reach + cols, :] = nhighs_ref[...]
    dst = place(core, reach + cols, 0)
    normed[:, pl.ds(dst, reach), :] = side_ref[...]
    dst = place(core, 0, reach + cols)
    normed[:, pl.ds(dst, reach), :] = jnp.zeros((rows, reach, channels), normed.dtype)
    stacked = jnp.concatenate(
        [
            normed[:, b * reach : b * reach + cols, :].reshape(rows * cols, channels)
            for b in range(3)
        ],
        axis=1,
    )
    loads[1].wait()
    response = jnp.dot(
        stacked, weights[1].reshape(3 * channels, channels), preferred_element_type=jnp.float32
    )
    out_ref[...] = update(
        x2[...].reshape(rows * cols, channels), response, bias_ref[2:3, :]
    ).reshape(rows, cols, channels)


def by_halves(context_map, norm_gains, conv_biases, conv_weights):
    rows, cols, channels = context_map.shape
    kind = context_map.dtype
    size = lax.axis_size("row")
    group = size // 2
    half = rows // 2
    step, reach = dilations[1], dilations[2]
    strip = step + reach
    mid = cols - 2 * strip
    pad = lane_pad
    wide = strip + pad
    core, row = lax.axis_index("col"), lax.axis_index("row")
    upper_half = row < group
    flags = jnp.stack(
        [core, row == group - 1, row == group, jnp.where(upper_half, 2, 0)]
    ).astype(jnp.int32)
    last_above, first_below = (1, 1), (2, 1)
    swap = [(0, 1), (1, 0)]
    partner = [(i, (i + group) % size) for i in range(size)]
    down = [(i, i + 1) for i in range(size - 1)]
    up = [(j, i) for i, j in down]
    within_down = [(i, j) for i, j in down if j != group]
    within_up = [(j, i) for i, j in within_down]
    ring_down = [(i, i // group * group + (i + 1) % group) for i in range(size)]
    ring_up = [(j, i) for i, j in ring_down]

    near_at, far_at = (cols - strip, 0), (0, cols - strip)
    near_wide_at, far_wide_at = (cols - wide, 0), (0, cols - wide)
    mid_halo_at, far_halo_at = (strip - pad, wide), (0, cols - strip + pad)
    far_halo = strip - pad
    raw, near_low, near_high, mid_low, mid_high, far_low, far_high = copies(
        flags,
        (context_map,),
        (
            (None, 0, 0, rows, far_wide_at, wide, 0, 0),
            (None, 0, half, half, near_wide_at, wide, 1, 0),
            (None, 0, 0, half, near_wide_at, wide, 2, 0),
            (None, 0, half, half, mid_halo_at, mid, 3, 0),
            (None, 0, 0, half, mid_halo_at, mid, 4, 0),
            (None, 0, half, half, far_halo_at, far_halo, 5, 0),
            (None, 0, 0, half, far_halo_at, far_halo, 6, 0),
        ),
    )
    raw = lax.ppermute(raw, "row", partner)
    above_near = lax.ppermute(near_low, "row", down)
    below_near = lax.ppermute(near_high, "row", up)
    above_mid = lax.ppermute(mid_low, "row", down)
    below_mid = lax.ppermute(mid_high, "row", up)
    above_far = lax.ppermute(far_low, "row", within_down)
    below_far = lax.ppermute(far_high, "row", within_up)

    params = (norm_gains, conv_biases, conv_weights)
    (rim,) = copies(
        flags,
        (context_map, above_near, below_near),
        (
            (None, 1, 0, half, (wide - pad, 0), pad, 0, 0),
            (None, 0, 0, rows, (cols - pad, 0), pad, 0, half),
            (None, 2, 0, half, (wide - pad, 0), pad, 0, half + rows),
        ),
    )
    rim = lax.ppermute(rim, "col", swap)
    near_segments = (
        (None, 0, 0, half, rows, near_wide_at, (0, pad), wide),
        (None, 1, 0, 0, half, (0, 0), (0, pad), wide),
        (None, 2, 0, half + rows, half, (0, 0), (0, pad), wide),
        (None, 3, 0, 0, 2 * rows, (0, 0), (wide, 0), pad),
    )
    near1, near_n = first_layer(
        flags, params, (context_map, above_near, below_near, rim), near_segments, near_at, strip
    )
    cross_near = lax.ppermute(near_n, "row", partner)
    mid_segments = (
        (None, 0, 0, half, rows, (strip - pad, strip - pad), (0, 0), mid + 2 * pad),
        (None, 1, 0, 0, half, (0, 0), (0, 2 * pad), mid),
        (None, 2, 0, half + rows, half, (0, 0), (0, 2 * pad), mid),
        (None, 3, 0, 0, half, (0, wide - 2 * pad), (mid, 0), 2 * pad),
        (None, 4, 0, half + rows, half, (0, wide - 2 * pad), (mid, 0), 2 * pad),
    )
    mid1, mid_n = first_layer(
        flags, params, (context_map, above_mid, below_mid, above_near, below_near), mid_segments,
        (strip, strip), mid,
    )
    cross_mid = lax.ppermute(mid_n, "row", partner)

    ring_low, ring_high = copies(
        flags,
        (context_map, raw),
        (
            ((1, 1), 0, half, half, far_wide_at, wide, 0, 0),
            ((1, 0), 1, half, half, (0, 0), wide, 0, 0),
            ((2, 1), 0, 0, half, far_wide_at, wide, 1, 0),
            ((2, 0), 1, 0, half, (0, 0), wide, 1, 0),
        ),
    )
    ring_above = lax.ppermute(ring_low, "row", ring_down)
    ring_below = lax.ppermute(ring_high, "row", ring_up)
    spare = (0, mid - 2 * pad)
    body_at, edge_at = (pad, 0), (0, wide)
    halo_at, inner_at = (pad, 2 * pad), (pad + far_halo, 0)
    far_segments = (
        (None, 0, 0, half, rows, far_wide_at, body_at, wide),
        (None, 1, 0, 0, half, (0, 0), halo_at, far_halo),
        (None, 2, 0, half + rows, half, (0, 0), halo_at, far_halo),
        (None, 3, 0, 0, half, spare, inner_at, 2 * pad),
        (None, 4, 0, half + rows, half, spare, inner_at, 2 * pad),
        (first_below, 5, 0, 0, half, (0, 0), body_at, wide),
        (last_above, 6, 0, half + rows, half, (0, 0), body_at, wide),
        (None, None, 0, 0, 2 * rows, (0, 0), edge_at, pad),
    )
    far1, far_n = first_layer(
        flags, params,
        (context_map, above_far, below_far, above_mid, below_mid, ring_above, ring_below),
        far_segments, far_at, strip,
    )
    partner_segments = (
        (None, 0, 0, half, rows, (0, 0), body_at, wide),
        (None, 1, 0, 0, half, (0, 0), body_at, wide),
        (None, 2, 0, half + rows, half, (0, 0), body_at, wide),
        (first_below, None, 0, 0, half, (0, 0), body_at, wide),
        (last_above, None, 0, half + rows, half, (0, 0), body_at, wide),
        (None, None, 0, 0, 2 * rows, (0, 0), edge_at, pad),
    )
    _, cross_far = first_layer(
        flags, params, (raw, ring_above, ring_below), partner_segments, (0, pad), strip
    )

    (side,) = copies(
        flags,
        (near_n, cross_near),
        (
            (None, 0, 0, rows, (strip - step, 0), step, 0, 0),
            (None, 1, 0, rows, (strip - step, 0), step, 0, rows),
        ),
    )
    side = lax.ppermute(side, "col", swap)
    edge = strip - step
    wider = mid + 2 * step
    edge_shape = jax.ShapeDtypeStruct((rows, edge, channels), kind)
    lows, highs, n_lows, n_highs, n_side, acc, mids = kernel_call(
        functools.partial(second_layer_kernel, strip),
        (
            edge_shape,
            edge_shape,
            edge_shape,
            edge_shape,
            edge_shape,
            jax.ShapeDtypeStruct((rows, wider, channels), jnp.float32),
            jax.ShapeDtypeStruct((rows, wider, channels), kind),
        ),
        [smem_spec(), vmem_spec(), vmem_spec(), any_spec()] + [vmem_spec()] * 9,
        [
            pltpu.VMEM((rows, cols + 2 * step, channels), kind),
            pltpu.VMEM((rows, cols + 2 * step, channels), kind),
            pltpu.VMEM((rows, cols, channels), kind),
            pltpu.VMEM((2, 3, channels, channels), kind),
            pltpu.SemaphoreType.DMA((2,)),
        ],
        12 * rows * cols * channels * channels,
        6 * channels * channels * 2,
    )(
        flags, norm_gains, conv_biases, conv_weights, near_n, mid_n, far_n,
        cross_near, cross_far, side, near1, mid1, far1,
    )
    last_side = lax.ppermute(n_side, "col", swap)
    return kernel_call(
        last_kernel,
        jax.ShapeDtypeStruct(context_map.shape, kind),
        [smem_spec(), vmem_spec(), vmem_spec(), any_spec()] + [vmem_spec()] * 8,
        [
            pltpu.VMEM((rows, mid + 4 * step, channels), kind),
            pltpu.VMEM((rows, cols + 2 * reach, channels), kind),
            pltpu.VMEM((rows, cols, channels), kind),
            pltpu.VMEM((2, 3, channels, channels), kind),
            pltpu.SemaphoreType.DMA((2,)),
        ],
        8 * rows * cols * channels * channels,
        3 * channels * channels * 2,
    )(
        flags, norm_gains, conv_biases, conv_weights, cross_mid, acc, mids, lows,
        highs, n_lows, n_highs, last_side,
    )


def shards(context_map, *params):
    rows, cols, _ = context_map.shape
    map_rows = lax.axis_size("row") * rows
    strip = dilations[1] + dilations[2]
    if (
        map_rows == 2 * dilations[1]
        and map_rows <= dilations[2]
        and rows == 2 * dilations[0]
        and dilations[1] % rows == 0
        and lax.axis_size("col") == 2
        and cols >= 2 * strip + 3 * lane_pad
        and cols % lane_pad == 0
    ):
        return by_halves(context_map, *params)
    return by_classes(context_map, *params)


def solution(mesh):
    return jax.shard_map(
        shards,
        mesh=mesh,
        in_specs=(P(("ctx", "row"), "col", None), P(), P(), P()),
        out_specs=P(("ctx", "row"), "col", None),
        check_vma=False,
    )
```

```python
import functools

import jax
import jax.numpy as jnp
from jax import lax
from jax.experimental import pallas as pl
from jax.experimental.pallas import tpu as pltpu
from jax.sharding import PartitionSpec as P

epsilon = 1e-05
dilations = (4, 32, 64)
lane_pad = 16
vmem_limit = 40 * 1024 * 1024


def extended(x, sides, width):
    for axis, dim in sides:
        size, length = (lax.axis_size(axis), x.shape[dim])
        up = [(i, (i + 1) % size) for i in range(size - 1)]
        down = [(j, i) for i, j in up]
        last = lax.slice_in_dim(x, length - width, length, axis=dim)
        first = lax.slice_in_dim(x, 0, width, axis=dim)
        before = lax.ppermute(last, axis, up)
        after = lax.ppermute(first, axis, down)
        x = jnp.concatenate([before, x, after], axis=dim)
    return x


def normalize(current, gain_row):
    values = current.astype(jnp.float32)
    centred = values - jnp.mean(values, axis=-1, keepdims=True)
    variance = jnp.mean(centred * centred, axis=-1, keepdims=True)
    return (centred * lax.rsqrt(variance + epsilon) * gain_row).astype(jnp.bfloat16)


def convolve(padded, kernel, row_step, col_step, out_rows, out_cols):
    channels = padded.shape[2]
    tap_list = []
    for tap_row in range(3):
        for tap_col in range(3):
            tap_list.append(
                lax.slice(
                    padded,
                    (tap_row * row_step, tap_col * col_step, 0),
                    (tap_row * row_step + out_rows, tap_col * col_step + out_cols, channels),
                )
            )
    stacked = jnp.concatenate(tap_list, axis=2).reshape(out_rows * out_cols, 9 * channels)
    product = jnp.dot(
        stacked, kernel.reshape(9 * channels, kernel.shape[3]), preferred_element_type=jnp.float32
    )
    return product.reshape(out_rows, out_cols, kernel.shape[3])


def update(current, response, bias_row):
    return (current.astype(jnp.float32) + jnp.maximum(response + bias_row, 0.0)).astype(
        jnp.bfloat16
    )


def by_classes(context_map, norm_gains, conv_biases, conv_weights):
    tile_rows, tile_cols, channels = context_map.shape
    normed = normalize(context_map, norm_gains[0])
    padded = extended(normed, (("row", 0), ("col", 1)), 4)
    current = update(
        context_map, convolve(padded, conv_weights[0], 4, 4, tile_rows, tile_cols), conv_biases[0]
    )
    class_count = lax.axis_size("row") // tile_rows
    sub_cols = tile_cols // class_count
    outgoing = (
        current.reshape(tile_rows, sub_cols, class_count, channels)
        .transpose(0, 2, 1, 3)
        .reshape(tile_rows * class_count, sub_cols, channels)
    )
    grouped = lax.all_to_all(outgoing, "row", split_axis=0, concat_axis=0, tiled=True)
    sub_rows = grouped.shape[0]
    for position, dilation in ((1, 32), (2, 64)):
        normed = normalize(grouped, norm_gains[position])
        row_gap = dilation // tile_rows
        col_gap = dilation // class_count
        with_sides = extended(normed, (("col", 1),), col_gap)
        padded = jnp.pad(with_sides, ((row_gap, row_gap), (0, 0), (0, 0)))
        response = convolve(padded, conv_weights[position], row_gap, col_gap, sub_rows, sub_cols)
        grouped = update(grouped, response, conv_biases[position])
    returned = lax.all_to_all(grouped, "row", split_axis=0, concat_axis=0, tiled=True)
    return (
        returned.reshape(tile_rows, class_count, sub_cols, channels)
        .transpose(0, 2, 1, 3)
        .reshape(tile_rows, tile_cols, channels)
    )


def vmem_spec():
    return pl.BlockSpec(memory_space=pltpu.VMEM)


def smem_spec():
    return pl.BlockSpec(memory_space=pltpu.SMEM)


def any_spec():
    return pl.BlockSpec(memory_space=pl.ANY)


def kernel_call(body, out_shape, in_specs, scratch):
    return pl.pallas_call(
        body,
        out_shape=out_shape,
        in_specs=in_specs,
        out_specs=jax.tree.map(lambda _: vmem_spec(), out_shape),
        scratch_shapes=scratch,
        compiler_params=pltpu.CompilerParams(vmem_limit_bytes=vmem_limit),
        cost_estimate=pl.CostEstimate(flops=1, bytes_accessed=1, transcendentals=0),
    )


def place(core, at_zero, at_one):
    return pl.multiple_of(jnp.where(core == 0, at_zero, at_one), lane_pad)


def guarded(flag_ref, condition, action):
    if condition is None:
        action()
    else:
        number, value = condition
        pl.when(flag_ref[number] == value)(action)


def copy_kernel(moves, inputs, flag_ref, *refs):
    sources, targets = refs[:inputs], refs[inputs:]

    def move(which, row, count, column, width, target, target_row):
        src = place(flag_ref[0], *column)
        for r in range(count):
            targets[target][target_row + r] = sources[which][row + r, pl.ds(src, width), :]

    for parts in moves:
        guarded(flag_ref, parts[0], functools.partial(move, *parts[1:]))


def copies(flags, arrays, moves):
    channels, kind = arrays[0].shape[2], arrays[0].dtype
    shapes = {}
    for _, _, _, count, _, width, target, target_row in moves:
        height = max(target_row + count, shapes.get(target, (0, 0))[0])
        shapes[target] = (height, width)
    out = tuple(
        jax.ShapeDtypeStruct(shapes[target] + (channels,), kind) for target in range(len(shapes))
    )
    return kernel_call(
        functools.partial(copy_kernel, moves, len(arrays)),
        out,
        [smem_spec()] + [vmem_spec()] * len(arrays),
        [],
    )(flags, *arrays)


def hold_kernel(flag_ref, gain_ref, bias_ref, w_ref, scale_ref, first_ref, second_ref, last_ref):
    scale_ref[0:3, :] = gain_ref[...]
    scale_ref[3:6, :] = bias_ref[...]
    first_ref[...] = w_ref[0]
    second_ref[0] = w_ref[1, 1]
    second_ref[1] = w_ref[1, flag_ref[3]]
    last_ref[...] = w_ref[2, 1]


def first_layer_kernel(segments, out_at, rows, width, flag_ref, scale_ref, w_ref, *rest):
    parts, (next_ref, normed_ref, window, taps) = rest[:-4], rest[-4:]
    core = flag_ref[0]
    half = rows // 2
    channels = window.shape[2]
    gain = scale_ref[0:1, :]

    def fill(which, source_row, window_row, count, source, target, columns):
        src, dst = place(core, *source), place(core, *target)
        for r in range(count):
            if which is None:
                values = jnp.zeros((columns, channels), window.dtype)
            else:
                values = normalize(
                    parts[which][source_row + r, pl.ds(src, columns), :], gain
                )
            window[window_row + r, pl.ds(dst, columns), :] = values

    for segment in segments:
        guarded(flag_ref, segment[0], functools.partial(fill, *segment[1:]))
    step = dilations[0]
    for b in range(3):
        first = lane_pad + (b - 1) * step
        for r in range(2 * rows):
            taps[b, r] = window[r, first : first + width, :]
    stacked = jnp.concatenate(
        [
            taps[b, a * half : a * half + rows].reshape(rows * width, channels)
            for a in range(3)
            for b in range(3)
        ],
        axis=1,
    )
    response = jnp.dot(
        stacked, w_ref[...].reshape(9 * channels, channels), preferred_element_type=jnp.float32
    )
    out_col = place(core, *out_at)
    current = parts[0][:, pl.ds(out_col, width), :].reshape(rows * width, channels)
    result = update(current, response, scale_ref[3:4, :])
    next_ref[...] = result.reshape(rows, width, channels)
    normed_ref[...] = normalize(result, scale_ref[1:2, :]).reshape(rows, width, channels)


def first_layer(flags, params, parts, segments, out_at, width):
    rows, _, channels = parts[0].shape
    kind = parts[0].dtype
    out = jax.ShapeDtypeStruct((rows, width, channels), kind)
    return kernel_call(
        functools.partial(first_layer_kernel, segments, out_at, rows, width),
        (out, out),
        [smem_spec()] + [vmem_spec()] * (2 + len(parts)),
        [
            pltpu.VMEM((2 * rows, width + 2 * lane_pad, channels), kind),
            pltpu.VMEM((3, 2 * rows, width, channels), kind),
        ],
    )(flags, *params, *parts)


def partial_kernel(
    flag_ref, scale_ref, w_ref, near_ref, mid_ref, far_ref, cfar_ref, side_ref, near1_ref, mid1_ref,
    far1_ref, acc_ref, next_ref, own, other,
):
    core = flag_ref[0]
    step = dilations[1]
    rows, near, channels = near_ref.shape
    mid, far = mid_ref.shape[1], far_ref.shape[1]
    cols = near + mid + far
    other[...] = jnp.zeros(other.shape, other.dtype)
    pieces = (
        (near_ref, near1_ref, (cols - near, 0)),
        (mid_ref, mid1_ref, (far, near)),
        (far_ref, far1_ref, (0, cols - far)),
    )
    for normed, current, at in pieces:
        width = normed.shape[1]
        next_ref[:, pl.ds(place(core, *at), width), :] = current[...]
        inside = pl.ds(place(core, at[0] + step, at[1] + step), width)
        own[:, inside, :] = normed[...]
        if normed is far_ref:
            other[:, inside, :] = cfar_ref[...]
    spare = side_ref.shape[1] - step
    own[:, pl.ds(place(core, step + cols, 0), step), :] = side_ref[
        :, pl.ds(place(core, 0, spare), step), :
    ]
    own[:, pl.ds(place(core, 0, step + cols), step), :] = jnp.zeros(
        (rows, step, channels), own.dtype
    )
    stacked = jnp.concatenate(
        [
            ref[:, b * step : b * step + cols, :].reshape(rows * cols, channels)
            for ref in (own, other)
            for b in range(3)
        ],
        axis=1,
    )
    acc_ref[...] = jnp.dot(
        stacked, w_ref[...].reshape(6 * channels, channels), preferred_element_type=jnp.float32
    ).reshape(rows, cols, channels)


def second_layer(flag_ref, scale_ref, w_ref, window, acc, current):
    step = dilations[1]
    rows, width, channels = current.shape
    cells = rows * width
    stacked = jnp.concatenate(
        [window[:, b * step : b * step + width, :].reshape(cells, channels) for b in range(3)],
        axis=1,
    )
    response = acc.reshape(cells, channels) + jnp.dot(
        stacked,
        w_ref[1].reshape(3 * channels, channels),
        preferred_element_type=jnp.float32,
    )
    result = update(current.reshape(cells, channels), response, scale_ref[4:5, :])
    normed = normalize(result, scale_ref[2:3, :])
    return result.reshape(current.shape), normed.reshape(current.shape)


def near_kernel(
    flag_ref, scale_ref, w_ref, cnear_ref, side_ref, acc_ref, x1_ref, next_ref, normed_ref, window
):
    core = flag_ref[0]
    step, reach = dilations[1], dilations[2]
    near, cols = cnear_ref.shape[1], x1_ref.shape[1]
    window[:, pl.ds(place(core, 0, step), near), :] = cnear_ref[...]
    window[:, pl.ds(place(core, near, 0), step), :] = side_ref[...]
    at = pl.ds(place(core, cols - reach, 0), reach)
    next_ref[...], normed_ref[...] = second_layer(
        flag_ref, scale_ref, w_ref, window[...], acc_ref[:, at, :], x1_ref[:, at, :]
    )


def rest_kernel(
    flag_ref, scale_ref, w_ref, cmid_ref, cnear_ref, acc_ref, x1_ref, next_ref, normed_ref, window
):
    core = flag_ref[0]
    step, reach = dilations[1], dilations[2]
    rows, mid, channels = cmid_ref.shape
    near, cols = cnear_ref.shape[1], x1_ref.shape[1]
    width, far = cols - reach, cols - near - mid
    count = width + step - far - mid
    window[:, pl.ds(place(core, step + far + mid, 0), count), :] = cnear_ref[
        :, pl.ds(place(core, 0, near - count), count), :
    ]
    window[:, pl.ds(place(core, step + far, count), mid), :] = cmid_ref[...]
    window[:, pl.ds(place(core, 0, count + mid), step + far), :] = jnp.zeros(
        (rows, step + far, channels), window.dtype
    )
    at = pl.ds(place(core, 0, reach), width)
    next_ref[...], normed_ref[...] = second_layer(
        flag_ref, scale_ref, w_ref, window[...], acc_ref[:, at, :], x1_ref[:, at, :]
    )


def last_kernel(
    flag_ref, scale_ref, w_ref, near2_ref, rest2_ref, near_ref, rest_ref, side_ref, out_ref, window,
    current,
):
    core = flag_ref[0]
    reach = dilations[2]
    rows, cols, channels = out_ref.shape
    rest = cols - reach
    dst = place(core, rest, 0)
    current[:, pl.ds(dst, reach), :] = near2_ref[...]
    window[:, pl.ds(pl.multiple_of(dst + reach, lane_pad), reach), :] = near_ref[...]
    dst = place(core, 0, reach)
    current[:, pl.ds(dst, rest), :] = rest2_ref[...]
    window[:, pl.ds(pl.multiple_of(dst + reach, lane_pad), rest), :] = rest_ref[...]
    window[:, pl.ds(place(core, reach + cols, 0), reach), :] = side_ref[...]
    window[:, pl.ds(place(core, 0, reach + cols), reach), :] = jnp.zeros(
        (rows, reach, channels), window.dtype
    )
    stacked = jnp.concatenate(
        [
            window[:, b * reach : b * reach + cols, :].reshape(rows * cols, channels)
            for b in range(3)
        ],
        axis=1,
    )
    response = jnp.dot(
        stacked, w_ref[...].reshape(3 * channels, channels), preferred_element_type=jnp.float32
    )
    out_ref[...] = update(
        current[...].reshape(rows * cols, channels), response, scale_ref[5:6, :]
    ).reshape(rows, cols, channels)


def by_halves(context_map, norm_gains, conv_biases, conv_weights):
    rows, cols, channels = context_map.shape
    kind = context_map.dtype
    size = lax.axis_size("row")
    group = size // 2
    half = rows // 2
    step, reach = dilations[1], dilations[2]
    strip = step + reach
    mid = cols - 2 * strip
    pad = lane_pad
    wide = strip + pad
    core, row = lax.axis_index("col"), lax.axis_index("row")
    upper_half = row < group
    flags = jnp.stack(
        [core, row == group - 1, row == group, jnp.where(upper_half, 2, 0)]
    ).astype(jnp.int32)
    swap = [(0, 1), (1, 0)]
    partner = [(i, (i + group) % size) for i in range(size)]
    down = [(i, i + 1) for i in range(size - 1)]
    up = [(j, i) for i, j in down]
    within_down = [(i, j) for i, j in down if j != group]
    within_up = [(j, i) for i, j in within_down]

    far_wide_at, near_wide_at = (0, cols - wide), (cols - wide, 0)
    span, span_at = cols - wide, (wide, 0)
    parts = (
        (None, 0, 0, rows, far_wide_at, wide, 0, 0),
        (None, 0, 0, rows, near_wide_at, wide, 1, 0),
        (None, 0, 0, rows, (strip - pad, strip - pad), mid + 2 * pad, 2, 0),
        (None, 0, half, half, far_wide_at, wide, 3, 0),
        (None, 0, 0, half, far_wide_at, wide, 4, 0),
        (None, 0, half, half, span_at, span, 5, 0),
        (None, 0, 0, half, span_at, span, 6, 0),
        ((1, 1), 0, half, half, span_at, span, 7, 0),
        ((1, 0), 0, 0, half, span_at, span, 7, 0),
    )
    (
        far_x, near_x, mid_x, far_low, far_high, low, high, middle
    ) = copies(flags, (context_map,), parts)
    above_far = lax.ppermute(far_low, "row", down)
    below_far = lax.ppermute(far_high, "row", up)
    above = lax.ppermute(low, "row", within_down)
    below = lax.ppermute(high, "row", within_up)
    middle = lax.ppermute(middle, "row", [(group - 1, group), (group, group - 1)])

    tail = conv_weights.shape[2:]
    scales, first_w, second_w, last_w = kernel_call(
        hold_kernel,
        (
            jax.ShapeDtypeStruct((2 * norm_gains.shape[0], channels), jnp.float32),
            jax.ShapeDtypeStruct((3,) + tail, kind),
            jax.ShapeDtypeStruct((2,) + tail, kind),
            jax.ShapeDtypeStruct(tail, kind),
        ),
        [smem_spec()] + [vmem_spec()] * 3,
        [],
    )(flags, norm_gains, conv_biases, conv_weights)
    params = (scales, first_w)
    far_body, far_edge = (pad, 0), (0, wide)
    far_segments = (
        (None, 0, 0, half, rows, (0, 0), far_body, wide),
        (None, 1, 0, 0, half, (0, 0), far_body, wide),
        (None, 2, 0, half + rows, half, (0, 0), far_body, wide),
        (None, None, 0, 0, 2 * rows, (0, 0), far_edge, pad),
    )
    far1, far_n = first_layer(
        flags, params, (far_x, above_far, below_far), far_segments, (0, pad), strip
    )
    cross_far = lax.ppermute(far_n, "row", partner)

    near_end, span_end = (wide - pad, 0), (span - pad, 0)
    (rim,) = copies(
        flags,
        (near_x, above, below, middle),
        (
            ((2, 0), 1, 0, half, span_end, pad, 0, 0),
            ((2, 1), 3, 0, half, span_end, pad, 0, 0),
            (None, 0, 0, rows, near_end, pad, 0, half),
            ((1, 0), 2, 0, half, span_end, pad, 0, half + rows),
            ((1, 1), 3, 0, half, span_end, pad, 0, half + rows),
        ),
    )
    rim = lax.ppermute(rim, "col", swap)
    near_body, near_span = (0, pad), (span - wide, 0)
    near_segments = (
        (None, 0, 0, half, rows, (0, 0), near_body, wide),
        ((2, 0), 1, 0, 0, half, near_span, near_body, wide),
        ((2, 1), 4, 0, 0, half, near_span, near_body, wide),
        ((1, 0), 2, 0, half + rows, half, near_span, near_body, wide),
        ((1, 1), 4, 0, half + rows, half, near_span, near_body, wide),
        (None, 3, 0, 0, 2 * rows, (0, 0), (wide, 0), pad),
    )
    near1, near_n = first_layer(
        flags, params, (near_x, above, below, rim, middle), near_segments, (pad, 0), strip
    )
    cross_near = lax.ppermute(near_n, "row", partner)
    two = 2 * pad
    far_side, rest_side = ((wide - two, 0), (0, mid)), ((0, span - mid), (two, 0))
    mid_segments = (
        (None, 0, 0, half, rows, (0, 0), (0, 0), mid + two),
        (None, 1, 0, 0, half, *far_side, two),
        (None, 2, 0, half + rows, half, *far_side, two),
        ((2, 0), 3, 0, 0, half, *rest_side, mid),
        ((2, 1), 5, 0, 0, half, *rest_side, mid),
        ((1, 0), 4, 0, half + rows, half, *rest_side, mid),
        ((1, 1), 5, 0, half + rows, half, *rest_side, mid),
    )
    mid1, mid_n = first_layer(
        flags,
        params,
        (
            mid_x, above_far, below_far, above, below, middle
        ),
        mid_segments,
        (pad, pad),
        mid,
    )
    cross_mid = lax.ppermute(mid_n, "row", partner)

    (near_side,) = copies(
        flags, (near_n, cross_far), ((None, 0, 0, rows, (strip - reach, 0), reach, 0, 0),)
    )
    near_side = lax.ppermute(near_side, "col", swap)
    def plain(body, weights, out, operands, scratch):
        return kernel_call(
            body,
            out,
            [smem_spec()] + [vmem_spec()] * (len(operands) + 2),
            [pltpu.VMEM((rows, width, channels), kind) for width in scratch],
        )(flags, scales, weights, *operands)

    def strip_shape(width, kind=kind):
        return jax.ShapeDtypeStruct((rows, width, channels), kind)

    acc, x1 = plain(
        partial_kernel,
        second_w,
        (strip_shape(cols, jnp.float32), strip_shape(cols)),
        (near_n, mid_n, far_n, cross_far, near_side, near1, mid1, far1),
        (cols + 2 * step, cols + 2 * step),
    )
    cross_near, acc = lax.optimization_barrier((cross_near, acc))
    (cross_side,) = copies(
        flags, (cross_near,), ((None, 0, 0, rows, (strip - step, 0), step, 0, 0),)
    )
    cross_side = lax.ppermute(cross_side, "col", swap)
    near2, near_n = plain(
        near_kernel,
        second_w,
        (strip_shape(reach), strip_shape(reach)),
        (cross_near, cross_side, acc, x1),
        (reach + 2 * step,),
    )
    near_n, cross_mid = lax.optimization_barrier((near_n, cross_mid))
    last_side = lax.ppermute(near_n, "col", swap)
    rest2, rest_n = plain(
        rest_kernel,
        second_w,
        (strip_shape(cols - reach), strip_shape(cols - reach)),
        (cross_mid, cross_near, acc, x1),
        (cols - reach + 2 * step,),
    )
    return plain(
        last_kernel,
        last_w,
        strip_shape(cols),
        (near2, rest2, near_n, rest_n, last_side),
        (cols + 2 * reach, cols),
    )


def shards(context_map, *params):
    rows, cols, _ = context_map.shape
    map_rows = lax.axis_size("row") * rows
    strip = dilations[1] + dilations[2]
    if (
        map_rows == 2 * dilations[1]
        and map_rows <= dilations[2]
        and rows == 2 * dilations[0]
        and dilations[1] % rows == 0
        and lax.axis_size("col") == 2
        and cols >= 2 * strip + 3 * lane_pad
        and cols % lane_pad == 0
    ):
        return by_halves(context_map, *params)
    return by_classes(context_map, *params)


def solution(mesh):
    return jax.shard_map(
        shards,
        mesh=mesh,
        in_specs=(P(("ctx", "row"), "col", None), P(), P(), P()),
        out_specs=P(("ctx", "row"), "col", None),
        check_vma=False,
    )
```

```python
import functools

import jax
import jax.numpy as jnp
from jax import lax
from jax.experimental import pallas as pl
from jax.experimental.pallas import tpu as pltpu
from jax.sharding import PartitionSpec as P

epsilon = 1e-05
dilations = (4, 32, 64)
lane_pad = 16
vmem_limit = 40 * 1024 * 1024


def extended(x, sides, width):
    for axis, dim in sides:
        size, length = (lax.axis_size(axis), x.shape[dim])
        up = [(i, (i + 1) % size) for i in range(size - 1)]
        down = [(j, i) for i, j in up]
        last = lax.slice_in_dim(x, length - width, length, axis=dim)
        first = lax.slice_in_dim(x, 0, width, axis=dim)
        before = lax.ppermute(last, axis, up)
        after = lax.ppermute(first, axis, down)
        x = jnp.concatenate([before, x, after], axis=dim)
    return x


def normalize(current, gain_row):
    values = current.astype(jnp.float32)
    centred = values - jnp.mean(values, axis=-1, keepdims=True)
    variance = jnp.mean(centred * centred, axis=-1, keepdims=True)
    return (centred * lax.rsqrt(variance + epsilon) * gain_row).astype(jnp.bfloat16)


def convolve(padded, kernel, row_step, col_step, out_rows, out_cols):
    channels = padded.shape[2]
    tap_list = []
    for tap_row in range(3):
        for tap_col in range(3):
            tap_list.append(
                lax.slice(
                    padded,
                    (tap_row * row_step, tap_col * col_step, 0),
                    (tap_row * row_step + out_rows, tap_col * col_step + out_cols, channels),
                )
            )
    stacked = jnp.concatenate(tap_list, axis=2).reshape(out_rows * out_cols, 9 * channels)
    product = jnp.dot(
        stacked, kernel.reshape(9 * channels, kernel.shape[3]), preferred_element_type=jnp.float32
    )
    return product.reshape(out_rows, out_cols, kernel.shape[3])


def update(current, response, bias_row):
    return (current.astype(jnp.float32) + jnp.maximum(response + bias_row, 0.0)).astype(
        jnp.bfloat16
    )


def by_classes(context_map, norm_gains, conv_biases, conv_weights):
    tile_rows, tile_cols, channels = context_map.shape
    normed = normalize(context_map, norm_gains[0])
    padded = extended(normed, (("row", 0), ("col", 1)), 4)
    current = update(
        context_map, convolve(padded, conv_weights[0], 4, 4, tile_rows, tile_cols), conv_biases[0]
    )
    class_count = lax.axis_size("row") // tile_rows
    sub_cols = tile_cols // class_count
    outgoing = (
        current.reshape(tile_rows, sub_cols, class_count, channels)
        .transpose(0, 2, 1, 3)
        .reshape(tile_rows * class_count, sub_cols, channels)
    )
    grouped = lax.all_to_all(outgoing, "row", split_axis=0, concat_axis=0, tiled=True)
    sub_rows = grouped.shape[0]
    for position, dilation in ((1, 32), (2, 64)):
        normed = normalize(grouped, norm_gains[position])
        row_gap = dilation // tile_rows
        col_gap = dilation // class_count
        with_sides = extended(normed, (("col", 1),), col_gap)
        padded = jnp.pad(with_sides, ((row_gap, row_gap), (0, 0), (0, 0)))
        response = convolve(padded, conv_weights[position], row_gap, col_gap, sub_rows, sub_cols)
        grouped = update(grouped, response, conv_biases[position])
    returned = lax.all_to_all(grouped, "row", split_axis=0, concat_axis=0, tiled=True)
    return (
        returned.reshape(tile_rows, class_count, sub_cols, channels)
        .transpose(0, 2, 1, 3)
        .reshape(tile_rows, tile_cols, channels)
    )


def vmem_spec():
    return pl.BlockSpec(memory_space=pltpu.VMEM)


def smem_spec():
    return pl.BlockSpec(memory_space=pltpu.SMEM)


def any_spec():
    return pl.BlockSpec(memory_space=pl.ANY)


def kernel_call(body, out_shape, in_specs, scratch):
    return pl.pallas_call(
        body,
        out_shape=out_shape,
        in_specs=in_specs,
        out_specs=jax.tree.map(lambda _: vmem_spec(), out_shape),
        scratch_shapes=scratch,
        compiler_params=pltpu.CompilerParams(vmem_limit_bytes=vmem_limit),
        cost_estimate=pl.CostEstimate(flops=1, bytes_accessed=1, transcendentals=0),
    )


def place(core, at_zero, at_one):
    return pl.multiple_of(jnp.where(core == 0, at_zero, at_one), lane_pad)


def guarded(flag_ref, condition, action):
    if condition is None:
        action()
    else:
        number, value = condition
        pl.when(flag_ref[number] == value)(action)


def copy_kernel(moves, inputs, flag_ref, *refs):
    sources, targets = refs[:inputs], refs[inputs:]

    def move(which, row, count, column, width, target, target_row):
        src = place(flag_ref[0], *column)
        for r in range(count):
            targets[target][target_row + r] = sources[which][row + r, pl.ds(src, width), :]

    for parts in moves:
        guarded(flag_ref, parts[0], functools.partial(move, *parts[1:]))


def copies(flags, arrays, moves):
    channels, kind = arrays[0].shape[2], arrays[0].dtype
    shapes = {}
    for _, _, _, count, _, width, target, target_row in moves:
        height = max(target_row + count, shapes.get(target, (0, 0))[0])
        shapes[target] = (height, width)
    out = tuple(
        jax.ShapeDtypeStruct(shapes[target] + (channels,), kind) for target in range(len(shapes))
    )
    return kernel_call(
        functools.partial(copy_kernel, moves, len(arrays)),
        out,
        [smem_spec()] + [vmem_spec()] * len(arrays),
        [],
    )(flags, *arrays)


def hold_kernel(flag_ref, gain_ref, bias_ref, w_ref, scale_ref, first_ref, second_ref, last_ref):
    scale_ref[0:3, :] = gain_ref[...]
    scale_ref[3:6, :] = bias_ref[...]
    first_ref[...] = w_ref[0]
    second_ref[0] = w_ref[1, 1]
    second_ref[1] = w_ref[1, flag_ref[3]]
    last_ref[...] = w_ref[2, 1]


def first_layer_kernel(segments, out_at, rows, width, flag_ref, scale_ref, w_ref, *rest):
    parts, (next_ref, normed_ref, window, taps) = rest[:-4], rest[-4:]
    core = flag_ref[0]
    half = rows // 2
    channels = window.shape[2]
    gain = scale_ref[0:1, :]

    def fill(which, source_row, window_row, count, source, target, columns):
        src, dst = place(core, *source), place(core, *target)
        for r in range(count):
            if which is None:
                values = jnp.zeros((columns, channels), window.dtype)
            else:
                values = normalize(
                    parts[which][source_row + r, pl.ds(src, columns), :], gain
                )
            window[window_row + r, pl.ds(dst, columns), :] = values

    for segment in segments:
        guarded(flag_ref, segment[0], functools.partial(fill, *segment[1:]))
    step = dilations[0]
    for b in range(3):
        first = lane_pad + (b - 1) * step
        for r in range(2 * rows):
            taps[b, r] = window[r, first : first + width, :]
    stacked = jnp.concatenate(
        [
            taps[b, a * half : a * half + rows].reshape(rows * width, channels)
            for a in range(3)
            for b in range(3)
        ],
        axis=1,
    )
    response = jnp.dot(
        stacked, w_ref[...].reshape(9 * channels, channels), preferred_element_type=jnp.float32
    )
    out_col = place(core, *out_at)
    current = parts[0][:, pl.ds(out_col, width), :].reshape(rows * width, channels)
    result = update(current, response, scale_ref[3:4, :])
    next_ref[...] = result.reshape(rows, width, channels)
    normed_ref[...] = normalize(result, scale_ref[1:2, :]).reshape(rows, width, channels)


def first_layer(flags, params, parts, segments, out_at, width):
    rows, _, channels = parts[0].shape
    kind = parts[0].dtype
    out = jax.ShapeDtypeStruct((rows, width, channels), kind)
    return kernel_call(
        functools.partial(first_layer_kernel, segments, out_at, rows, width),
        (out, out),
        [smem_spec()] + [vmem_spec()] * (2 + len(parts)),
        [
            pltpu.VMEM((2 * rows, width + 2 * lane_pad, channels), kind),
            pltpu.VMEM((3, 2 * rows, width, channels), kind),
        ],
    )(flags, *params, *parts)


def partial_kernel(
    flag_ref, scale_ref, w_ref, near_ref, mid_ref, far_ref, cfar_ref, side_ref, near1_ref, mid1_ref,
    far1_ref, acc_ref, next_ref, own, other,
):
    core = flag_ref[0]
    step = dilations[1]
    rows, near, channels = near_ref.shape
    mid, far = mid_ref.shape[1], far_ref.shape[1]
    cols = near + mid + far
    other[...] = jnp.zeros(other.shape, other.dtype)
    pieces = (
        (near_ref, near1_ref, (cols - near, 0)),
        (mid_ref, mid1_ref, (far, near)),
        (far_ref, far1_ref, (0, cols - far)),
    )
    for normed, current, at in pieces:
        width = normed.shape[1]
        next_ref[:, pl.ds(place(core, *at), width), :] = current[...]
        inside = pl.ds(place(core, at[0] + step, at[1] + step), width)
        own[:, inside, :] = normed[...]
        if normed is far_ref:
            other[:, inside, :] = cfar_ref[...]
    own[:, pl.ds(place(core, step + cols, 0), step), :] = side_ref[...]
    own[:, pl.ds(place(core, 0, step + cols), step), :] = jnp.zeros(
        (rows, step, channels), own.dtype
    )
    stacked = jnp.concatenate(
        [
            ref[:, b * step : b * step + cols, :].reshape(rows * cols, channels)
            for ref in (own, other)
            for b in range(3)
        ],
        axis=1,
    )
    acc_ref[...] = jnp.dot(
        stacked, w_ref[...].reshape(6 * channels, channels), preferred_element_type=jnp.float32
    ).reshape(rows, cols, channels)


def second_layer(flag_ref, scale_ref, w_ref, window, acc, current):
    step = dilations[1]
    rows, width, channels = current.shape
    cells = rows * width
    stacked = jnp.concatenate(
        [window[:, b * step : b * step + width, :].reshape(cells, channels) for b in range(3)],
        axis=1,
    )
    response = acc.reshape(cells, channels) + jnp.dot(
        stacked,
        w_ref[1].reshape(3 * channels, channels),
        preferred_element_type=jnp.float32,
    )
    result = update(current.reshape(cells, channels), response, scale_ref[4:5, :])
    normed = normalize(result, scale_ref[2:3, :])
    return result.reshape(current.shape), normed.reshape(current.shape)


def near_kernel(
    flag_ref, scale_ref, w_ref, cnear_ref, rim_ref, side_ref, acc_ref, x1_ref, next_ref, normed_ref,
    window,
):
    core = flag_ref[0]
    step, reach = dilations[1], dilations[2]
    near, cols = cnear_ref.shape[1], x1_ref.shape[1]
    window[:, pl.ds(place(core, 0, 2 * step), near), :] = cnear_ref[...]
    window[:, pl.ds(place(core, near, step), step), :] = rim_ref[...]
    window[:, pl.ds(place(core, near + step, 0), step), :] = side_ref[...]
    at = pl.ds(place(core, cols - reach, 0), reach)
    next_ref[...], normed_ref[...] = second_layer(
        flag_ref, scale_ref, w_ref, window[...], acc_ref[:, at, :], x1_ref[:, at, :]
    )


def rest_kernel(
    flag_ref, scale_ref, w_ref, cmid_ref, cnear_ref, acc_ref, x1_ref, next_ref, normed_ref, window
):
    core = flag_ref[0]
    step, reach = dilations[1], dilations[2]
    rows, mid, channels = cmid_ref.shape
    near, cols = cnear_ref.shape[1], x1_ref.shape[1]
    width, far = cols - reach, cols - near - step - mid
    count = width + step - far - mid
    window[:, pl.ds(place(core, step + far + mid, 0), count), :] = cnear_ref[
        :, pl.ds(place(core, 0, near - count), count), :
    ]
    window[:, pl.ds(place(core, step + far, count), mid), :] = cmid_ref[...]
    window[:, pl.ds(place(core, 0, count + mid), step + far), :] = jnp.zeros(
        (rows, step + far, channels), window.dtype
    )
    at = pl.ds(place(core, 0, reach), width)
    next_ref[...], normed_ref[...] = second_layer(
        flag_ref, scale_ref, w_ref, window[...], acc_ref[:, at, :], x1_ref[:, at, :]
    )


def last_kernel(
    flag_ref, scale_ref, w_ref, near2_ref, rest2_ref, near_ref, rest_ref, side_ref, out_ref, window,
    current,
):
    core = flag_ref[0]
    reach = dilations[2]
    rows, cols, channels = out_ref.shape
    rest = cols - reach
    dst = place(core, rest, 0)
    current[:, pl.ds(dst, reach), :] = near2_ref[...]
    window[:, pl.ds(pl.multiple_of(dst + reach, lane_pad), reach), :] = near_ref[...]
    dst = place(core, 0, reach)
    current[:, pl.ds(dst, rest), :] = rest2_ref[...]
    window[:, pl.ds(pl.multiple_of(dst + reach, lane_pad), rest), :] = rest_ref[...]
    window[:, pl.ds(place(core, reach + cols, 0), reach), :] = side_ref[...]
    window[:, pl.ds(place(core, 0, reach + cols), reach), :] = jnp.zeros(
        (rows, reach, channels), window.dtype
    )
    stacked = jnp.concatenate(
        [
            window[:, b * reach : b * reach + cols, :].reshape(rows * cols, channels)
            for b in range(3)
        ],
        axis=1,
    )
    response = jnp.dot(
        stacked, w_ref[...].reshape(3 * channels, channels), preferred_element_type=jnp.float32
    )
    out_ref[...] = update(
        current[...].reshape(rows * cols, channels), response, scale_ref[5:6, :]
    ).reshape(rows, cols, channels)


def by_halves(context_map, norm_gains, conv_biases, conv_weights):
    rows, cols, channels = context_map.shape
    kind = context_map.dtype
    size = lax.axis_size("row")
    group = size // 2
    half = rows // 2
    step, reach = dilations[1], dilations[2]
    strip = step + reach
    mid = cols - 2 * strip
    pad = lane_pad
    wide = strip + pad
    core, row = lax.axis_index("col"), lax.axis_index("row")
    upper_half = row < group
    flags = jnp.stack(
        [core, row == group - 1, row == group, jnp.where(upper_half, 2, 0)]
    ).astype(jnp.int32)
    swap = [(0, 1), (1, 0)]
    partner = [(i, (i + group) % size) for i in range(size)]
    down = [(i, i + 1) for i in range(size - 1)]
    up = [(j, i) for i, j in down]
    within_down = [(i, j) for i, j in down if j != group]
    within_up = [(j, i) for i, j in within_down]

    far_wide_at, near_wide_at = (0, cols - wide), (cols - wide, 0)
    span, span_at = cols - wide, (wide, 0)
    parts = (
        (None, 0, 0, rows, far_wide_at, wide, 0, 0),
        (None, 0, 0, rows, near_wide_at, wide, 1, 0),
        (None, 0, 0, rows, (strip - pad, strip - pad), mid + 2 * pad, 2, 0),
        (None, 0, half, half, far_wide_at, wide, 3, 0),
        (None, 0, 0, half, far_wide_at, wide, 4, 0),
        (None, 0, half, half, span_at, span, 5, 0),
        (None, 0, 0, half, span_at, span, 6, 0),
        ((1, 1), 0, half, half, span_at, span, 7, 0),
        ((1, 0), 0, 0, half, span_at, span, 7, 0),
    )
    (
        far_x, near_x, mid_x, far_low, far_high, low, high, middle
    ) = copies(flags, (context_map,), parts)
    above_far = lax.ppermute(far_low, "row", down)
    below_far = lax.ppermute(far_high, "row", up)
    above = lax.ppermute(low, "row", within_down)
    below = lax.ppermute(high, "row", within_up)
    middle = lax.ppermute(middle, "row", [(group - 1, group), (group, group - 1)])

    tail = conv_weights.shape[2:]
    scales, first_w, second_w, last_w = kernel_call(
        hold_kernel,
        (
            jax.ShapeDtypeStruct((2 * norm_gains.shape[0], channels), jnp.float32),
            jax.ShapeDtypeStruct((3,) + tail, kind),
            jax.ShapeDtypeStruct((2,) + tail, kind),
            jax.ShapeDtypeStruct(tail, kind),
        ),
        [smem_spec()] + [vmem_spec()] * 3,
        [],
    )(flags, norm_gains, conv_biases, conv_weights)
    params = (scales, first_w)
    far_body, far_edge = (pad, 0), (0, wide)
    far_segments = (
        (None, 0, 0, half, rows, (0, 0), far_body, wide),
        (None, 1, 0, 0, half, (0, 0), far_body, wide),
        (None, 2, 0, half + rows, half, (0, 0), far_body, wide),
        (None, None, 0, 0, 2 * rows, (0, 0), far_edge, pad),
    )
    far1, far_n = first_layer(
        flags, params, (far_x, above_far, below_far), far_segments, (0, pad), strip
    )
    cross_far = lax.ppermute(far_n, "row", partner)

    near_end, span_end = (wide - pad, 0), (span - pad, 0)
    (rim,) = copies(
        flags,
        (near_x, above, below, middle),
        (
            ((2, 0), 1, 0, half, span_end, pad, 0, 0),
            ((2, 1), 3, 0, half, span_end, pad, 0, 0),
            (None, 0, 0, rows, near_end, pad, 0, half),
            ((1, 0), 2, 0, half, span_end, pad, 0, half + rows),
            ((1, 1), 3, 0, half, span_end, pad, 0, half + rows),
        ),
    )
    rim = lax.ppermute(rim, "col", swap)
    near_body, near_span = (0, pad), (span - wide, 0)
    near_segments = (
        (None, 0, 0, half, rows, (0, 0), near_body, wide),
        ((2, 0), 1, 0, 0, half, near_span, near_body, wide),
        ((2, 1), 4, 0, 0, half, near_span, near_body, wide),
        ((1, 0), 2, 0, half + rows, half, near_span, near_body, wide),
        ((1, 1), 4, 0, half + rows, half, near_span, near_body, wide),
        (None, 3, 0, 0, 2 * rows, (0, 0), (wide, 0), pad),
    )
    near1, near_n = first_layer(
        flags, params, (near_x, above, below, rim, middle), near_segments, (pad, 0), strip
    )
    near_rim, near_rest = copies(
        flags,
        (near_n,),
        (
            (None, 0, 0, rows, (strip - step, 0), step, 0, 0),
            (None, 0, 0, rows, (0, step), strip - step, 1, 0),
        ),
    )
    cross_rim = lax.ppermute(near_rim, "row", partner)
    cross_near = lax.ppermute(near_rest, "row", partner)
    two = 2 * pad
    far_side, rest_side = ((wide - two, 0), (0, mid)), ((0, span - mid), (two, 0))
    mid_segments = (
        (None, 0, 0, half, rows, (0, 0), (0, 0), mid + two),
        (None, 1, 0, 0, half, *far_side, two),
        (None, 2, 0, half + rows, half, *far_side, two),
        ((2, 0), 3, 0, 0, half, *rest_side, mid),
        ((2, 1), 5, 0, 0, half, *rest_side, mid),
        ((1, 0), 4, 0, half + rows, half, *rest_side, mid),
        ((1, 1), 5, 0, half + rows, half, *rest_side, mid),
    )
    mid1, mid_n = first_layer(
        flags,
        params,
        (
            mid_x, above_far, below_far, above, below, middle
        ),
        mid_segments,
        (pad, pad),
        mid,
    )
    cross_mid = lax.ppermute(mid_n, "row", partner)

    near_rim, cross_far = lax.optimization_barrier((near_rim, cross_far))
    near_side = lax.ppermute(near_rim, "col", swap)
    def plain(body, weights, out, operands, scratch):
        return kernel_call(
            body,
            out,
            [smem_spec()] + [vmem_spec()] * (len(operands) + 2),
            [pltpu.VMEM((rows, width, channels), kind) for width in scratch],
        )(flags, scales, weights, *operands)

    def strip_shape(width, kind=kind):
        return jax.ShapeDtypeStruct((rows, width, channels), kind)

    acc, x1 = plain(
        partial_kernel,
        second_w,
        (strip_shape(cols, jnp.float32), strip_shape(cols)),
        (near_n, mid_n, far_n, cross_far, near_side, near1, mid1, far1),
        (cols + 2 * step, cols + 2 * step),
    )
    cross_side = lax.ppermute(cross_rim, "col", swap)
    near2, near_n = plain(
        near_kernel,
        second_w,
        (strip_shape(reach), strip_shape(reach)),
        (cross_near, cross_rim, cross_side, acc, x1),
        (reach + 2 * step,),
    )
    near_n, cross_mid = lax.optimization_barrier((near_n, cross_mid))
    last_side = lax.ppermute(near_n, "col", swap)
    rest2, rest_n = plain(
        rest_kernel,
        second_w,
        (strip_shape(cols - reach), strip_shape(cols - reach)),
        (cross_mid, cross_near, acc, x1),
        (cols - reach + 2 * step,),
    )
    return plain(
        last_kernel,
        last_w,
        strip_shape(cols),
        (near2, rest2, near_n, rest_n, last_side),
        (cols + 2 * reach, cols),
    )


def shards(context_map, *params):
    rows, cols, _ = context_map.shape
    map_rows = lax.axis_size("row") * rows
    strip = dilations[1] + dilations[2]
    if (
        map_rows == 2 * dilations[1]
        and map_rows <= dilations[2]
        and rows == 2 * dilations[0]
        and dilations[1] % rows == 0
        and lax.axis_size("col") == 2
        and cols >= 2 * strip + 3 * lane_pad
        and cols % lane_pad == 0
    ):
        return by_halves(context_map, *params)
    return by_classes(context_map, *params)


def solution(mesh):
    return jax.shard_map(
        shards,
        mesh=mesh,
        in_specs=(P(("ctx", "row"), "col", None), P(), P(), P()),
        out_specs=P(("ctx", "row"), "col", None),
        check_vma=False,
    )
```

```python
import functools

import jax
import jax.numpy as jnp
from jax import lax
from jax.experimental import pallas as pl
from jax.experimental.pallas import tpu as pltpu
from jax.sharding import PartitionSpec as P

epsilon = 1e-05
dilations = (4, 32, 64)
lane_pad = 16
vmem_limit = 40 * 1024 * 1024


def extended(x, sides, width):
    for axis, dim in sides:
        size, length = (lax.axis_size(axis), x.shape[dim])
        up = [(i, (i + 1) % size) for i in range(size - 1)]
        down = [(j, i) for i, j in up]
        last = lax.slice_in_dim(x, length - width, length, axis=dim)
        first = lax.slice_in_dim(x, 0, width, axis=dim)
        before = lax.ppermute(last, axis, up)
        after = lax.ppermute(first, axis, down)
        x = jnp.concatenate([before, x, after], axis=dim)
    return x


def normalize(current, gain_row):
    values = current.astype(jnp.float32)
    centred = values - jnp.mean(values, axis=-1, keepdims=True)
    variance = jnp.mean(centred * centred, axis=-1, keepdims=True)
    return (centred * lax.rsqrt(variance + epsilon) * gain_row).astype(jnp.bfloat16)


def convolve(padded, kernel, row_step, col_step, out_rows, out_cols):
    channels = padded.shape[2]
    tap_list = []
    for tap_row in range(3):
        for tap_col in range(3):
            tap_list.append(
                lax.slice(
                    padded,
                    (tap_row * row_step, tap_col * col_step, 0),
                    (tap_row * row_step + out_rows, tap_col * col_step + out_cols, channels),
                )
            )
    stacked = jnp.concatenate(tap_list, axis=2).reshape(out_rows * out_cols, 9 * channels)
    product = jnp.dot(
        stacked, kernel.reshape(9 * channels, kernel.shape[3]), preferred_element_type=jnp.float32
    )
    return product.reshape(out_rows, out_cols, kernel.shape[3])


def update(current, response, bias_row):
    return (current.astype(jnp.float32) + jnp.maximum(response + bias_row, 0.0)).astype(
        jnp.bfloat16
    )


def by_classes(context_map, norm_gains, conv_biases, conv_weights):
    tile_rows, tile_cols, channels = context_map.shape
    normed = normalize(context_map, norm_gains[0])
    padded = extended(normed, (("row", 0), ("col", 1)), 4)
    current = update(
        context_map, convolve(padded, conv_weights[0], 4, 4, tile_rows, tile_cols), conv_biases[0]
    )
    class_count = lax.axis_size("row") // tile_rows
    sub_cols = tile_cols // class_count
    outgoing = (
        current.reshape(tile_rows, sub_cols, class_count, channels)
        .transpose(0, 2, 1, 3)
        .reshape(tile_rows * class_count, sub_cols, channels)
    )
    grouped = lax.all_to_all(outgoing, "row", split_axis=0, concat_axis=0, tiled=True)
    sub_rows = grouped.shape[0]
    for position, dilation in ((1, 32), (2, 64)):
        normed = normalize(grouped, norm_gains[position])
        row_gap = dilation // tile_rows
        col_gap = dilation // class_count
        with_sides = extended(normed, (("col", 1),), col_gap)
        padded = jnp.pad(with_sides, ((row_gap, row_gap), (0, 0), (0, 0)))
        response = convolve(padded, conv_weights[position], row_gap, col_gap, sub_rows, sub_cols)
        grouped = update(grouped, response, conv_biases[position])
    returned = lax.all_to_all(grouped, "row", split_axis=0, concat_axis=0, tiled=True)
    return (
        returned.reshape(tile_rows, class_count, sub_cols, channels)
        .transpose(0, 2, 1, 3)
        .reshape(tile_rows, tile_cols, channels)
    )


def vmem_spec():
    return pl.BlockSpec(memory_space=pltpu.VMEM)


def smem_spec():
    return pl.BlockSpec(memory_space=pltpu.SMEM)


def any_spec():
    return pl.BlockSpec(memory_space=pl.ANY)


def kernel_call(body, out_shape, in_specs, scratch):
    return pl.pallas_call(
        body,
        out_shape=out_shape,
        in_specs=in_specs,
        out_specs=jax.tree.map(lambda _: vmem_spec(), out_shape),
        scratch_shapes=scratch,
        compiler_params=pltpu.CompilerParams(vmem_limit_bytes=vmem_limit),
        cost_estimate=pl.CostEstimate(flops=1, bytes_accessed=1, transcendentals=0),
    )


def place(core, at_zero, at_one):
    return pl.multiple_of(jnp.where(core == 0, at_zero, at_one), lane_pad)


def guarded(flag_ref, condition, action):
    if condition is None:
        action()
    else:
        number, value = condition
        pl.when(flag_ref[number] == value)(action)


def copy_kernel(moves, inputs, flag_ref, *refs):
    sources, targets = refs[:inputs], refs[inputs:]

    def move(which, row, count, column, width, target, target_row):
        src = place(flag_ref[0], *column)
        for r in range(count):
            targets[target][target_row + r] = sources[which][row + r, pl.ds(src, width), :]

    for parts in moves:
        guarded(flag_ref, parts[0], functools.partial(move, *parts[1:]))


def copies(flags, arrays, moves):
    channels, kind = arrays[0].shape[2], arrays[0].dtype
    shapes = {}
    for _, _, _, count, _, width, target, target_row in moves:
        height = max(target_row + count, shapes.get(target, (0, 0))[0])
        shapes[target] = (height, width)
    out = tuple(
        jax.ShapeDtypeStruct(shapes[target] + (channels,), kind) for target in range(len(shapes))
    )
    return kernel_call(
        functools.partial(copy_kernel, moves, len(arrays)),
        out,
        [smem_spec()] + [vmem_spec()] * len(arrays),
        [],
    )(flags, *arrays)


def hold_kernel(flag_ref, gain_ref, bias_ref, w_ref, scale_ref, first_ref, second_ref, last_ref):
    scale_ref[0:3, :] = gain_ref[...]
    scale_ref[3:6, :] = bias_ref[...]
    first_ref[...] = w_ref[0]
    second_ref[0] = w_ref[1, 1]
    second_ref[1] = w_ref[1, flag_ref[3]]
    last_ref[...] = w_ref[2, 1]


def first_layer_kernel(segments, out_at, rows, width, flag_ref, scale_ref, w_ref, *rest):
    parts, (next_ref, normed_ref, window, taps) = rest[:-4], rest[-4:]
    core = flag_ref[0]
    half = rows // 2
    channels = window.shape[2]
    gain = scale_ref[0:1, :]

    def fill(which, source_row, window_row, count, source, target, columns):
        src, dst = place(core, *source), place(core, *target)
        for r in range(count):
            if which is None:
                values = jnp.zeros((columns, channels), window.dtype)
            else:
                values = normalize(
                    parts[which][source_row + r, pl.ds(src, columns), :], gain
                )
            window[window_row + r, pl.ds(dst, columns), :] = values

    for segment in segments:
        guarded(flag_ref, segment[0], functools.partial(fill, *segment[1:]))
    step = dilations[0]
    for b in range(3):
        first = lane_pad + (b - 1) * step
        for r in range(2 * rows):
            taps[b, r] = window[r, first : first + width, :]
    stacked = jnp.concatenate(
        [
            taps[b, a * half : a * half + rows].reshape(rows * width, channels)
            for a in range(3)
            for b in range(3)
        ],
        axis=1,
    )
    response = jnp.dot(
        stacked, w_ref[...].reshape(9 * channels, channels), preferred_element_type=jnp.float32
    )
    out_col = place(core, *out_at)
    current = parts[0][:, pl.ds(out_col, width), :].reshape(rows * width, channels)
    result = update(current, response, scale_ref[3:4, :])
    next_ref[...] = result.reshape(rows, width, channels)
    normed_ref[...] = normalize(result, scale_ref[1:2, :]).reshape(rows, width, channels)


def first_layer(flags, params, parts, segments, out_at, width):
    rows, _, channels = parts[0].shape
    kind = parts[0].dtype
    out = jax.ShapeDtypeStruct((rows, width, channels), kind)
    return kernel_call(
        functools.partial(first_layer_kernel, segments, out_at, rows, width),
        (out, out),
        [smem_spec()] + [vmem_spec()] * (2 + len(parts)),
        [
            pltpu.VMEM((2 * rows, width + 2 * lane_pad, channels), kind),
            pltpu.VMEM((3, 2 * rows, width, channels), kind),
        ],
    )(flags, *params, *parts)


def partial_kernel(
    flag_ref, scale_ref, w_ref, near_ref, mid_ref, far_ref, cfar_ref, side_ref, near1_ref, mid1_ref,
    far1_ref, acc_ref, next_ref, own, other,
):
    core = flag_ref[0]
    step = dilations[1]
    rows, near, channels = near_ref.shape
    mid, far = mid_ref.shape[1], far_ref.shape[1]
    cols = near + mid + far
    other[...] = jnp.zeros(other.shape, other.dtype)
    pieces = (
        (near_ref, near1_ref, (cols - near, 0)),
        (mid_ref, mid1_ref, (far, near)),
        (far_ref, far1_ref, (0, cols - far)),
    )
    for normed, current, at in pieces:
        width = normed.shape[1]
        next_ref[:, pl.ds(place(core, *at), width), :] = current[...]
        inside = pl.ds(place(core, at[0] + step, at[1] + step), width)
        own[:, inside, :] = normed[...]
        if normed is far_ref:
            other[:, inside, :] = cfar_ref[...]
    own[:, pl.ds(place(core, step + cols, 0), step), :] = side_ref[...]
    own[:, pl.ds(place(core, 0, step + cols), step), :] = jnp.zeros(
        (rows, step, channels), own.dtype
    )
    stacked = jnp.concatenate(
        [
            ref[:, b * step : b * step + cols, :].reshape(rows * cols, channels)
            for ref in (own, other)
            for b in range(3)
        ],
        axis=1,
    )
    acc_ref[...] = jnp.dot(
        stacked, w_ref[...].reshape(6 * channels, channels), preferred_element_type=jnp.float32
    ).reshape(rows, cols, channels)


def second_layer(flag_ref, scale_ref, w_ref, window, acc, current):
    step = dilations[1]
    rows, width, channels = current.shape
    cells = rows * width
    stacked = jnp.concatenate(
        [window[:, b * step : b * step + width, :].reshape(cells, channels) for b in range(3)],
        axis=1,
    )
    response = acc.reshape(cells, channels) + jnp.dot(
        stacked,
        w_ref[1].reshape(3 * channels, channels),
        preferred_element_type=jnp.float32,
    )
    result = update(current.reshape(cells, channels), response, scale_ref[4:5, :])
    normed = normalize(result, scale_ref[2:3, :])
    return result.reshape(current.shape), normed.reshape(current.shape)


def near_kernel(
    flag_ref, scale_ref, w_ref, cnear_ref, rim_ref, side_ref, acc_ref, x1_ref, next_ref, normed_ref,
    window,
):
    core = flag_ref[0]
    step, reach = dilations[1], dilations[2]
    near, cols = cnear_ref.shape[1], x1_ref.shape[1]
    window[:, pl.ds(place(core, 0, 2 * step), near), :] = cnear_ref[...]
    window[:, pl.ds(place(core, near, step), step), :] = rim_ref[...]
    window[:, pl.ds(place(core, near + step, 0), step), :] = side_ref[...]
    at = pl.ds(place(core, cols - reach, 0), reach)
    next_ref[...], normed_ref[...] = second_layer(
        flag_ref, scale_ref, w_ref, window[...], acc_ref[:, at, :], x1_ref[:, at, :]
    )


def rest_kernel(
    flag_ref, scale_ref, w_ref, cmid_ref, cnear_ref, acc_ref, x1_ref, next_ref, normed_ref, window
):
    core = flag_ref[0]
    step, reach = dilations[1], dilations[2]
    rows, mid, channels = cmid_ref.shape
    near, cols = cnear_ref.shape[1], x1_ref.shape[1]
    width, far = cols - reach, cols - near - step - mid
    count = width + step - far - mid
    window[:, pl.ds(place(core, step + far + mid, 0), count), :] = cnear_ref[
        :, pl.ds(place(core, 0, near - count), count), :
    ]
    window[:, pl.ds(place(core, step + far, count), mid), :] = cmid_ref[...]
    window[:, pl.ds(place(core, 0, count + mid), step + far), :] = jnp.zeros(
        (rows, step + far, channels), window.dtype
    )
    at = pl.ds(place(core, 0, reach), width)
    next_ref[...], normed_ref[...] = second_layer(
        flag_ref, scale_ref, w_ref, window[...], acc_ref[:, at, :], x1_ref[:, at, :]
    )


def last_kernel(
    flag_ref, scale_ref, w_ref, near2_ref, rest2_ref, near_ref, rest_ref, side_ref, out_ref, window,
    current,
):
    core = flag_ref[0]
    reach = dilations[2]
    rows, cols, channels = out_ref.shape
    rest = cols - reach
    dst = place(core, rest, 0)
    current[:, pl.ds(dst, reach), :] = near2_ref[...]
    window[:, pl.ds(pl.multiple_of(dst + reach, lane_pad), reach), :] = near_ref[...]
    dst = place(core, 0, reach)
    current[:, pl.ds(dst, rest), :] = rest2_ref[...]
    window[:, pl.ds(pl.multiple_of(dst + reach, lane_pad), rest), :] = rest_ref[...]
    window[:, pl.ds(place(core, reach + cols, 0), reach), :] = side_ref[...]
    window[:, pl.ds(place(core, 0, reach + cols), reach), :] = jnp.zeros(
        (rows, reach, channels), window.dtype
    )
    stacked = jnp.concatenate(
        [
            window[:, b * reach : b * reach + cols, :].reshape(rows * cols, channels)
            for b in range(3)
        ],
        axis=1,
    )
    response = jnp.dot(
        stacked, w_ref[...].reshape(3 * channels, channels), preferred_element_type=jnp.float32
    )
    out_ref[...] = update(
        current[...].reshape(rows * cols, channels), response, scale_ref[5:6, :]
    ).reshape(rows, cols, channels)


def by_halves(context_map, norm_gains, conv_biases, conv_weights):
    rows, cols, channels = context_map.shape
    kind = context_map.dtype
    size = lax.axis_size("row")
    group = size // 2
    half = rows // 2
    step, reach = dilations[1], dilations[2]
    strip = step + reach
    mid = cols - 2 * strip
    pad = lane_pad
    wide = strip + pad
    core, row = lax.axis_index("col"), lax.axis_index("row")
    upper_half = row < group
    flags = jnp.stack(
        [core, row == group - 1, row == group, jnp.where(upper_half, 2, 0)]
    ).astype(jnp.int32)
    swap = [(0, 1), (1, 0)]
    partner = [(i, (i + group) % size) for i in range(size)]
    down = [(i, i + 1) for i in range(size - 1)]
    up = [(j, i) for i, j in down]
    within_down = [(i, j) for i, j in down if j != group]
    within_up = [(j, i) for i, j in within_down]

    far_wide_at, near_wide_at = (0, cols - wide), (cols - wide, 0)
    span, span_at = cols - wide, (wide, 0)
    middle_at = (wide - pad, 0)
    parts = (
        (None, 0, 0, rows, far_wide_at, wide, 0, 0),
        (None, 0, 0, rows, near_wide_at, wide, 1, 0),
        (None, 0, 0, rows, (strip - pad, strip - pad), mid + 2 * pad, 2, 0),
        (None, 0, half, half, far_wide_at, wide, 3, 0),
        (None, 0, 0, half, far_wide_at, wide, 4, 0),
        (None, 0, half, half, span_at, span, 5, 0),
        (None, 0, 0, half, span_at, span, 6, 0),
        ((1, 1), 0, half, half, middle_at, span + pad, 7, 0),
        ((1, 0), 0, 0, half, middle_at, span + pad, 7, 0),
    )
    (
        far_x, near_x, mid_x, far_low, far_high, low, high, middle
    ) = copies(flags, (context_map,), parts)
    above_far = lax.ppermute(far_low, "row", down)
    below_far = lax.ppermute(far_high, "row", up)
    tail = conv_weights.shape[2:]
    scales, first_w, second_w, last_w = kernel_call(
        hold_kernel,
        (
            jax.ShapeDtypeStruct((2 * norm_gains.shape[0], channels), jnp.float32),
            jax.ShapeDtypeStruct((3,) + tail, kind),
            jax.ShapeDtypeStruct((2,) + tail, kind),
            jax.ShapeDtypeStruct(tail, kind),
        ),
        [smem_spec()] + [vmem_spec()] * 3,
        [],
    )(flags, norm_gains, conv_biases, conv_weights)
    low, high, middle, scales = lax.optimization_barrier((low, high, middle, scales))
    above = lax.ppermute(low, "row", within_down)
    below = lax.ppermute(high, "row", within_up)
    middle = lax.ppermute(middle, "row", [(group - 1, group), (group, group - 1)])

    params = (scales, first_w)
    far_body, far_edge = (pad, 0), (0, wide)
    far_segments = (
        (None, 0, 0, half, rows, (0, 0), far_body, wide),
        (None, 1, 0, 0, half, (0, 0), far_body, wide),
        (None, 2, 0, half + rows, half, (0, 0), far_body, wide),
        (None, None, 0, 0, 2 * rows, (0, 0), far_edge, pad),
    )
    far1, far_n = first_layer(
        flags, params, (far_x, above_far, below_far), far_segments, (0, pad), strip
    )
    cross_far = lax.ppermute(far_n, "row", partner)

    near_end, span_end, middle_end = (wide - pad, 0), (span - pad, 0), (span, 0)
    (rim,) = copies(
        flags,
        (near_x, above, below, middle),
        (
            ((2, 0), 1, 0, half, span_end, pad, 0, 0),
            ((2, 1), 3, 0, half, middle_end, pad, 0, 0),
            (None, 0, 0, rows, near_end, pad, 0, half),
            ((1, 0), 2, 0, half, span_end, pad, 0, half + rows),
            ((1, 1), 3, 0, half, middle_end, pad, 0, half + rows),
        ),
    )
    rim = lax.ppermute(rim, "col", swap)
    near_body, near_span, near_middle = (0, pad), (span - wide, 0), (span + pad - wide, 0)
    near_segments = (
        (None, 0, 0, half, rows, (0, 0), near_body, wide),
        ((2, 0), 1, 0, 0, half, near_span, near_body, wide),
        ((2, 1), 4, 0, 0, half, near_middle, near_body, wide),
        ((1, 0), 2, 0, half + rows, half, near_span, near_body, wide),
        ((1, 1), 4, 0, half + rows, half, near_middle, near_body, wide),
        (None, 3, 0, 0, 2 * rows, (0, 0), (wide, 0), pad),
    )
    near1, near_n = first_layer(
        flags, params, (near_x, above, below, rim, middle), near_segments, (pad, 0), strip
    )
    near_rim, near_rest = copies(
        flags,
        (near_n,),
        (
            (None, 0, 0, rows, (strip - step, 0), step, 0, 0),
            (None, 0, 0, rows, (0, step), strip - step, 1, 0),
        ),
    )
    cross_rim = lax.ppermute(near_rim, "row", partner)
    cross_near = lax.ppermute(near_rest, "row", partner)
    two = 2 * pad
    far_side, rest_side = ((wide - two, 0), (0, mid)), ((0, span - mid), (two, 0))
    middle_side = ((pad, span - mid), (two, 0))
    mid_segments = (
        (None, 0, 0, half, rows, (0, 0), (0, 0), mid + two),
        (None, 1, 0, 0, half, *far_side, two),
        (None, 2, 0, half + rows, half, *far_side, two),
        ((2, 0), 3, 0, 0, half, *rest_side, mid),
        ((2, 1), 5, 0, 0, half, *middle_side, mid),
        ((1, 0), 4, 0, half + rows, half, *rest_side, mid),
        ((1, 1), 5, 0, half + rows, half, *middle_side, mid),
    )
    mid1, mid_n = first_layer(
        flags,
        params,
        (
            mid_x, above_far, below_far, above, below, middle
        ),
        mid_segments,
        (pad, pad),
        mid,
    )
    cross_mid = lax.ppermute(mid_n, "row", partner)

    near_rim, cross_far = lax.optimization_barrier((near_rim, cross_far))
    near_side = lax.ppermute(near_rim, "col", swap)
    def plain(body, weights, out, operands, scratch):
        return kernel_call(
            body,
            out,
            [smem_spec()] + [vmem_spec()] * (len(operands) + 2),
            [pltpu.VMEM((rows, width, channels), kind) for width in scratch],
        )(flags, scales, weights, *operands)

    def strip_shape(width, kind=kind):
        return jax.ShapeDtypeStruct((rows, width, channels), kind)

    acc, x1 = plain(
        partial_kernel,
        second_w,
        (strip_shape(cols, jnp.float32), strip_shape(cols)),
        (near_n, mid_n, far_n, cross_far, near_side, near1, mid1, far1),
        (cols + 2 * step, cols + 2 * step),
    )
    cross_side = lax.ppermute(cross_rim, "col", swap)
    near2, near_n = plain(
        near_kernel,
        second_w,
        (strip_shape(reach), strip_shape(reach)),
        (cross_near, cross_rim, cross_side, acc, x1),
        (reach + 2 * step,),
    )
    near_n, cross_mid = lax.optimization_barrier((near_n, cross_mid))
    last_side = lax.ppermute(near_n, "col", swap)
    rest2, rest_n = plain(
        rest_kernel,
        second_w,
        (strip_shape(cols - reach), strip_shape(cols - reach)),
        (cross_mid, cross_near, acc, x1),
        (cols - reach + 2 * step,),
    )
    return plain(
        last_kernel,
        last_w,
        strip_shape(cols),
        (near2, rest2, near_n, rest_n, last_side),
        (cols + 2 * reach, cols),
    )


def shards(context_map, *params):
    rows, cols, _ = context_map.shape
    map_rows = lax.axis_size("row") * rows
    strip = dilations[1] + dilations[2]
    if (
        map_rows == 2 * dilations[1]
        and map_rows <= dilations[2]
        and rows == 2 * dilations[0]
        and dilations[1] % rows == 0
        and lax.axis_size("col") == 2
        and cols >= 2 * strip + 3 * lane_pad
        and cols % lane_pad == 0
    ):
        return by_halves(context_map, *params)
    return by_classes(context_map, *params)


def solution(mesh):
    return jax.shard_map(
        shards,
        mesh=mesh,
        in_specs=(P(("ctx", "row"), "col", None), P(), P(), P()),
        out_specs=P(("ctx", "row"), "col", None),
        check_vma=False,
    )
```

```python
import functools

import jax
import jax.numpy as jnp
from jax import lax
from jax.experimental import pallas as pl
from jax.experimental.pallas import tpu as pltpu
from jax.sharding import PartitionSpec as P

epsilon = 1e-05
dilations = (4, 32, 64)
lane_pad = 16
vmem_limit = 40 * 1024 * 1024


def extended(x, sides, width):
    for axis, dim in sides:
        size, length = (lax.axis_size(axis), x.shape[dim])
        up = [(i, (i + 1) % size) for i in range(size - 1)]
        down = [(j, i) for i, j in up]
        last = lax.slice_in_dim(x, length - width, length, axis=dim)
        first = lax.slice_in_dim(x, 0, width, axis=dim)
        before = lax.ppermute(last, axis, up)
        after = lax.ppermute(first, axis, down)
        x = jnp.concatenate([before, x, after], axis=dim)
    return x


def normalize(current, gain_row):
    values = current.astype(jnp.float32)
    centred = values - jnp.mean(values, axis=-1, keepdims=True)
    variance = jnp.mean(centred * centred, axis=-1, keepdims=True)
    return (centred * lax.rsqrt(variance + epsilon) * gain_row).astype(jnp.bfloat16)


def convolve(padded, kernel, row_step, col_step, out_rows, out_cols):
    channels = padded.shape[2]
    tap_list = []
    for tap_row in range(3):
        for tap_col in range(3):
            tap_list.append(
                lax.slice(
                    padded,
                    (tap_row * row_step, tap_col * col_step, 0),
                    (tap_row * row_step + out_rows, tap_col * col_step + out_cols, channels),
                )
            )
    stacked = jnp.concatenate(tap_list, axis=2).reshape(out_rows * out_cols, 9 * channels)
    product = jnp.dot(
        stacked, kernel.reshape(9 * channels, kernel.shape[3]), preferred_element_type=jnp.float32
    )
    return product.reshape(out_rows, out_cols, kernel.shape[3])


def update(current, response, bias_row):
    return (current.astype(jnp.float32) + jnp.maximum(response + bias_row, 0.0)).astype(
        jnp.bfloat16
    )


def by_classes(context_map, norm_gains, conv_biases, conv_weights):
    tile_rows, tile_cols, channels = context_map.shape
    normed = normalize(context_map, norm_gains[0])
    padded = extended(normed, (("row", 0), ("col", 1)), 4)
    current = update(
        context_map, convolve(padded, conv_weights[0], 4, 4, tile_rows, tile_cols), conv_biases[0]
    )
    class_count = lax.axis_size("row") // tile_rows
    sub_cols = tile_cols // class_count
    outgoing = (
        current.reshape(tile_rows, sub_cols, class_count, channels)
        .transpose(0, 2, 1, 3)
        .reshape(tile_rows * class_count, sub_cols, channels)
    )
    grouped = lax.all_to_all(outgoing, "row", split_axis=0, concat_axis=0, tiled=True)
    sub_rows = grouped.shape[0]
    for position, dilation in ((1, 32), (2, 64)):
        normed = normalize(grouped, norm_gains[position])
        row_gap = dilation // tile_rows
        col_gap = dilation // class_count
        with_sides = extended(normed, (("col", 1),), col_gap)
        padded = jnp.pad(with_sides, ((row_gap, row_gap), (0, 0), (0, 0)))
        response = convolve(padded, conv_weights[position], row_gap, col_gap, sub_rows, sub_cols)
        grouped = update(grouped, response, conv_biases[position])
    returned = lax.all_to_all(grouped, "row", split_axis=0, concat_axis=0, tiled=True)
    return (
        returned.reshape(tile_rows, class_count, sub_cols, channels)
        .transpose(0, 2, 1, 3)
        .reshape(tile_rows, tile_cols, channels)
    )


def vmem_spec():
    return pl.BlockSpec(memory_space=pltpu.VMEM)


def smem_spec():
    return pl.BlockSpec(memory_space=pltpu.SMEM)


def any_spec():
    return pl.BlockSpec(memory_space=pl.ANY)


def kernel_call(body, out_shape, in_specs, scratch, out_specs=None):
    return pl.pallas_call(
        body,
        out_shape=out_shape,
        in_specs=in_specs,
        out_specs=out_specs or jax.tree.map(lambda _: vmem_spec(), out_shape),
        scratch_shapes=scratch,
        compiler_params=pltpu.CompilerParams(vmem_limit_bytes=vmem_limit),
        cost_estimate=pl.CostEstimate(flops=1, bytes_accessed=1, transcendentals=0),
    )


def place(core, at_zero, at_one):
    return pl.multiple_of(jnp.where(core == 0, at_zero, at_one), lane_pad)


def guarded(flag_ref, condition, action):
    if condition is None:
        action()
    else:
        number, value = condition
        pl.when(flag_ref[number] == value)(action)


def copy_kernel(moves, inputs, flag_ref, *refs):
    sources, targets = refs[:inputs], refs[inputs:]

    def move(which, row, count, column, width, target, target_row):
        src = place(flag_ref[0], *column)
        for r in range(count):
            targets[target][target_row + r] = sources[which][row + r, pl.ds(src, width), :]

    for parts in moves:
        guarded(flag_ref, parts[0], functools.partial(move, *parts[1:]))


def copies(flags, arrays, moves):
    channels, kind = arrays[0].shape[2], arrays[0].dtype
    shapes = {}
    for _, _, _, count, _, width, target, target_row in moves:
        height = max(target_row + count, shapes.get(target, (0, 0))[0])
        shapes[target] = (height, width)
    out = tuple(
        jax.ShapeDtypeStruct(shapes[target] + (channels,), kind) for target in range(len(shapes))
    )
    return kernel_call(
        functools.partial(copy_kernel, moves, len(arrays)),
        out,
        [smem_spec()] + [vmem_spec()] * len(arrays),
        [],
    )(flags, *arrays)


def hold_kernel(flag_ref, gain_ref, bias_ref, w_ref, scale_ref, first_ref, second_ref, last_ref):
    scale_ref[0:3, :] = gain_ref[...]
    scale_ref[3:6, :] = bias_ref[...]
    first_ref[...] = w_ref[0]
    second_ref[0] = w_ref[1, 1]
    second_ref[1] = w_ref[1, flag_ref[3]]
    last_ref[...] = w_ref[2, 1]


def first_layer_kernel(segments, out_at, rows, width, flag_ref, scale_ref, w_ref, *rest):
    parts, (next_ref, normed_ref, window, taps) = rest[:-4], rest[-4:]
    core = flag_ref[0]
    half = rows // 2
    channels = window.shape[2]
    gain = scale_ref[0:1, :]

    def fill(which, source_row, window_row, count, source, target, columns):
        src, dst = place(core, *source), place(core, *target)
        for r in range(count):
            if which is None:
                values = jnp.zeros((columns, channels), window.dtype)
            else:
                values = normalize(
                    parts[which][source_row + r, pl.ds(src, columns), :], gain
                )
            window[window_row + r, pl.ds(dst, columns), :] = values

    for segment in segments:
        guarded(flag_ref, segment[0], functools.partial(fill, *segment[1:]))
    step = dilations[0]
    for b in range(3):
        first = lane_pad + (b - 1) * step
        for r in range(2 * rows):
            taps[b, r] = window[r, first : first + width, :]
    stacked = jnp.concatenate(
        [
            taps[b, a * half : a * half + rows].reshape(rows * width, channels)
            for a in range(3)
            for b in range(3)
        ],
        axis=1,
    )
    response = jnp.dot(
        stacked, w_ref[...].reshape(9 * channels, channels), preferred_element_type=jnp.float32
    )
    out_col = place(core, *out_at)
    current = parts[0][:, pl.ds(out_col, width), :].reshape(rows * width, channels)
    result = update(current, response, scale_ref[3:4, :])
    next_ref[...] = result.reshape(rows, width, channels)
    normed_ref[...] = normalize(result, scale_ref[1:2, :]).reshape(rows, width, channels)


def first_layer(flags, params, parts, segments, out_at, width):
    rows, _, channels = parts[0].shape
    kind = parts[0].dtype
    out = jax.ShapeDtypeStruct((rows, width, channels), kind)
    return kernel_call(
        functools.partial(first_layer_kernel, segments, out_at, rows, width),
        (out, out),
        [smem_spec()] + [vmem_spec()] * (2 + len(parts)),
        [
            pltpu.VMEM((2 * rows, width + 2 * lane_pad, channels), kind),
            pltpu.VMEM((3, 2 * rows, width, channels), kind),
        ],
    )(flags, *params, *parts)


def partial_kernel(
    flag_ref, scale_ref, w_ref, near_ref, mid_ref, far_ref, cfar_ref, side_ref, near1_ref, mid1_ref,
    far1_ref, acc_ref, next_ref, far2_ref, farn_ref, own, other,
):
    core = flag_ref[0]
    step = dilations[1]
    rows, near, channels = near_ref.shape
    mid, far = mid_ref.shape[1], far_ref.shape[1]
    cols = near + mid + far
    other[...] = jnp.zeros(other.shape, other.dtype)
    pieces = (
        (near_ref, near1_ref, (cols - near, 0)),
        (mid_ref, mid1_ref, (far, near)),
        (far_ref, far1_ref, (0, cols - far)),
    )
    for normed, current, at in pieces:
        width = normed.shape[1]
        next_ref[:, pl.ds(place(core, *at), width), :] = current[...]
        inside = pl.ds(place(core, at[0] + step, at[1] + step), width)
        own[:, inside, :] = normed[...]
        if normed is far_ref:
            other[:, inside, :] = cfar_ref[...]
    own[:, pl.ds(place(core, step + cols, 0), step), :] = side_ref[...]
    own[:, pl.ds(place(core, 0, step + cols), step), :] = jnp.zeros(
        (rows, step, channels), own.dtype
    )
    stacked = jnp.concatenate(
        [
            ref[:, b * step : b * step + cols, :].reshape(rows * cols, channels)
            for ref in (own, other)
            for b in range(3)
        ],
        axis=1,
    )
    acc_ref[...] = jnp.dot(
        stacked, w_ref[...].reshape(6 * channels, channels), preferred_element_type=jnp.float32
    ).reshape(rows, cols, channels)
    edge = pl.ds(place(core, 0, cols - far2_ref.shape[1]), far2_ref.shape[1])
    far2_ref[...], farn_ref[...] = after_second(
        scale_ref, acc_ref[:, edge, :], next_ref[:, edge, :]
    )


def second_layer(flag_ref, scale_ref, w_ref, window, acc, current):
    step = dilations[1]
    rows, width, channels = current.shape
    cells = rows * width
    stacked = jnp.concatenate(
        [window[:, b * step : b * step + width, :].reshape(cells, channels) for b in range(3)],
        axis=1,
    )
    response = acc.reshape(cells, channels) + jnp.dot(
        stacked,
        w_ref[1].reshape(3 * channels, channels),
        preferred_element_type=jnp.float32,
    )
    return after_second(scale_ref, response, current)


def after_second(scale_ref, response, current):
    cells, channels = current.shape[0] * current.shape[1], current.shape[2]
    result = update(
        current.reshape(cells, channels), response.reshape(cells, channels), scale_ref[4:5, :]
    )
    normed = normalize(result, scale_ref[2:3, :])
    return result.reshape(current.shape), normed.reshape(current.shape)


def near_kernel(
    flag_ref, scale_ref, w_ref, cnear_ref, rim_ref, side_ref, acc_ref, x1_ref, next_ref, normed_ref,
    window,
):
    core = flag_ref[0]
    step, reach = dilations[1], dilations[2]
    near, cols = cnear_ref.shape[1], x1_ref.shape[1]
    window[:, pl.ds(place(core, 0, 2 * step), near), :] = cnear_ref[...]
    window[:, pl.ds(place(core, near, step), step), :] = rim_ref[...]
    window[:, pl.ds(place(core, near + step, 0), step), :] = side_ref[...]
    at = pl.ds(place(core, cols - reach, 0), reach)
    next_ref[...], normed_ref[...] = second_layer(
        flag_ref, scale_ref, w_ref, window[...], acc_ref[:, at, :], x1_ref[:, at, :]
    )


def mid_kernel(
    flag_ref, scale_ref, w_ref, cmid_ref, cnear_ref, acc_ref, x1_ref, next_ref, normed_ref, window
):
    core = flag_ref[0]
    step, reach = dilations[1], dilations[2]
    rows, mid, channels = cmid_ref.shape
    near, width = cnear_ref.shape[1], next_ref.shape[1]
    blank = width + 2 * step - near - mid
    window[:, pl.ds(place(core, blank + mid, 0), near), :] = cnear_ref[...]
    window[:, pl.ds(place(core, blank, near), mid), :] = cmid_ref[...]
    window[:, pl.ds(place(core, 0, near + mid), blank), :] = jnp.zeros(
        (rows, blank, channels), window.dtype
    )
    at = pl.ds(place(core, x1_ref.shape[1] - reach - width, reach), width)
    next_ref[...], normed_ref[...] = second_layer(
        flag_ref, scale_ref, w_ref, window[...], acc_ref[:, at, :], x1_ref[:, at, :]
    )


def sides_kernel(
    flag_ref, scale_ref, w_ref, near2_ref, far2_ref, near_ref, far_ref, acc_ref, ends_ref, normed
):
    core = flag_ref[0]
    rows, reach, channels = near_ref.shape
    ends_ref[core], ends_ref[1 - core] = far2_ref[...], near2_ref[...]
    normed[core], normed[1 - core] = far_ref[...], near_ref[...]
    for block, (end, tap) in enumerate(((0, 1), (0, 0), (1, 2), (1, 1))):
        acc_ref[:, block * reach : (block + 1) * reach, :] = jnp.dot(
            normed[end].reshape(rows * reach, channels),
            w_ref[tap],
            preferred_element_type=jnp.float32,
        ).reshape(rows, reach, channels)


def last_kernel(
    flag_ref, scale_ref, w_ref, ends_ref, mid2_ref, mid_ref, side_ref, acc_ref, out_ref, total,
    result, sems,
):
    core = flag_ref[0]
    rows, reach, channels = side_ref.shape
    cells = rows * reach
    side = side_ref[...].reshape(cells, channels)
    nothing = jnp.zeros_like(side)
    inner = [
        mid_ref[:, at * reach : (at + 1) * reach, :].reshape(cells, channels) for at in range(2)
    ]
    blocks = (
        (inner[0], 2, jnp.where(core == 1, side, nothing), 0, ends_ref[0]),
        (inner[0], 1, inner[1], 2, mid2_ref[:, 0:reach, :]),
        (inner[0], 0, inner[1], 1, mid2_ref[:, reach : 2 * reach, :]),
        (inner[1], 0, jnp.where(core == 0, side, nothing), 2, ends_ref[1]),
    )
    for block, (one, tap, two, other_tap, _) in enumerate(blocks):
        at = slice(block * reach, (block + 1) * reach)
        total[:, at, :] = acc_ref[:, at, :] + jnp.dot(
            jnp.concatenate([one, two], axis=1),
            jnp.concatenate([w_ref[tap], w_ref[other_tap]], axis=0),
            preferred_element_type=jnp.float32,
        ).reshape(rows, reach, channels)
    leaving = [pltpu.make_async_copy(result.at[r], out_ref.at[r], sems.at[r]) for r in range(rows)]
    for r in range(rows):
        for block, (*_, current) in enumerate(blocks):
            at = slice(block * reach, (block + 1) * reach)
            result[r, at, :] = update(current[r], total[r, at, :], scale_ref[5:6, :])
        leaving[r].start()
    for copy in leaving:
        copy.wait()


def by_halves(context_map, norm_gains, conv_biases, conv_weights):
    rows, cols, channels = context_map.shape
    kind = context_map.dtype
    size = lax.axis_size("row")
    group = size // 2
    half = rows // 2
    step, reach = dilations[1], dilations[2]
    strip = step + reach
    mid = cols - 2 * strip
    pad = lane_pad
    wide = strip + pad
    core, row = lax.axis_index("col"), lax.axis_index("row")
    upper_half = row < group
    flags = jnp.stack(
        [core, row == group - 1, row == group, jnp.where(upper_half, 2, 0)]
    ).astype(jnp.int32)
    swap = [(0, 1), (1, 0)]
    partner = [(i, (i + group) % size) for i in range(size)]
    down = [(i, i + 1) for i in range(size - 1)]
    up = [(j, i) for i, j in down]
    within_down = [(i, j) for i, j in down if j != group]
    within_up = [(j, i) for i, j in within_down]

    far_wide_at, near_wide_at = (0, cols - wide), (cols - wide, 0)
    span, span_at = cols - wide, (wide, 0)
    middle_at = (wide - pad, 0)
    parts = (
        (None, 0, 0, rows, far_wide_at, wide, 0, 0),
        (None, 0, 0, rows, near_wide_at, wide, 1, 0),
        (None, 0, 0, rows, (strip - pad, strip - pad), mid + 2 * pad, 2, 0),
        (None, 0, half, half, far_wide_at, wide, 3, 0),
        (None, 0, 0, half, far_wide_at, wide, 4, 0),
        (None, 0, half, half, span_at, span, 5, 0),
        (None, 0, 0, half, span_at, span, 6, 0),
        ((1, 1), 0, half, half, middle_at, span + pad, 7, 0),
        ((1, 0), 0, 0, half, middle_at, span + pad, 7, 0),
    )
    (
        far_x, near_x, mid_x, far_low, far_high, low, high, middle
    ) = copies(flags, (context_map,), parts)
    above_far = lax.ppermute(far_low, "row", down)
    below_far = lax.ppermute(far_high, "row", up)
    tail = conv_weights.shape[2:]
    scales, first_w, second_w, last_w = kernel_call(
        hold_kernel,
        (
            jax.ShapeDtypeStruct((2 * norm_gains.shape[0], channels), jnp.float32),
            jax.ShapeDtypeStruct((3,) + tail, kind),
            jax.ShapeDtypeStruct((2,) + tail, kind),
            jax.ShapeDtypeStruct(tail, kind),
        ),
        [smem_spec()] + [vmem_spec()] * 3,
        [],
    )(flags, norm_gains, conv_biases, conv_weights)
    low, high, middle, scales = lax.optimization_barrier((low, high, middle, scales))
    above = lax.ppermute(low, "row", within_down)
    below = lax.ppermute(high, "row", within_up)
    middle = lax.ppermute(middle, "row", [(group - 1, group), (group, group - 1)])

    params = (scales, first_w)
    far_body, far_edge = (pad, 0), (0, wide)
    far_segments = (
        (None, 0, 0, half, rows, (0, 0), far_body, wide),
        (None, 1, 0, 0, half, (0, 0), far_body, wide),
        (None, 2, 0, half + rows, half, (0, 0), far_body, wide),
        (None, None, 0, 0, 2 * rows, (0, 0), far_edge, pad),
    )
    far1, far_n = first_layer(
        flags, params, (far_x, above_far, below_far), far_segments, (0, pad), strip
    )
    cross_far = lax.ppermute(far_n, "row", partner)

    near_end, span_end, middle_end = (wide - pad, 0), (span - pad, 0), (span, 0)
    (rim,) = copies(
        flags,
        (near_x, above, below, middle),
        (
            ((2, 0), 1, 0, half, span_end, pad, 0, 0),
            ((2, 1), 3, 0, half, middle_end, pad, 0, 0),
            (None, 0, 0, rows, near_end, pad, 0, half),
            ((1, 0), 2, 0, half, span_end, pad, 0, half + rows),
            ((1, 1), 3, 0, half, middle_end, pad, 0, half + rows),
        ),
    )
    rim = lax.ppermute(rim, "col", swap)
    near_body, near_span, near_middle = (0, pad), (span - wide, 0), (span + pad - wide, 0)
    near_segments = (
        (None, 0, 0, half, rows, (0, 0), near_body, wide),
        ((2, 0), 1, 0, 0, half, near_span, near_body, wide),
        ((2, 1), 4, 0, 0, half, near_middle, near_body, wide),
        ((1, 0), 2, 0, half + rows, half, near_span, near_body, wide),
        ((1, 1), 4, 0, half + rows, half, near_middle, near_body, wide),
        (None, 3, 0, 0, 2 * rows, (0, 0), (wide, 0), pad),
    )
    near1, near_n = first_layer(
        flags, params, (near_x, above, below, rim, middle), near_segments, (pad, 0), strip
    )
    near_rim, near_rest = copies(
        flags,
        (near_n,),
        (
            (None, 0, 0, rows, (strip - step, 0), step, 0, 0),
            (None, 0, 0, rows, (0, step), strip - step, 1, 0),
        ),
    )
    cross_rim = lax.ppermute(near_rim, "row", partner)
    cross_near = lax.ppermute(near_rest, "row", partner)
    two = 2 * pad
    far_side, rest_side = ((wide - two, 0), (0, mid)), ((0, span - mid), (two, 0))
    middle_side = ((pad, span - mid), (two, 0))
    mid_segments = (
        (None, 0, 0, half, rows, (0, 0), (0, 0), mid + two),
        (None, 1, 0, 0, half, *far_side, two),
        (None, 2, 0, half + rows, half, *far_side, two),
        ((2, 0), 3, 0, 0, half, *rest_side, mid),
        ((2, 1), 5, 0, 0, half, *middle_side, mid),
        ((1, 0), 4, 0, half + rows, half, *rest_side, mid),
        ((1, 1), 5, 0, half + rows, half, *middle_side, mid),
    )
    mid1, mid_n = first_layer(
        flags,
        params,
        (
            mid_x, above_far, below_far, above, below, middle
        ),
        mid_segments,
        (pad, pad),
        mid,
    )
    cross_mid = lax.ppermute(mid_n, "row", partner)

    near_rim, cross_far = lax.optimization_barrier((near_rim, cross_far))
    near_side = lax.ppermute(near_rim, "col", swap)
    def plain(body, weights, out, operands, scratch, more=()):
        return kernel_call(
            body,
            out,
            [smem_spec()] + [vmem_spec()] * (len(operands) + 2),
            [pltpu.VMEM((rows, width, channels), kind) for width in scratch] + list(more),
        )(flags, scales, weights, *operands)

    def strip_shape(width, kind=kind):
        return jax.ShapeDtypeStruct((rows, width, channels), kind)

    acc, x1, far2, far_n = plain(
        partial_kernel,
        second_w,
        (
            strip_shape(cols, jnp.float32),
            strip_shape(cols),
            strip_shape(strip - step),
            strip_shape(strip - step),
        ),
        (near_n, mid_n, far_n, cross_far, near_side, near1, mid1, far1),
        (cols + 2 * step, cols + 2 * step),
    )
    cross_side = lax.ppermute(cross_rim, "col", swap)
    near2, near_n = plain(
        near_kernel,
        second_w,
        (strip_shape(reach), strip_shape(reach)),
        (cross_near, cross_rim, cross_side, acc, x1),
        (reach + 2 * step,),
    )
    sums, ends = plain(
        sides_kernel,
        last_w,
        (
            strip_shape(cols, jnp.float32),
            jax.ShapeDtypeStruct((2, rows, reach, channels), kind),
        ),
        (near2, far2, near_n, far_n),
        (),
        [pltpu.VMEM((2, rows, reach, channels), kind)],
    )
    near_n, cross_mid, sums = lax.optimization_barrier((near_n, cross_mid, sums))
    last_side = lax.ppermute(near_n, "col", swap)
    mid2, mid_n = plain(
        mid_kernel,
        second_w,
        (strip_shape(2 * reach), strip_shape(2 * reach)),
        (cross_mid, cross_near, acc, x1),
        (2 * reach + 2 * step,),
    )
    return kernel_call(
        last_kernel,
        strip_shape(cols),
        [smem_spec()] + [vmem_spec()] * 7,
        [
            pltpu.VMEM((rows, cols, channels), jnp.float32),
            pltpu.VMEM((rows, cols, channels), kind),
            pltpu.SemaphoreType.DMA((rows,)),
        ],
        any_spec(),
    )(flags, scales, last_w, ends, mid2, mid_n, last_side, sums)


def shards(context_map, *params):
    rows, cols, _ = context_map.shape
    map_rows = lax.axis_size("row") * rows
    strip = dilations[1] + dilations[2]
    if (
        map_rows == 2 * dilations[1]
        and map_rows <= dilations[2]
        and rows == 2 * dilations[0]
        and dilations[1] % rows == 0
        and lax.axis_size("col") == 2
        and cols == 4 * dilations[2]
        and dilations[2] == 2 * dilations[1]
    ):
        return by_halves(context_map, *params)
    return by_classes(context_map, *params)


def solution(mesh):
    return jax.shard_map(
        shards,
        mesh=mesh,
        in_specs=(P(("ctx", "row"), "col", None), P(), P(), P()),
        out_specs=P(("ctx", "row"), "col", None),
        check_vma=False,
    )
```

```python
import functools

import jax
import jax.numpy as jnp
from jax import lax
from jax.experimental import pallas as pl
from jax.experimental.pallas import tpu as pltpu
from jax.sharding import PartitionSpec as P

epsilon = 1e-05
dilations = (4, 32, 64)
lane_pad = 16
vmem_limit = 40 * 1024 * 1024


def extended(x, sides, width):
    for axis, dim in sides:
        size, length = (lax.axis_size(axis), x.shape[dim])
        up = [(i, (i + 1) % size) for i in range(size - 1)]
        down = [(j, i) for i, j in up]
        last = lax.slice_in_dim(x, length - width, length, axis=dim)
        first = lax.slice_in_dim(x, 0, width, axis=dim)
        before = lax.ppermute(last, axis, up)
        after = lax.ppermute(first, axis, down)
        x = jnp.concatenate([before, x, after], axis=dim)
    return x


def normalize(current, gain_row):
    values = current.astype(jnp.float32)
    centred = values - jnp.mean(values, axis=-1, keepdims=True)
    variance = jnp.mean(centred * centred, axis=-1, keepdims=True)
    return (centred * lax.rsqrt(variance + epsilon) * gain_row).astype(jnp.bfloat16)


def convolve(padded, kernel, row_step, col_step, out_rows, out_cols):
    channels = padded.shape[2]
    tap_list = []
    for tap_row in range(3):
        for tap_col in range(3):
            tap_list.append(
                lax.slice(
                    padded,
                    (tap_row * row_step, tap_col * col_step, 0),
                    (tap_row * row_step + out_rows, tap_col * col_step + out_cols, channels),
                )
            )
    stacked = jnp.concatenate(tap_list, axis=2).reshape(out_rows * out_cols, 9 * channels)
    product = jnp.dot(
        stacked, kernel.reshape(9 * channels, kernel.shape[3]), preferred_element_type=jnp.float32
    )
    return product.reshape(out_rows, out_cols, kernel.shape[3])


def update(current, response, bias_row):
    return (current.astype(jnp.float32) + jnp.maximum(response + bias_row, 0.0)).astype(
        jnp.bfloat16
    )


def by_classes(context_map, norm_gains, conv_biases, conv_weights):
    tile_rows, tile_cols, channels = context_map.shape
    normed = normalize(context_map, norm_gains[0])
    padded = extended(normed, (("row", 0), ("col", 1)), 4)
    current = update(
        context_map, convolve(padded, conv_weights[0], 4, 4, tile_rows, tile_cols), conv_biases[0]
    )
    class_count = lax.axis_size("row") // tile_rows
    sub_cols = tile_cols // class_count
    outgoing = (
        current.reshape(tile_rows, sub_cols, class_count, channels)
        .transpose(0, 2, 1, 3)
        .reshape(tile_rows * class_count, sub_cols, channels)
    )
    grouped = lax.all_to_all(outgoing, "row", split_axis=0, concat_axis=0, tiled=True)
    sub_rows = grouped.shape[0]
    for position, dilation in ((1, 32), (2, 64)):
        normed = normalize(grouped, norm_gains[position])
        row_gap = dilation // tile_rows
        col_gap = dilation // class_count
        with_sides = extended(normed, (("col", 1),), col_gap)
        padded = jnp.pad(with_sides, ((row_gap, row_gap), (0, 0), (0, 0)))
        response = convolve(padded, conv_weights[position], row_gap, col_gap, sub_rows, sub_cols)
        grouped = update(grouped, response, conv_biases[position])
    returned = lax.all_to_all(grouped, "row", split_axis=0, concat_axis=0, tiled=True)
    return (
        returned.reshape(tile_rows, class_count, sub_cols, channels)
        .transpose(0, 2, 1, 3)
        .reshape(tile_rows, tile_cols, channels)
    )


def vmem_spec():
    return pl.BlockSpec(memory_space=pltpu.VMEM)


def smem_spec():
    return pl.BlockSpec(memory_space=pltpu.SMEM)


def any_spec():
    return pl.BlockSpec(memory_space=pl.ANY)


def kernel_call(body, out_shape, in_specs, scratch, out_specs=None):
    return pl.pallas_call(
        body,
        out_shape=out_shape,
        in_specs=in_specs,
        out_specs=out_specs or jax.tree.map(lambda _: vmem_spec(), out_shape),
        scratch_shapes=scratch,
        compiler_params=pltpu.CompilerParams(vmem_limit_bytes=vmem_limit),
        cost_estimate=pl.CostEstimate(flops=1, bytes_accessed=1, transcendentals=0),
    )


def place(core, at_zero, at_one):
    return pl.multiple_of(jnp.where(core == 0, at_zero, at_one), lane_pad)


def guarded(flag_ref, condition, action):
    if condition is None:
        action()
    else:
        number, value = condition
        pl.when(flag_ref[number] == value)(action)


def copy_kernel(moves, inputs, flag_ref, *refs):
    sources, targets = refs[:inputs], refs[inputs:]

    def move(which, row, count, column, width, target, target_row):
        src = place(flag_ref[0], *column)
        for r in range(count):
            targets[target][target_row + r] = sources[which][row + r, pl.ds(src, width), :]

    for parts in moves:
        guarded(flag_ref, parts[0], functools.partial(move, *parts[1:]))


def copies(flags, arrays, moves):
    channels, kind = arrays[0].shape[2], arrays[0].dtype
    shapes = {}
    for _, _, _, count, _, width, target, target_row in moves:
        height = max(target_row + count, shapes.get(target, (0, 0))[0])
        shapes[target] = (height, width)
    out = tuple(
        jax.ShapeDtypeStruct(shapes[target] + (channels,), kind) for target in range(len(shapes))
    )
    return kernel_call(
        functools.partial(copy_kernel, moves, len(arrays)),
        out,
        [smem_spec()] + [vmem_spec()] * len(arrays),
        [],
    )(flags, *arrays)


def hold_kernel(flag_ref, gain_ref, bias_ref, w_ref, scale_ref, first_ref, second_ref, last_ref):
    scale_ref[0:3, :] = gain_ref[...]
    scale_ref[3:6, :] = bias_ref[...]
    first_ref[...] = w_ref[0]
    second_ref[0] = w_ref[1, 1]
    second_ref[1] = w_ref[1, flag_ref[3]]
    last_ref[...] = w_ref[2, 1]


def first_layer_kernel(segments, out_at, rows, width, flag_ref, scale_ref, w_ref, *rest):
    parts, (next_ref, normed_ref, window, taps) = rest[:-4], rest[-4:]
    core = flag_ref[0]
    half = rows // 2
    channels = window.shape[2]
    gain = scale_ref[0:1, :]

    def fill(which, source_row, window_row, count, source, target, columns):
        src, dst = place(core, *source), place(core, *target)
        for r in range(count):
            if which is None:
                values = jnp.zeros((columns, channels), window.dtype)
            else:
                values = normalize(
                    parts[which][source_row + r, pl.ds(src, columns), :], gain
                )
            window[window_row + r, pl.ds(dst, columns), :] = values

    for segment in segments:
        guarded(flag_ref, segment[0], functools.partial(fill, *segment[1:]))
    step = dilations[0]
    for b in range(3):
        first = lane_pad + (b - 1) * step
        for r in range(2 * rows):
            taps[b, r] = window[r, first : first + width, :]
    stacked = jnp.concatenate(
        [
            taps[b, a * half : a * half + rows].reshape(rows * width, channels)
            for a in range(3)
            for b in range(3)
        ],
        axis=1,
    )
    response = jnp.dot(
        stacked, w_ref[...].reshape(9 * channels, channels), preferred_element_type=jnp.float32
    )
    out_col = place(core, *out_at)
    current = parts[0][:, pl.ds(out_col, width), :].reshape(rows * width, channels)
    result = update(current, response, scale_ref[3:4, :])
    next_ref[...] = result.reshape(rows, width, channels)
    normed_ref[...] = normalize(result, scale_ref[1:2, :]).reshape(rows, width, channels)


def first_layer(flags, params, parts, segments, out_at, width):
    rows, _, channels = parts[0].shape
    kind = parts[0].dtype
    out = jax.ShapeDtypeStruct((rows, width, channels), kind)
    return kernel_call(
        functools.partial(first_layer_kernel, segments, out_at, rows, width),
        (out, out),
        [smem_spec()] + [vmem_spec()] * (2 + len(parts)),
        [
            pltpu.VMEM((2 * rows, width + 2 * lane_pad, channels), kind),
            pltpu.VMEM((3, 2 * rows, width, channels), kind),
        ],
    )(flags, *params, *parts)


def partial_kernel(
    flag_ref, scale_ref, w_ref, near_ref, mid_ref, far_ref, cfar_ref, side_ref, near1_ref, mid1_ref,
    far1_ref, acc_ref, next_ref, far2_ref, farn_ref, own, other,
):
    core = flag_ref[0]
    step = dilations[1]
    rows, near, channels = near_ref.shape
    mid, far = mid_ref.shape[1], far_ref.shape[1]
    cols = near + mid + far
    other[...] = jnp.zeros(other.shape, other.dtype)
    pieces = (
        (near_ref, near1_ref, (cols - near, 0)),
        (mid_ref, mid1_ref, (far, near)),
        (far_ref, far1_ref, (0, cols - far)),
    )
    for normed, current, at in pieces:
        width = normed.shape[1]
        next_ref[:, pl.ds(place(core, *at), width), :] = current[...]
        inside = pl.ds(place(core, at[0] + step, at[1] + step), width)
        own[:, inside, :] = normed[...]
        if normed is far_ref:
            other[:, inside, :] = cfar_ref[...]
    own[:, pl.ds(place(core, step + cols, 0), step), :] = side_ref[...]
    own[:, pl.ds(place(core, 0, step + cols), step), :] = jnp.zeros(
        (rows, step, channels), own.dtype
    )
    stacked = jnp.concatenate(
        [
            ref[:, b * step : b * step + cols, :].reshape(rows * cols, channels)
            for ref in (own, other)
            for b in range(3)
        ],
        axis=1,
    )
    acc_ref[...] = jnp.dot(
        stacked, w_ref[...].reshape(6 * channels, channels), preferred_element_type=jnp.float32
    ).reshape(rows, cols, channels)
    edge = pl.ds(place(core, 0, cols - far2_ref.shape[1]), far2_ref.shape[1])
    far2_ref[...], farn_ref[...] = after_second(
        scale_ref, acc_ref[:, edge, :], next_ref[:, edge, :]
    )


def second_layer(flag_ref, scale_ref, w_ref, window, acc, current):
    step = dilations[1]
    rows, width, channels = current.shape
    cells = rows * width
    stacked = jnp.concatenate(
        [window[:, b * step : b * step + width, :].reshape(cells, channels) for b in range(3)],
        axis=1,
    )
    response = acc.reshape(cells, channels) + jnp.dot(
        stacked,
        w_ref[1].reshape(3 * channels, channels),
        preferred_element_type=jnp.float32,
    )
    return after_second(scale_ref, response, current)


def after_second(scale_ref, response, current):
    cells, channels = current.shape[0] * current.shape[1], current.shape[2]
    result = update(
        current.reshape(cells, channels), response.reshape(cells, channels), scale_ref[4:5, :]
    )
    normed = normalize(result, scale_ref[2:3, :])
    return result.reshape(current.shape), normed.reshape(current.shape)


def near_kernel(
    flag_ref, scale_ref, w_ref, cnear_ref, rim_ref, side_ref, acc_ref, x1_ref, next_ref, normed_ref,
    window,
):
    core = flag_ref[0]
    step, reach = dilations[1], dilations[2]
    near, cols = cnear_ref.shape[1], x1_ref.shape[1]
    window[:, pl.ds(place(core, 0, 2 * step), near), :] = cnear_ref[...]
    window[:, pl.ds(place(core, near, step), step), :] = rim_ref[...]
    window[:, pl.ds(place(core, near + step, 0), step), :] = side_ref[...]
    at = pl.ds(place(core, cols - reach, 0), reach)
    next_ref[...], normed_ref[...] = second_layer(
        flag_ref, scale_ref, w_ref, window[...], acc_ref[:, at, :], x1_ref[:, at, :]
    )


def mid_kernel(
    flag_ref, scale_ref, w_ref, cmid_ref, cnear_ref, acc_ref, x1_ref, next_ref, normed_ref, window
):
    core = flag_ref[0]
    step, reach = dilations[1], dilations[2]
    rows, mid, channels = cmid_ref.shape
    near, width = cnear_ref.shape[1], next_ref.shape[1]
    blank = width + 2 * step - near - mid
    window[:, pl.ds(place(core, blank + mid, 0), near), :] = cnear_ref[...]
    window[:, pl.ds(place(core, blank, near), mid), :] = cmid_ref[...]
    window[:, pl.ds(place(core, 0, near + mid), blank), :] = jnp.zeros(
        (rows, blank, channels), window.dtype
    )
    at = pl.ds(place(core, x1_ref.shape[1] - reach - width, reach), width)
    next_ref[...], normed_ref[...] = second_layer(
        flag_ref, scale_ref, w_ref, window[...], acc_ref[:, at, :], x1_ref[:, at, :]
    )


def sides_kernel(
    flag_ref, scale_ref, w_ref, near2_ref, far2_ref, near_ref, far_ref, acc_ref, ends_ref, normed
):
    core = flag_ref[0]
    rows, reach, channels = near_ref.shape
    ends_ref[core], ends_ref[1 - core] = far2_ref[...], near2_ref[...]
    normed[core], normed[1 - core] = far_ref[...], near_ref[...]
    for block, (end, tap) in enumerate(((0, 1), (0, 0), (1, 2), (1, 1))):
        acc_ref[:, block * reach : (block + 1) * reach, :] = jnp.dot(
            normed[end].reshape(rows * reach, channels),
            w_ref[tap],
            preferred_element_type=jnp.float32,
        ).reshape(rows, reach, channels)


def last_kernel(
    flag_ref, scale_ref, w_ref, ends_ref, mid2_ref, mid_ref, side_ref, acc_ref, out_ref, result, sems
):
    core = flag_ref[0]
    rows, reach, channels = side_ref.shape
    group = 2
    leaving = []
    for first in range(0, rows, group):
        some = slice(first, first + group)
        cells = group * reach
        side = side_ref[some].reshape(cells, channels)
        nothing = jnp.zeros_like(side)
        inner = [
            mid_ref[some, at * reach : (at + 1) * reach, :].reshape(cells, channels)
            for at in range(2)
        ]
        blocks = (
            (inner[0], 2, jnp.where(core == 1, side, nothing), 0, ends_ref[0, some]),
            (inner[0], 1, inner[1], 2, mid2_ref[some, 0:reach, :]),
            (inner[0], 0, inner[1], 1, mid2_ref[some, reach : 2 * reach, :]),
            (inner[1], 0, jnp.where(core == 0, side, nothing), 2, ends_ref[1, some]),
        )
        for block, (one, tap, two, other_tap, current) in enumerate(blocks):
            at = slice(block * reach, (block + 1) * reach)
            response = acc_ref[some, at, :].reshape(cells, channels) + jnp.dot(
                jnp.concatenate([one, two], axis=1),
                jnp.concatenate([w_ref[tap], w_ref[other_tap]], axis=0),
                preferred_element_type=jnp.float32,
            )
            result[some, at, :] = update(
                current.reshape(cells, channels), response, scale_ref[5:6, :]
            ).reshape(group, reach, channels)
        leaving.append(
            pltpu.make_async_copy(result.at[some], out_ref.at[some], sems.at[first // group])
        )
        leaving[-1].start()
    for copy in leaving:
        copy.wait()


def by_halves(context_map, norm_gains, conv_biases, conv_weights):
    rows, cols, channels = context_map.shape
    kind = context_map.dtype
    size = lax.axis_size("row")
    group = size // 2
    half = rows // 2
    step, reach = dilations[1], dilations[2]
    strip = step + reach
    mid = cols - 2 * strip
    pad = lane_pad
    wide = strip + pad
    core, row = lax.axis_index("col"), lax.axis_index("row")
    upper_half = row < group
    parity = row % 2
    flags = jnp.stack(
        [
            core,
            row == group - 1,
            row == group,
            jnp.where(upper_half, 2, 0),
            parity,
            jnp.where(row == group, 3, 2 - parity),
            jnp.where(row == group - 1, 3, 1 + parity),
        ]
    ).astype(jnp.int32)
    even, odd = (4, 0), (4, 1)
    above_in, below_in = ([(flag, which) for which in (1, 2, 3)] for flag in (5, 6))
    swap = [(0, 1), (1, 0)]
    partner = [(i, (i + group) % size) for i in range(size)]
    first_pairs = [(i, i ^ 1) for i in range(size)]
    second_pairs = [(i, ((i + 1) ^ 1) - 1) for i in range(1, size - 1)]
    across = [(group - 1, group), (group, group - 1)]
    second_within = [pair for pair in second_pairs if pair not in across]

    far_wide_at, near_wide_at = (0, cols - wide), (cols - wide, 0)
    span, span_at = cols - wide, (wide, 0)
    middle_at = (wide - pad, 0)
    parts = (
        (None, 0, 0, rows, far_wide_at, wide, 0, 0),
        (None, 0, 0, rows, near_wide_at, wide, 1, 0),
        (None, 0, 0, rows, (strip - pad, strip - pad), mid + 2 * pad, 2, 0),
        (even, 0, half, half, far_wide_at, wide, 3, 0),
        (odd, 0, 0, half, far_wide_at, wide, 3, 0),
        (even, 0, 0, half, far_wide_at, wide, 4, 0),
        (odd, 0, half, half, far_wide_at, wide, 4, 0),
        (even, 0, half, half, span_at, span, 5, 0),
        (odd, 0, 0, half, span_at, span, 5, 0),
        (even, 0, 0, half, span_at, span, 6, 0),
        (odd, 0, half, half, span_at, span, 6, 0),
        ((1, 1), 0, half, half, middle_at, span + pad, 7, 0),
        ((1, 0), 0, 0, half, middle_at, span + pad, 7, 0),
    )
    (
        far_x, near_x, mid_x, far_one, far_two, one, two, middle
    ) = copies(flags, (context_map,), parts)
    far_one = lax.ppermute(far_one, "row", first_pairs)
    far_two = lax.ppermute(far_two, "row", second_pairs)
    tail = conv_weights.shape[2:]
    scales, first_w, second_w, last_w = kernel_call(
        hold_kernel,
        (
            jax.ShapeDtypeStruct((2 * norm_gains.shape[0], channels), jnp.float32),
            jax.ShapeDtypeStruct((3,) + tail, kind),
            jax.ShapeDtypeStruct((2,) + tail, kind),
            jax.ShapeDtypeStruct(tail, kind),
        ),
        [smem_spec()] + [vmem_spec()] * 3,
        [],
    )(flags, norm_gains, conv_biases, conv_weights)
    one, two, middle, scales = lax.optimization_barrier((one, two, middle, scales))
    one = lax.ppermute(one, "row", first_pairs)
    two = lax.ppermute(two, "row", second_within)
    middle = lax.ppermute(middle, "row", across)

    params = (scales, first_w)
    far_body, far_edge = (pad, 0), (0, wide)
    far_segments = (
        (None, 0, 0, half, rows, (0, 0), far_body, wide),
        (odd, 1, 0, 0, half, (0, 0), far_body, wide),
        (even, 2, 0, 0, half, (0, 0), far_body, wide),
        (even, 1, 0, half + rows, half, (0, 0), far_body, wide),
        (odd, 2, 0, half + rows, half, (0, 0), far_body, wide),
        (None, None, 0, 0, 2 * rows, (0, 0), far_edge, pad),
    )
    far1, far_n = first_layer(
        flags, params, (far_x, far_one, far_two), far_segments, (0, pad), strip
    )
    cross_far = lax.ppermute(far_n, "row", partner)

    near_end, span_end, middle_end = (wide - pad, 0), (span - pad, 0), (span, 0)
    (rim,) = copies(
        flags,
        (near_x, one, two, middle),
        (
            (above_in[0], 1, 0, half, span_end, pad, 0, 0),
            (above_in[1], 2, 0, half, span_end, pad, 0, 0),
            (above_in[2], 3, 0, half, middle_end, pad, 0, 0),
            (None, 0, 0, rows, near_end, pad, 0, half),
            (below_in[0], 1, 0, half, span_end, pad, 0, half + rows),
            (below_in[1], 2, 0, half, span_end, pad, 0, half + rows),
            (below_in[2], 3, 0, half, middle_end, pad, 0, half + rows),
        ),
    )
    rim = lax.ppermute(rim, "col", swap)
    near_body, near_span, near_middle = (0, pad), (span - wide, 0), (span + pad - wide, 0)
    near_segments = (
        (None, 0, 0, half, rows, (0, 0), near_body, wide),
        (above_in[0], 1, 0, 0, half, near_span, near_body, wide),
        (above_in[1], 2, 0, 0, half, near_span, near_body, wide),
        (above_in[2], 4, 0, 0, half, near_middle, near_body, wide),
        (below_in[0], 1, 0, half + rows, half, near_span, near_body, wide),
        (below_in[1], 2, 0, half + rows, half, near_span, near_body, wide),
        (below_in[2], 4, 0, half + rows, half, near_middle, near_body, wide),
        (None, 3, 0, 0, 2 * rows, (0, 0), (wide, 0), pad),
    )
    near1, near_n = first_layer(
        flags, params, (near_x, one, two, rim, middle), near_segments, (pad, 0), strip
    )
    near_rim, near_rest = copies(
        flags,
        (near_n,),
        (
            (None, 0, 0, rows, (strip - step, 0), step, 0, 0),
            (None, 0, 0, rows, (0, step), strip - step, 1, 0),
        ),
    )
    cross_rim = lax.ppermute(near_rim, "row", partner)
    cross_near = lax.ppermute(near_rest, "row", partner)
    side_pads = 2 * pad
    far_side, rest_side = ((wide - side_pads, 0), (0, mid)), ((0, span - mid), (side_pads, 0))
    middle_side = ((pad, span - mid), (side_pads, 0))
    mid_segments = (
        (None, 0, 0, half, rows, (0, 0), (0, 0), mid + side_pads),
        (odd, 1, 0, 0, half, *far_side, side_pads),
        (even, 2, 0, 0, half, *far_side, side_pads),
        (even, 1, 0, half + rows, half, *far_side, side_pads),
        (odd, 2, 0, half + rows, half, *far_side, side_pads),
        (above_in[0], 3, 0, 0, half, *rest_side, mid),
        (above_in[1], 4, 0, 0, half, *rest_side, mid),
        (above_in[2], 5, 0, 0, half, *middle_side, mid),
        (below_in[0], 3, 0, half + rows, half, *rest_side, mid),
        (below_in[1], 4, 0, half + rows, half, *rest_side, mid),
        (below_in[2], 5, 0, half + rows, half, *middle_side, mid),
    )
    mid1, mid_n = first_layer(
        flags,
        params,
        (
            mid_x, far_one, far_two, one, two, middle
        ),
        mid_segments,
        (pad, pad),
        mid,
    )
    cross_mid = lax.ppermute(mid_n, "row", partner)

    near_rim, cross_far = lax.optimization_barrier((near_rim, cross_far))
    near_side = lax.ppermute(near_rim, "col", swap)
    def plain(body, weights, out, operands, scratch, more=()):
        return kernel_call(
            body,
            out,
            [smem_spec()] + [vmem_spec()] * (len(operands) + 2),
            [pltpu.VMEM((rows, width, channels), kind) for width in scratch] + list(more),
        )(flags, scales, weights, *operands)

    def strip_shape(width, kind=kind):
        return jax.ShapeDtypeStruct((rows, width, channels), kind)

    acc, x1, far2, far_n = plain(
        partial_kernel,
        second_w,
        (
            strip_shape(cols, jnp.float32),
            strip_shape(cols),
            strip_shape(strip - step),
            strip_shape(strip - step),
        ),
        (near_n, mid_n, far_n, cross_far, near_side, near1, mid1, far1),
        (cols + 2 * step, cols + 2 * step),
    )
    cross_side = lax.ppermute(cross_rim, "col", swap)
    near2, near_n = plain(
        near_kernel,
        second_w,
        (strip_shape(reach), strip_shape(reach)),
        (cross_near, cross_rim, cross_side, acc, x1),
        (reach + 2 * step,),
    )
    sums, ends = plain(
        sides_kernel,
        last_w,
        (
            strip_shape(cols, jnp.float32),
            jax.ShapeDtypeStruct((2, rows, reach, channels), kind),
        ),
        (near2, far2, near_n, far_n),
        (),
        [pltpu.VMEM((2, rows, reach, channels), kind)],
    )
    near_n, cross_mid, sums = lax.optimization_barrier((near_n, cross_mid, sums))
    last_side = lax.ppermute(near_n, "col", swap)
    mid2, mid_n = plain(
        mid_kernel,
        second_w,
        (strip_shape(2 * reach), strip_shape(2 * reach)),
        (cross_mid, cross_near, acc, x1),
        (2 * reach + 2 * step,),
    )
    return kernel_call(
        last_kernel,
        strip_shape(cols),
        [smem_spec()] + [vmem_spec()] * 7,
        [
            pltpu.VMEM((rows, cols, channels), kind),
            pltpu.SemaphoreType.DMA((rows,)),
        ],
        any_spec(),
    )(flags, scales, last_w, ends, mid2, mid_n, last_side, sums)


def shards(context_map, *params):
    rows, cols, _ = context_map.shape
    map_rows = lax.axis_size("row") * rows
    strip = dilations[1] + dilations[2]
    if (
        map_rows == 2 * dilations[1]
        and map_rows <= dilations[2]
        and rows == 2 * dilations[0]
        and dilations[1] % rows == 0
        and lax.axis_size("col") == 2
        and cols == 4 * dilations[2]
        and dilations[2] == 2 * dilations[1]
    ):
        return by_halves(context_map, *params)
    return by_classes(context_map, *params)


def solution(mesh):
    return jax.shard_map(
        shards,
        mesh=mesh,
        in_specs=(P(("ctx", "row"), "col", None), P(), P(), P()),
        out_specs=P(("ctx", "row"), "col", None),
        check_vma=False,
    )
```

```python
import functools

import jax
import jax.numpy as jnp
from jax import lax
from jax.experimental import pallas as pl
from jax.experimental.pallas import tpu as pltpu
from jax.sharding import PartitionSpec as P

epsilon = 1e-05
dilations = (4, 32, 64)
lane_pad = 16
vmem_limit = 40 * 1024 * 1024


def extended(x, sides, width):
    for axis, dim in sides:
        size, length = (lax.axis_size(axis), x.shape[dim])
        up = [(i, (i + 1) % size) for i in range(size - 1)]
        down = [(j, i) for i, j in up]
        last = lax.slice_in_dim(x, length - width, length, axis=dim)
        first = lax.slice_in_dim(x, 0, width, axis=dim)
        before = lax.ppermute(last, axis, up)
        after = lax.ppermute(first, axis, down)
        x = jnp.concatenate([before, x, after], axis=dim)
    return x


def normalize(current, gain_row):
    values = current.astype(jnp.float32)
    centred = values - jnp.mean(values, axis=-1, keepdims=True)
    variance = jnp.mean(centred * centred, axis=-1, keepdims=True)
    return (centred * lax.rsqrt(variance + epsilon) * gain_row).astype(jnp.bfloat16)


def convolve(padded, kernel, row_step, col_step, out_rows, out_cols):
    channels = padded.shape[2]
    tap_list = []
    for tap_row in range(3):
        for tap_col in range(3):
            tap_list.append(
                lax.slice(
                    padded,
                    (tap_row * row_step, tap_col * col_step, 0),
                    (tap_row * row_step + out_rows, tap_col * col_step + out_cols, channels),
                )
            )
    stacked = jnp.concatenate(tap_list, axis=2).reshape(out_rows * out_cols, 9 * channels)
    product = jnp.dot(
        stacked, kernel.reshape(9 * channels, kernel.shape[3]), preferred_element_type=jnp.float32
    )
    return product.reshape(out_rows, out_cols, kernel.shape[3])


def update(current, response, bias_row):
    return (current.astype(jnp.float32) + jnp.maximum(response + bias_row, 0.0)).astype(
        jnp.bfloat16
    )


def by_classes(context_map, norm_gains, conv_biases, conv_weights):
    tile_rows, tile_cols, channels = context_map.shape
    normed = normalize(context_map, norm_gains[0])
    padded = extended(normed, (("row", 0), ("col", 1)), 4)
    current = update(
        context_map, convolve(padded, conv_weights[0], 4, 4, tile_rows, tile_cols), conv_biases[0]
    )
    class_count = lax.axis_size("row") // tile_rows
    sub_cols = tile_cols // class_count
    outgoing = (
        current.reshape(tile_rows, sub_cols, class_count, channels)
        .transpose(0, 2, 1, 3)
        .reshape(tile_rows * class_count, sub_cols, channels)
    )
    grouped = lax.all_to_all(outgoing, "row", split_axis=0, concat_axis=0, tiled=True)
    sub_rows = grouped.shape[0]
    for position, dilation in ((1, 32), (2, 64)):
        normed = normalize(grouped, norm_gains[position])
        row_gap = dilation // tile_rows
        col_gap = dilation // class_count
        with_sides = extended(normed, (("col", 1),), col_gap)
        padded = jnp.pad(with_sides, ((row_gap, row_gap), (0, 0), (0, 0)))
        response = convolve(padded, conv_weights[position], row_gap, col_gap, sub_rows, sub_cols)
        grouped = update(grouped, response, conv_biases[position])
    returned = lax.all_to_all(grouped, "row", split_axis=0, concat_axis=0, tiled=True)
    return (
        returned.reshape(tile_rows, class_count, sub_cols, channels)
        .transpose(0, 2, 1, 3)
        .reshape(tile_rows, tile_cols, channels)
    )


def vmem_spec():
    return pl.BlockSpec(memory_space=pltpu.VMEM)


def smem_spec():
    return pl.BlockSpec(memory_space=pltpu.SMEM)


def any_spec():
    return pl.BlockSpec(memory_space=pl.ANY)


def kernel_call(body, out_shape, in_specs, scratch, out_specs=None):
    return pl.pallas_call(
        body,
        out_shape=out_shape,
        in_specs=in_specs,
        out_specs=out_specs or jax.tree.map(lambda _: vmem_spec(), out_shape),
        scratch_shapes=scratch,
        compiler_params=pltpu.CompilerParams(vmem_limit_bytes=vmem_limit),
        cost_estimate=pl.CostEstimate(flops=1, bytes_accessed=1, transcendentals=0),
    )


def place(core, at_zero, at_one):
    return pl.multiple_of(jnp.where(core == 0, at_zero, at_one), lane_pad)


def row_of(flag_ref, row):
    return row if isinstance(row, int) else jnp.where(flag_ref[4] == 0, *row)


def guarded(flag_ref, condition, action):
    if condition is None:
        action()
    else:
        number, value = condition
        pl.when(flag_ref[number] == value)(action)


def copy_kernel(moves, inputs, flag_ref, *refs):
    sources, targets = refs[:inputs], refs[inputs:]

    def move(which, row, count, column, width, target, target_row):
        src = place(flag_ref[0], *column)
        first = row_of(flag_ref, target_row)
        for r in range(count):
            targets[target][first + r] = sources[which][row + r, pl.ds(src, width), :]

    for parts in moves:
        guarded(flag_ref, parts[0], functools.partial(move, *parts[1:]))


def copies(flags, arrays, moves):
    channels, kind = arrays[0].shape[2], arrays[0].dtype
    shapes = {}
    for _, _, _, count, _, width, target, target_row in moves:
        end = count + (target_row if isinstance(target_row, int) else max(target_row))
        height = max(end, shapes.get(target, (0, 0))[0])
        shapes[target] = (height, width)
    out = tuple(
        jax.ShapeDtypeStruct(shapes[target] + (channels,), kind) for target in range(len(shapes))
    )
    return kernel_call(
        functools.partial(copy_kernel, moves, len(arrays)),
        out,
        [smem_spec()] + [vmem_spec()] * len(arrays),
        [],
    )(flags, *arrays)


def hold_kernel(flag_ref, w_ref, first_ref, second_ref, last_ref):
    first_ref[...] = w_ref[0]
    second_ref[0] = w_ref[1, 1]
    second_ref[1] = w_ref[1, flag_ref[3]]
    last_ref[...] = w_ref[2, 1]


def first_layer_kernel(segments, out_at, rows, width, flag_ref, scale_ref, w_ref, *rest):
    parts, (next_ref, normed_ref, window, taps) = rest[:-4], rest[-4:]
    core = flag_ref[0]
    half = rows // 2
    channels = window.shape[2]
    gain = scale_ref[0:1, :]

    def fill(which, source_row, window_row, count, source, target, columns):
        src, dst = place(core, *source), place(core, *target)
        first = row_of(flag_ref, window_row)
        for r in range(count):
            if which is None:
                values = jnp.zeros((columns, channels), window.dtype)
            else:
                values = normalize(
                    parts[which][source_row + r, pl.ds(src, columns), :], gain
                )
            window[first + r, pl.ds(dst, columns), :] = values

    for segment in segments:
        guarded(flag_ref, segment[0], functools.partial(fill, *segment[1:]))
    step = dilations[0]
    for b in range(3):
        first = lane_pad + (b - 1) * step
        for r in range(2 * rows):
            taps[b, r] = window[r, first : first + width, :]
    stacked = jnp.concatenate(
        [
            taps[b, a * half : a * half + rows].reshape(rows * width, channels)
            for a in range(3)
            for b in range(3)
        ],
        axis=1,
    )
    response = jnp.dot(
        stacked, w_ref[...].reshape(9 * channels, channels), preferred_element_type=jnp.float32
    )
    out_col = place(core, *out_at)
    current = parts[0][:, pl.ds(out_col, width), :].reshape(rows * width, channels)
    result = update(current, response, scale_ref[3:4, :])
    next_ref[...] = result.reshape(rows, width, channels)
    normed_ref[...] = normalize(result, scale_ref[1:2, :]).reshape(rows, width, channels)


def first_layer(flags, params, parts, segments, out_at, width):
    rows, _, channels = parts[0].shape
    kind = parts[0].dtype
    out = jax.ShapeDtypeStruct((rows, width, channels), kind)
    return kernel_call(
        functools.partial(first_layer_kernel, segments, out_at, rows, width),
        (out, out),
        [smem_spec()] + [vmem_spec()] * (2 + len(parts)),
        [
            pltpu.VMEM((2 * rows, width + 2 * lane_pad, channels), kind),
            pltpu.VMEM((3, 2 * rows, width, channels), kind),
        ],
    )(flags, *params, *parts)


def partial_kernel(
    flag_ref, scale_ref, w_ref, near_ref, mid_ref, far_ref, cfar_ref, side_ref, near1_ref, mid1_ref,
    far1_ref, acc_ref, next_ref, far2_ref, farn_ref, own, other,
):
    core = flag_ref[0]
    step = dilations[1]
    rows, near, channels = near_ref.shape
    mid, far = mid_ref.shape[1], far_ref.shape[1]
    cols = near + mid + far
    other[...] = jnp.zeros(other.shape, other.dtype)
    pieces = (
        (near_ref, near1_ref, (cols - near, 0)),
        (mid_ref, mid1_ref, (far, near)),
        (far_ref, far1_ref, (0, cols - far)),
    )
    for normed, current, at in pieces:
        width = normed.shape[1]
        next_ref[:, pl.ds(place(core, *at), width), :] = current[...]
        inside = pl.ds(place(core, at[0] + step, at[1] + step), width)
        own[:, inside, :] = normed[...]
        if normed is far_ref:
            other[:, inside, :] = cfar_ref[...]
    own[:, pl.ds(place(core, step + cols, 0), step), :] = side_ref[...]
    own[:, pl.ds(place(core, 0, step + cols), step), :] = jnp.zeros(
        (rows, step, channels), own.dtype
    )
    stacked = jnp.concatenate(
        [
            ref[:, b * step : b * step + cols, :].reshape(rows * cols, channels)
            for ref in (own, other)
            for b in range(3)
        ],
        axis=1,
    )
    acc_ref[...] = jnp.dot(
        stacked, w_ref[...].reshape(6 * channels, channels), preferred_element_type=jnp.float32
    ).reshape(rows, cols, channels)
    edge = pl.ds(place(core, 0, cols - far2_ref.shape[1]), far2_ref.shape[1])
    far2_ref[...], farn_ref[...] = after_second(
        scale_ref, acc_ref[:, edge, :], next_ref[:, edge, :]
    )


def second_layer(flag_ref, scale_ref, w_ref, window, acc, current):
    step = dilations[1]
    rows, width, channels = current.shape
    cells = rows * width
    stacked = jnp.concatenate(
        [window[:, b * step : b * step + width, :].reshape(cells, channels) for b in range(3)],
        axis=1,
    )
    response = acc.reshape(cells, channels) + jnp.dot(
        stacked,
        w_ref[1].reshape(3 * channels, channels),
        preferred_element_type=jnp.float32,
    )
    return after_second(scale_ref, response, current)


def after_second(scale_ref, response, current):
    cells, channels = current.shape[0] * current.shape[1], current.shape[2]
    result = update(
        current.reshape(cells, channels), response.reshape(cells, channels), scale_ref[4:5, :]
    )
    normed = normalize(result, scale_ref[2:3, :])
    return result.reshape(current.shape), normed.reshape(current.shape)


def near_kernel(
    flag_ref, scale_ref, w_ref, cnear_ref, rim_ref, side_ref, acc_ref, x1_ref, next_ref, normed_ref,
    window,
):
    core = flag_ref[0]
    step, reach = dilations[1], dilations[2]
    near, cols = cnear_ref.shape[1], x1_ref.shape[1]
    window[:, pl.ds(place(core, 0, 2 * step), near), :] = cnear_ref[...]
    window[:, pl.ds(place(core, near, step), step), :] = rim_ref[...]
    window[:, pl.ds(place(core, near + step, 0), step), :] = side_ref[...]
    at = pl.ds(place(core, cols - reach, 0), reach)
    next_ref[...], normed_ref[...] = second_layer(
        flag_ref, scale_ref, w_ref, window[...], acc_ref[:, at, :], x1_ref[:, at, :]
    )


def mid_kernel(
    flag_ref, scale_ref, w_ref, cmid_ref, cnear_ref, acc_ref, x1_ref, next_ref, normed_ref, window
):
    core = flag_ref[0]
    step, reach = dilations[1], dilations[2]
    rows, mid, channels = cmid_ref.shape
    near, width = cnear_ref.shape[1], next_ref.shape[1]
    blank = width + 2 * step - near - mid
    window[:, pl.ds(place(core, blank + mid, 0), near), :] = cnear_ref[...]
    window[:, pl.ds(place(core, blank, near), mid), :] = cmid_ref[...]
    window[:, pl.ds(place(core, 0, near + mid), blank), :] = jnp.zeros(
        (rows, blank, channels), window.dtype
    )
    at = pl.ds(place(core, x1_ref.shape[1] - reach - width, reach), width)
    next_ref[...], normed_ref[...] = second_layer(
        flag_ref, scale_ref, w_ref, window[...], acc_ref[:, at, :], x1_ref[:, at, :]
    )


def sides_kernel(
    flag_ref, scale_ref, w_ref, near2_ref, far2_ref, near_ref, far_ref, acc_ref, ends_ref, normed
):
    core = flag_ref[0]
    rows, reach, channels = near_ref.shape
    ends_ref[core], ends_ref[1 - core] = far2_ref[...], near2_ref[...]
    normed[core], normed[1 - core] = far_ref[...], near_ref[...]
    for block, (end, tap) in enumerate(((0, 1), (0, 0), (1, 2), (1, 1))):
        acc_ref[:, block * reach : (block + 1) * reach, :] = jnp.dot(
            normed[end].reshape(rows * reach, channels),
            w_ref[tap],
            preferred_element_type=jnp.float32,
        ).reshape(rows, reach, channels)


def last_kernel(
    flag_ref, scale_ref, w_ref, ends_ref, mid2_ref, mid_ref, side_ref, acc_ref, out_ref, result, sems
):
    core = flag_ref[0]
    rows, reach, channels = side_ref.shape
    group = 2
    leaving = []
    for first in range(0, rows, group):
        some = slice(first, first + group)
        cells = group * reach
        side = side_ref[some].reshape(cells, channels)
        nothing = jnp.zeros_like(side)
        inner = [
            mid_ref[some, at * reach : (at + 1) * reach, :].reshape(cells, channels)
            for at in range(2)
        ]
        blocks = (
            (inner[0], 2, jnp.where(core == 1, side, nothing), 0, ends_ref[0, some]),
            (inner[0], 1, inner[1], 2, mid2_ref[some, 0:reach, :]),
            (inner[0], 0, inner[1], 1, mid2_ref[some, reach : 2 * reach, :]),
            (inner[1], 0, jnp.where(core == 0, side, nothing), 2, ends_ref[1, some]),
        )
        for block, (one, tap, two, other_tap, current) in enumerate(blocks):
            at = slice(block * reach, (block + 1) * reach)
            response = acc_ref[some, at, :].reshape(cells, channels) + jnp.dot(
                jnp.concatenate([one, two], axis=1),
                jnp.concatenate([w_ref[tap], w_ref[other_tap]], axis=0),
                preferred_element_type=jnp.float32,
            )
            result[some, at, :] = update(
                current.reshape(cells, channels), response, scale_ref[5:6, :]
            ).reshape(group, reach, channels)
        leaving.append(
            pltpu.make_async_copy(result.at[some], out_ref.at[some], sems.at[first // group])
        )
        leaving[-1].start()
    for copy in leaving:
        copy.wait()


def by_halves(context_map, norm_gains, conv_biases, conv_weights):
    rows, cols, channels = context_map.shape
    kind = context_map.dtype
    size = lax.axis_size("row")
    group = size // 2
    half = rows // 2
    step, reach = dilations[1], dilations[2]
    strip = step + reach
    mid = cols - 2 * strip
    pad = lane_pad
    wide = strip + pad
    core, row = lax.axis_index("col"), lax.axis_index("row")
    upper_half = row < group
    beside = (row == group) | (row == group - 1)
    flags = jnp.stack(
        [core, row == group - 1, row == group, jnp.where(upper_half, 2, 0), row % 2, beside]
    ).astype(jnp.int32)
    even, odd, apart, at_middle = (4, 0), (4, 1), (5, 0), (5, 1)
    one_at, two_at = (half + rows, 0), (0, half + rows)
    swap = [(0, 1), (1, 0)]
    partner = [(i, (i + group) % size) for i in range(size)]
    first_pairs = [(i, i ^ 1) for i in range(size)]
    second_pairs = [(i, ((i + 1) ^ 1) - 1) for i in range(1, size - 1)]
    across = [(group - 1, group), (group, group - 1)]
    second_within = [pair for pair in second_pairs if pair not in across]

    far_wide_at, near_wide_at = (0, cols - wide), (cols - wide, 0)
    span, span_at = cols - wide, (wide, 0)
    middle_at = (wide - pad, 0)
    parts = (
        (None, 0, 0, rows, far_wide_at, wide, 0, 0),
        (None, 0, 0, rows, near_wide_at, wide, 1, 0),
        (None, 0, 0, rows, (strip - pad, strip - pad), mid + 2 * pad, 2, 0),
        (even, 0, half, half, far_wide_at, wide, 3, 0),
        (odd, 0, 0, half, far_wide_at, wide, 3, 0),
        (even, 0, 0, half, far_wide_at, wide, 4, 0),
        (odd, 0, half, half, far_wide_at, wide, 4, 0),
        (even, 0, half, half, span_at, span, 5, 0),
        (odd, 0, 0, half, span_at, span, 5, 0),
        (even, 0, 0, half, span_at, span, 6, 0),
        (odd, 0, half, half, span_at, span, 6, 0),
        ((1, 1), 0, half, half, middle_at, span + pad, 7, 0),
        ((1, 0), 0, 0, half, middle_at, span + pad, 7, 0),
    )
    (
        far_x, near_x, mid_x, far_one, far_two, one, two, middle
    ) = copies(flags, (context_map,), parts)
    far_one = lax.ppermute(far_one, "row", first_pairs)
    far_two = lax.ppermute(far_two, "row", second_pairs)
    tail = conv_weights.shape[2:]
    scales = jnp.concatenate([norm_gains, conv_biases], axis=0)
    first_w, second_w, last_w = kernel_call(
        hold_kernel,
        (
            jax.ShapeDtypeStruct((3,) + tail, kind),
            jax.ShapeDtypeStruct((2,) + tail, kind),
            jax.ShapeDtypeStruct(tail, kind),
        ),
        [smem_spec(), vmem_spec()],
        [],
    )(flags, conv_weights)
    one, two, middle, first_w = lax.optimization_barrier((one, two, middle, first_w))
    one = lax.ppermute(one, "row", first_pairs)
    two = lax.ppermute(two, "row", second_within)
    middle = lax.ppermute(middle, "row", across)

    params = (scales, first_w)
    far_body, far_edge = (pad, 0), (0, wide)
    far_segments = (
        (None, 0, 0, half, rows, (0, 0), far_body, wide),
        (None, 1, 0, one_at, half, (0, 0), far_body, wide),
        (None, 2, 0, two_at, half, (0, 0), far_body, wide),
        (None, None, 0, 0, 2 * rows, (0, 0), far_edge, pad),
    )
    far1, far_n = first_layer(
        flags, params, (far_x, far_one, far_two), far_segments, (0, pad), strip
    )
    cross_far = lax.ppermute(far_n, "row", partner)

    near_end, span_end, middle_end = (wide - pad, 0), (span - pad, 0), (span, 0)
    (rim,) = copies(
        flags,
        (near_x, one, two, middle),
        (
            (None, 1, 0, half, span_end, pad, 0, one_at),
            (apart, 2, 0, half, span_end, pad, 0, two_at),
            (at_middle, 3, 0, half, middle_end, pad, 0, two_at),
            (None, 0, 0, rows, near_end, pad, 0, half),
        ),
    )
    rim = lax.ppermute(rim, "col", swap)
    near_body, near_span, near_middle = (0, pad), (span - wide, 0), (span + pad - wide, 0)
    near_segments = (
        (None, 0, 0, half, rows, (0, 0), near_body, wide),
        (None, 1, 0, one_at, half, near_span, near_body, wide),
        (apart, 2, 0, two_at, half, near_span, near_body, wide),
        (at_middle, 4, 0, two_at, half, near_middle, near_body, wide),
        (None, 3, 0, 0, 2 * rows, (0, 0), (wide, 0), pad),
    )
    near1, near_n = first_layer(
        flags, params, (near_x, one, two, rim, middle), near_segments, (pad, 0), strip
    )
    near_rim, near_rest = copies(
        flags,
        (near_n,),
        (
            (None, 0, 0, rows, (strip - step, 0), step, 0, 0),
            (None, 0, 0, rows, (0, step), strip - step, 1, 0),
        ),
    )
    cross_rim = lax.ppermute(near_rim, "row", partner)
    cross_near = lax.ppermute(near_rest, "row", partner)
    side_pads = 2 * pad
    far_side, rest_side = ((wide - side_pads, 0), (0, mid)), ((0, span - mid), (side_pads, 0))
    middle_side = ((pad, span - mid), (side_pads, 0))
    mid_segments = (
        (None, 0, 0, half, rows, (0, 0), (0, 0), mid + side_pads),
        (None, 1, 0, one_at, half, *far_side, side_pads),
        (None, 2, 0, two_at, half, *far_side, side_pads),
        (None, 3, 0, one_at, half, *rest_side, mid),
        (apart, 4, 0, two_at, half, *rest_side, mid),
        (at_middle, 5, 0, two_at, half, *middle_side, mid),
    )
    mid1, mid_n = first_layer(
        flags,
        params,
        (
            mid_x, far_one, far_two, one, two, middle
        ),
        mid_segments,
        (pad, pad),
        mid,
    )
    cross_mid = lax.ppermute(mid_n, "row", partner)

    near_rim, cross_far = lax.optimization_barrier((near_rim, cross_far))
    near_side = lax.ppermute(near_rim, "col", swap)
    def plain(body, weights, out, operands, scratch, more=()):
        return kernel_call(
            body,
            out,
            [smem_spec()] + [vmem_spec()] * (len(operands) + 2),
            [pltpu.VMEM((rows, width, channels), kind) for width in scratch] + list(more),
        )(flags, scales, weights, *operands)

    def strip_shape(width, kind=kind):
        return jax.ShapeDtypeStruct((rows, width, channels), kind)

    acc, x1, far2, far_n = plain(
        partial_kernel,
        second_w,
        (
            strip_shape(cols, jnp.float32),
            strip_shape(cols),
            strip_shape(strip - step),
            strip_shape(strip - step),
        ),
        (near_n, mid_n, far_n, cross_far, near_side, near1, mid1, far1),
        (cols + 2 * step, cols + 2 * step),
    )
    cross_side = lax.ppermute(cross_rim, "col", swap)
    near2, near_n = plain(
        near_kernel,
        second_w,
        (strip_shape(reach), strip_shape(reach)),
        (cross_near, cross_rim, cross_side, acc, x1),
        (reach + 2 * step,),
    )
    sums, ends = plain(
        sides_kernel,
        last_w,
        (
            strip_shape(cols, jnp.float32),
            jax.ShapeDtypeStruct((2, rows, reach, channels), kind),
        ),
        (near2, far2, near_n, far_n),
        (),
        [pltpu.VMEM((2, rows, reach, channels), kind)],
    )
    near_n, cross_mid, sums = lax.optimization_barrier((near_n, cross_mid, sums))
    last_side = lax.ppermute(near_n, "col", swap)
    mid2, mid_n = plain(
        mid_kernel,
        second_w,
        (strip_shape(2 * reach), strip_shape(2 * reach)),
        (cross_mid, cross_near, acc, x1),
        (2 * reach + 2 * step,),
    )
    return kernel_call(
        last_kernel,
        strip_shape(cols),
        [smem_spec()] + [vmem_spec()] * 7,
        [
            pltpu.VMEM((rows, cols, channels), kind),
            pltpu.SemaphoreType.DMA((rows,)),
        ],
        any_spec(),
    )(flags, scales, last_w, ends, mid2, mid_n, last_side, sums)


def shards(context_map, *params):
    rows, cols, _ = context_map.shape
    map_rows = lax.axis_size("row") * rows
    strip = dilations[1] + dilations[2]
    if (
        map_rows == 2 * dilations[1]
        and map_rows <= dilations[2]
        and rows == 2 * dilations[0]
        and dilations[1] % rows == 0
        and lax.axis_size("col") == 2
        and cols == 4 * dilations[2]
        and dilations[2] == 2 * dilations[1]
    ):
        return by_halves(context_map, *params)
    return by_classes(context_map, *params)


def solution(mesh):
    return jax.shard_map(
        shards,
        mesh=mesh,
        in_specs=(P(("ctx", "row"), "col", None), P(), P(), P()),
        out_specs=P(("ctx", "row"), "col", None),
        check_vma=False,
    )
```

```python
import functools

import jax
import jax.numpy as jnp
from jax import lax
from jax.experimental import pallas as pl
from jax.experimental.pallas import tpu as pltpu
from jax.sharding import PartitionSpec as P

epsilon = 1e-05
dilations = (4, 32, 64)
lane_pad = 16
vmem_limit = 40 * 1024 * 1024


def extended(x, sides, width):
    for axis, dim in sides:
        size, length = (lax.axis_size(axis), x.shape[dim])
        up = [(i, (i + 1) % size) for i in range(size - 1)]
        down = [(j, i) for i, j in up]
        last = lax.slice_in_dim(x, length - width, length, axis=dim)
        first = lax.slice_in_dim(x, 0, width, axis=dim)
        before = lax.ppermute(last, axis, up)
        after = lax.ppermute(first, axis, down)
        x = jnp.concatenate([before, x, after], axis=dim)
    return x


def normalize(current, gain_row):
    values = current.astype(jnp.float32)
    centred = values - jnp.mean(values, axis=-1, keepdims=True)
    variance = jnp.mean(centred * centred, axis=-1, keepdims=True)
    return (centred * lax.rsqrt(variance + epsilon) * gain_row).astype(jnp.bfloat16)


def convolve(padded, kernel, row_step, col_step, out_rows, out_cols):
    channels = padded.shape[2]
    tap_list = []
    for tap_row in range(3):
        for tap_col in range(3):
            tap_list.append(
                lax.slice(
                    padded,
                    (tap_row * row_step, tap_col * col_step, 0),
                    (tap_row * row_step + out_rows, tap_col * col_step + out_cols, channels),
                )
            )
    stacked = jnp.concatenate(tap_list, axis=2).reshape(out_rows * out_cols, 9 * channels)
    product = jnp.dot(
        stacked, kernel.reshape(9 * channels, kernel.shape[3]), preferred_element_type=jnp.float32
    )
    return product.reshape(out_rows, out_cols, kernel.shape[3])


def update(current, response, bias_row):
    return (current.astype(jnp.float32) + jnp.maximum(response + bias_row, 0.0)).astype(
        jnp.bfloat16
    )


def by_classes(context_map, norm_gains, conv_biases, conv_weights):
    tile_rows, tile_cols, channels = context_map.shape
    normed = normalize(context_map, norm_gains[0])
    padded = extended(normed, (("row", 0), ("col", 1)), 4)
    current = update(
        context_map, convolve(padded, conv_weights[0], 4, 4, tile_rows, tile_cols), conv_biases[0]
    )
    class_count = lax.axis_size("row") // tile_rows
    sub_cols = tile_cols // class_count
    outgoing = (
        current.reshape(tile_rows, sub_cols, class_count, channels)
        .transpose(0, 2, 1, 3)
        .reshape(tile_rows * class_count, sub_cols, channels)
    )
    grouped = lax.all_to_all(outgoing, "row", split_axis=0, concat_axis=0, tiled=True)
    sub_rows = grouped.shape[0]
    for position, dilation in ((1, 32), (2, 64)):
        normed = normalize(grouped, norm_gains[position])
        row_gap = dilation // tile_rows
        col_gap = dilation // class_count
        with_sides = extended(normed, (("col", 1),), col_gap)
        padded = jnp.pad(with_sides, ((row_gap, row_gap), (0, 0), (0, 0)))
        response = convolve(padded, conv_weights[position], row_gap, col_gap, sub_rows, sub_cols)
        grouped = update(grouped, response, conv_biases[position])
    returned = lax.all_to_all(grouped, "row", split_axis=0, concat_axis=0, tiled=True)
    return (
        returned.reshape(tile_rows, class_count, sub_cols, channels)
        .transpose(0, 2, 1, 3)
        .reshape(tile_rows, tile_cols, channels)
    )


def vmem_spec():
    return pl.BlockSpec(memory_space=pltpu.VMEM)


def smem_spec():
    return pl.BlockSpec(memory_space=pltpu.SMEM)


def any_spec():
    return pl.BlockSpec(memory_space=pl.ANY)


def kernel_call(body, out_shape, in_specs, scratch, out_specs=None):
    return pl.pallas_call(
        body,
        out_shape=out_shape,
        in_specs=in_specs,
        out_specs=out_specs or jax.tree.map(lambda _: vmem_spec(), out_shape),
        scratch_shapes=scratch,
        compiler_params=pltpu.CompilerParams(vmem_limit_bytes=vmem_limit),
        cost_estimate=pl.CostEstimate(flops=1, bytes_accessed=1, transcendentals=0),
    )


def place(core, at_zero, at_one):
    return pl.multiple_of(jnp.where(core == 0, at_zero, at_one), lane_pad)


def row_of(flag_ref, row):
    return row if isinstance(row, int) else jnp.where(flag_ref[2] == 0, *row)


def guarded(flag_ref, condition, action):
    if condition is None:
        action()
    else:
        number, value = condition
        pl.when(flag_ref[number] == value)(action)


def copy_kernel(moves, inputs, flag_ref, *refs):
    sources, targets = refs[:inputs], refs[inputs:]

    def move(which, row, count, column, width, target, target_row):
        src = place(flag_ref[0], *column)
        first = row_of(flag_ref, target_row)
        for r in range(count):
            targets[target][first + r] = sources[which][row + r, pl.ds(src, width), :]

    for parts in moves:
        guarded(flag_ref, parts[0], functools.partial(move, *parts[1:]))


def copies(flags, arrays, moves):
    channels, kind = arrays[0].shape[2], arrays[0].dtype
    shapes = {}
    for _, _, _, count, _, width, target, target_row in moves:
        end = count + (target_row if isinstance(target_row, int) else max(target_row))
        height = max(end, shapes.get(target, (0, 0))[0])
        shapes[target] = (height, width)
    out = tuple(
        jax.ShapeDtypeStruct(shapes[target] + (channels,), kind) for target in range(len(shapes))
    )
    return kernel_call(
        functools.partial(copy_kernel, moves, len(arrays)),
        out,
        [smem_spec()] + [vmem_spec()] * len(arrays),
        [],
    )(flags, *arrays)


def hold_kernel(flag_ref, w_ref, first_ref, second_ref, last_ref):
    first_ref[...] = w_ref[0]
    second_ref[0] = w_ref[1, 1]
    second_ref[1] = w_ref[1, flag_ref[1]]
    last_ref[...] = w_ref[2, 1]


def first_layer_kernel(segments, out_at, rows, width, flag_ref, scale_ref, w_ref, *rest):
    parts, (next_ref, normed_ref, window, taps) = rest[:-4], rest[-4:]
    core = flag_ref[0]
    half = rows // 2
    channels = window.shape[2]
    gain = scale_ref[0:1, :]

    def fill(which, source_row, window_row, count, source, target, columns):
        src, dst = place(core, *source), place(core, *target)
        first = row_of(flag_ref, window_row)
        for r in range(count):
            if which is None:
                values = jnp.zeros((columns, channels), window.dtype)
            else:
                values = normalize(
                    parts[which][source_row + r, pl.ds(src, columns), :], gain
                )
            window[first + r, pl.ds(dst, columns), :] = values

    for segment in segments:
        guarded(flag_ref, segment[0], functools.partial(fill, *segment[1:]))
    step = dilations[0]
    for b in range(3):
        first = lane_pad + (b - 1) * step
        for r in range(2 * rows):
            taps[b, r] = window[r, first : first + width, :]
    stacked = jnp.concatenate(
        [
            taps[b, a * half : a * half + rows].reshape(rows * width, channels)
            for a in range(3)
            for b in range(3)
        ],
        axis=1,
    )
    response = jnp.dot(
        stacked, w_ref[...].reshape(9 * channels, channels), preferred_element_type=jnp.float32
    )
    out_col = place(core, *out_at)
    current = parts[0][:, pl.ds(out_col, width), :].reshape(rows * width, channels)
    result = update(current, response, scale_ref[3:4, :])
    next_ref[...] = result.reshape(rows, width, channels)
    normed_ref[...] = normalize(result, scale_ref[1:2, :]).reshape(rows, width, channels)


def first_layer(flags, params, parts, segments, out_at, width):
    rows, _, channels = parts[0].shape
    kind = parts[0].dtype
    out = jax.ShapeDtypeStruct((rows, width, channels), kind)
    return kernel_call(
        functools.partial(first_layer_kernel, segments, out_at, rows, width),
        (out, out),
        [smem_spec()] + [vmem_spec()] * (2 + len(parts)),
        [
            pltpu.VMEM((2 * rows, width + 2 * lane_pad, channels), kind),
            pltpu.VMEM((3, 2 * rows, width, channels), kind),
        ],
    )(flags, *params, *parts)


def partial_kernel(
    flag_ref, scale_ref, w_ref, near_ref, mid_ref, far_ref, cfar_ref, side_ref, near1_ref, mid1_ref,
    far1_ref, acc_ref, next_ref, far2_ref, farn_ref, own, other,
):
    core = flag_ref[0]
    step = dilations[1]
    rows, near, channels = near_ref.shape
    mid, far = mid_ref.shape[1], far_ref.shape[1]
    cols = near + mid + far
    other[...] = jnp.zeros(other.shape, other.dtype)
    pieces = (
        (near_ref, near1_ref, (cols - near, 0)),
        (mid_ref, mid1_ref, (far, near)),
        (far_ref, far1_ref, (0, cols - far)),
    )
    for normed, current, at in pieces:
        width = normed.shape[1]
        next_ref[:, pl.ds(place(core, *at), width), :] = current[...]
        inside = pl.ds(place(core, at[0] + step, at[1] + step), width)
        own[:, inside, :] = normed[...]
        if normed is far_ref:
            other[:, inside, :] = cfar_ref[...]
    own[:, pl.ds(place(core, step + cols, 0), step), :] = side_ref[...]
    own[:, pl.ds(place(core, 0, step + cols), step), :] = jnp.zeros(
        (rows, step, channels), own.dtype
    )
    stacked = jnp.concatenate(
        [
            ref[:, b * step : b * step + cols, :].reshape(rows * cols, channels)
            for ref in (own, other)
            for b in range(3)
        ],
        axis=1,
    )
    acc_ref[...] = jnp.dot(
        stacked, w_ref[...].reshape(6 * channels, channels), preferred_element_type=jnp.float32
    ).reshape(rows, cols, channels)
    edge = pl.ds(place(core, 0, cols - far2_ref.shape[1]), far2_ref.shape[1])
    far2_ref[...], farn_ref[...] = after_second(
        scale_ref, acc_ref[:, edge, :], next_ref[:, edge, :]
    )


def second_layer(flag_ref, scale_ref, w_ref, window, acc, current):
    step = dilations[1]
    rows, width, channels = current.shape
    cells = rows * width
    stacked = jnp.concatenate(
        [window[:, b * step : b * step + width, :].reshape(cells, channels) for b in range(3)],
        axis=1,
    )
    response = acc.reshape(cells, channels) + jnp.dot(
        stacked,
        w_ref[1].reshape(3 * channels, channels),
        preferred_element_type=jnp.float32,
    )
    return after_second(scale_ref, response, current)


def after_second(scale_ref, response, current):
    cells, channels = current.shape[0] * current.shape[1], current.shape[2]
    result = update(
        current.reshape(cells, channels), response.reshape(cells, channels), scale_ref[4:5, :]
    )
    normed = normalize(result, scale_ref[2:3, :])
    return result.reshape(current.shape), normed.reshape(current.shape)


def near_kernel(
    flag_ref, scale_ref, w_ref, cnear_ref, rim_ref, side_ref, acc_ref, x1_ref, next_ref, normed_ref,
    window,
):
    core = flag_ref[0]
    step, reach = dilations[1], dilations[2]
    near, cols = cnear_ref.shape[1], x1_ref.shape[1]
    window[:, pl.ds(place(core, 0, 2 * step), near), :] = cnear_ref[...]
    window[:, pl.ds(place(core, near, step), step), :] = rim_ref[...]
    window[:, pl.ds(place(core, near + step, 0), step), :] = side_ref[...]
    at = pl.ds(place(core, cols - reach, 0), reach)
    next_ref[...], normed_ref[...] = second_layer(
        flag_ref, scale_ref, w_ref, window[...], acc_ref[:, at, :], x1_ref[:, at, :]
    )


def mid_kernel(
    flag_ref, scale_ref, w_ref, cmid_ref, cnear_ref, acc_ref, x1_ref, next_ref, normed_ref, window
):
    core = flag_ref[0]
    step, reach = dilations[1], dilations[2]
    rows, mid, channels = cmid_ref.shape
    near, width = cnear_ref.shape[1], next_ref.shape[1]
    blank = width + 2 * step - near - mid
    window[:, pl.ds(place(core, blank + mid, 0), near), :] = cnear_ref[...]
    window[:, pl.ds(place(core, blank, near), mid), :] = cmid_ref[...]
    window[:, pl.ds(place(core, 0, near + mid), blank), :] = jnp.zeros(
        (rows, blank, channels), window.dtype
    )
    at = pl.ds(place(core, x1_ref.shape[1] - reach - width, reach), width)
    next_ref[...], normed_ref[...] = second_layer(
        flag_ref, scale_ref, w_ref, window[...], acc_ref[:, at, :], x1_ref[:, at, :]
    )


def sides_kernel(
    flag_ref, scale_ref, w_ref, near2_ref, far2_ref, near_ref, far_ref, acc_ref, ends_ref, normed
):
    core = flag_ref[0]
    rows, reach, channels = near_ref.shape
    ends_ref[core], ends_ref[1 - core] = far2_ref[...], near2_ref[...]
    normed[core], normed[1 - core] = far_ref[...], near_ref[...]
    for block, (end, tap) in enumerate(((0, 1), (0, 0), (1, 2), (1, 1))):
        acc_ref[:, block * reach : (block + 1) * reach, :] = jnp.dot(
            normed[end].reshape(rows * reach, channels),
            w_ref[tap],
            preferred_element_type=jnp.float32,
        ).reshape(rows, reach, channels)


def last_kernel(
    flag_ref, scale_ref, w_ref, ends_ref, mid2_ref, mid_ref, side_ref, acc_ref, out_ref, result, sems
):
    core = flag_ref[0]
    rows, reach, channels = side_ref.shape
    group = 2
    leaving = []
    for first in range(0, rows, group):
        some = slice(first, first + group)
        cells = group * reach
        side = side_ref[some].reshape(cells, channels)
        nothing = jnp.zeros_like(side)
        inner = [
            mid_ref[some, at * reach : (at + 1) * reach, :].reshape(cells, channels)
            for at in range(2)
        ]
        blocks = (
            (inner[0], 2, jnp.where(core == 1, side, nothing), 0, ends_ref[0, some]),
            (inner[0], 1, inner[1], 2, mid2_ref[some, 0:reach, :]),
            (inner[0], 0, inner[1], 1, mid2_ref[some, reach : 2 * reach, :]),
            (inner[1], 0, jnp.where(core == 0, side, nothing), 2, ends_ref[1, some]),
        )
        for block, (one, tap, two, other_tap, current) in enumerate(blocks):
            at = slice(block * reach, (block + 1) * reach)
            response = acc_ref[some, at, :].reshape(cells, channels) + jnp.dot(
                jnp.concatenate([one, two], axis=1),
                jnp.concatenate([w_ref[tap], w_ref[other_tap]], axis=0),
                preferred_element_type=jnp.float32,
            )
            result[some, at, :] = update(
                current.reshape(cells, channels), response, scale_ref[5:6, :]
            ).reshape(group, reach, channels)
        leaving.append(
            pltpu.make_async_copy(result.at[some], out_ref.at[some], sems.at[first // group])
        )
        leaving[-1].start()
    for copy in leaving:
        copy.wait()


def by_halves(context_map, norm_gains, conv_biases, conv_weights):
    rows, cols, channels = context_map.shape
    kind = context_map.dtype
    size = lax.axis_size("row")
    group = size // 2
    half = rows // 2
    step, reach = dilations[1], dilations[2]
    strip = step + reach
    mid = cols - 2 * strip
    pad = lane_pad
    wide = strip + pad
    core, row = lax.axis_index("col"), lax.axis_index("row")
    upper_half = row < group
    flags = jnp.stack([core, jnp.where(upper_half, 2, 0), row % 2]).astype(jnp.int32)
    even, odd = (2, 0), (2, 1)
    one_at, two_at = (half + rows, 0), (0, half + rows)
    swap = [(0, 1), (1, 0)]
    partner = [(i, (i + group) % size) for i in range(size)]
    first_pairs = [(i, i ^ 1) for i in range(size)]
    second_pairs = [(i, ((i + 1) ^ 1) - 1) for i in range(1, size - 1)]

    far_wide_at, near_wide_at = (0, cols - wide), (cols - wide, 0)
    span, span_at = cols - wide, (wide, 0)
    parts = (
        (None, 0, 0, rows, far_wide_at, wide, 0, 0),
        (None, 0, 0, rows, near_wide_at, wide, 1, 0),
        (None, 0, 0, rows, (strip - pad, strip - pad), mid + 2 * pad, 2, 0),
        (even, 0, half, half, far_wide_at, wide, 3, 0),
        (odd, 0, 0, half, far_wide_at, wide, 3, 0),
        (even, 0, 0, half, far_wide_at, wide, 4, 0),
        (odd, 0, half, half, far_wide_at, wide, 4, 0),
        (even, 0, half, half, span_at, span, 5, 0),
        (odd, 0, 0, half, span_at, span, 5, 0),
        (even, 0, 0, half, span_at, span, 6, 0),
        (odd, 0, half, half, span_at, span, 6, 0),
    )
    (
        far_x, near_x, mid_x, far_one, far_two, one, two
    ) = copies(flags, (context_map,), parts)
    far_one = lax.ppermute(far_one, "row", first_pairs)
    far_two = lax.ppermute(far_two, "row", second_pairs)
    tail = conv_weights.shape[2:]
    scales = jnp.concatenate([norm_gains, conv_biases], axis=0)
    first_w, second_w, last_w = kernel_call(
        hold_kernel,
        (
            jax.ShapeDtypeStruct((3,) + tail, kind),
            jax.ShapeDtypeStruct((2,) + tail, kind),
            jax.ShapeDtypeStruct(tail, kind),
        ),
        [smem_spec(), vmem_spec()],
        [],
    )(flags, conv_weights)
    one, two, first_w = lax.optimization_barrier((one, two, first_w))
    one = lax.ppermute(one, "row", first_pairs)
    two = lax.ppermute(two, "row", second_pairs)

    params = (scales, first_w)
    far_body, far_edge = (pad, 0), (0, wide)
    far_segments = (
        (None, 0, 0, half, rows, (0, 0), far_body, wide),
        (None, 1, 0, one_at, half, (0, 0), far_body, wide),
        (None, 2, 0, two_at, half, (0, 0), far_body, wide),
        (None, None, 0, 0, 2 * rows, (0, 0), far_edge, pad),
    )
    far1, far_n = first_layer(
        flags, params, (far_x, far_one, far_two), far_segments, (0, pad), strip
    )
    cross_far = lax.ppermute(far_n, "row", partner)

    near_end, span_end = (wide - pad, 0), (span - pad, 0)
    (rim,) = copies(
        flags,
        (near_x, one, two),
        (
            (None, 1, 0, half, span_end, pad, 0, one_at),
            (None, 2, 0, half, span_end, pad, 0, two_at),
            (None, 0, 0, rows, near_end, pad, 0, half),
        ),
    )
    rim = lax.ppermute(rim, "col", swap)
    near_body, near_span = (0, pad), (span - wide, 0)
    near_segments = (
        (None, 0, 0, half, rows, (0, 0), near_body, wide),
        (None, 1, 0, one_at, half, near_span, near_body, wide),
        (None, 2, 0, two_at, half, near_span, near_body, wide),
        (None, 3, 0, 0, 2 * rows, (0, 0), (wide, 0), pad),
    )
    near1, near_n = first_layer(
        flags, params, (near_x, one, two, rim), near_segments, (pad, 0), strip
    )
    near_rim, near_rest = copies(
        flags,
        (near_n,),
        (
            (None, 0, 0, rows, (strip - step, 0), step, 0, 0),
            (None, 0, 0, rows, (0, step), strip - step, 1, 0),
        ),
    )
    cross_rim = lax.ppermute(near_rim, "row", partner)
    cross_near = lax.ppermute(near_rest, "row", partner)
    side_pads = 2 * pad
    far_side, rest_side = ((wide - side_pads, 0), (0, mid)), ((0, span - mid), (side_pads, 0))
    mid_segments = (
        (None, 0, 0, half, rows, (0, 0), (0, 0), mid + side_pads),
        (None, 1, 0, one_at, half, *far_side, side_pads),
        (None, 2, 0, two_at, half, *far_side, side_pads),
        (None, 3, 0, one_at, half, *rest_side, mid),
        (None, 4, 0, two_at, half, *rest_side, mid),
    )
    mid1, mid_n = first_layer(
        flags,
        params,
        (
            mid_x, far_one, far_two, one, two
        ),
        mid_segments,
        (pad, pad),
        mid,
    )
    cross_mid = lax.ppermute(mid_n, "row", partner)

    near_rim, cross_far = lax.optimization_barrier((near_rim, cross_far))
    near_side = lax.ppermute(near_rim, "col", swap)
    def plain(body, weights, out, operands, scratch, more=()):
        return kernel_call(
            body,
            out,
            [smem_spec()] + [vmem_spec()] * (len(operands) + 2),
            [pltpu.VMEM((rows, width, channels), kind) for width in scratch] + list(more),
        )(flags, scales, weights, *operands)

    def strip_shape(width, kind=kind):
        return jax.ShapeDtypeStruct((rows, width, channels), kind)

    acc, x1, far2, far_n = plain(
        partial_kernel,
        second_w,
        (
            strip_shape(cols, jnp.float32),
            strip_shape(cols),
            strip_shape(strip - step),
            strip_shape(strip - step),
        ),
        (near_n, mid_n, far_n, cross_far, near_side, near1, mid1, far1),
        (cols + 2 * step, cols + 2 * step),
    )
    cross_side = lax.ppermute(cross_rim, "col", swap)
    near2, near_n = plain(
        near_kernel,
        second_w,
        (strip_shape(reach), strip_shape(reach)),
        (cross_near, cross_rim, cross_side, acc, x1),
        (reach + 2 * step,),
    )
    sums, ends = plain(
        sides_kernel,
        last_w,
        (
            strip_shape(cols, jnp.float32),
            jax.ShapeDtypeStruct((2, rows, reach, channels), kind),
        ),
        (near2, far2, near_n, far_n),
        (),
        [pltpu.VMEM((2, rows, reach, channels), kind)],
    )
    near_n, cross_mid, sums = lax.optimization_barrier((near_n, cross_mid, sums))
    last_side = lax.ppermute(near_n, "col", swap)
    mid2, mid_n = plain(
        mid_kernel,
        second_w,
        (strip_shape(2 * reach), strip_shape(2 * reach)),
        (cross_mid, cross_near, acc, x1),
        (2 * reach + 2 * step,),
    )
    return kernel_call(
        last_kernel,
        strip_shape(cols),
        [smem_spec()] + [vmem_spec()] * 7,
        [
            pltpu.VMEM((rows, cols, channels), kind),
            pltpu.SemaphoreType.DMA((rows,)),
        ],
        any_spec(),
    )(flags, scales, last_w, ends, mid2, mid_n, last_side, sums)


def shards(context_map, *params):
    rows, cols, _ = context_map.shape
    map_rows = lax.axis_size("row") * rows
    strip = dilations[1] + dilations[2]
    if (
        map_rows == 2 * dilations[1]
        and map_rows <= dilations[2]
        and rows == 2 * dilations[0]
        and dilations[1] % rows == 0
        and lax.axis_size("col") == 2
        and cols == 4 * dilations[2]
        and dilations[2] == 2 * dilations[1]
    ):
        return by_halves(context_map, *params)
    return by_classes(context_map, *params)


def solution(mesh):
    return jax.shard_map(
        shards,
        mesh=mesh,
        in_specs=(P(("ctx", "row"), "col", None), P(), P(), P()),
        out_specs=P(("ctx", "row"), "col", None),
        check_vma=False,
    )
```

```python
import functools

import jax
import jax.numpy as jnp
from jax import lax
from jax.experimental import pallas as pl
from jax.experimental.pallas import tpu as pltpu
from jax.sharding import PartitionSpec as P

epsilon = 1e-05
dilations = (4, 32, 64)
lane_pad = 16
vmem_limit = 40 * 1024 * 1024


def extended(x, sides, width):
    for axis, dim in sides:
        size, length = (lax.axis_size(axis), x.shape[dim])
        up = [(i, (i + 1) % size) for i in range(size - 1)]
        down = [(j, i) for i, j in up]
        last = lax.slice_in_dim(x, length - width, length, axis=dim)
        first = lax.slice_in_dim(x, 0, width, axis=dim)
        before = lax.ppermute(last, axis, up)
        after = lax.ppermute(first, axis, down)
        x = jnp.concatenate([before, x, after], axis=dim)
    return x


def normalize(current, gain_row):
    values = current.astype(jnp.float32)
    centred = values - jnp.mean(values, axis=-1, keepdims=True)
    variance = jnp.mean(centred * centred, axis=-1, keepdims=True)
    return (centred * lax.rsqrt(variance + epsilon) * gain_row).astype(jnp.bfloat16)


def convolve(padded, kernel, row_step, col_step, out_rows, out_cols):
    channels = padded.shape[2]
    tap_list = []
    for tap_row in range(3):
        for tap_col in range(3):
            tap_list.append(
                lax.slice(
                    padded,
                    (tap_row * row_step, tap_col * col_step, 0),
                    (tap_row * row_step + out_rows, tap_col * col_step + out_cols, channels),
                )
            )
    stacked = jnp.concatenate(tap_list, axis=2).reshape(out_rows * out_cols, 9 * channels)
    product = jnp.dot(
        stacked, kernel.reshape(9 * channels, kernel.shape[3]), preferred_element_type=jnp.float32
    )
    return product.reshape(out_rows, out_cols, kernel.shape[3])


def update(current, response, bias_row):
    return (current.astype(jnp.float32) + jnp.maximum(response + bias_row, 0.0)).astype(
        jnp.bfloat16
    )


def by_classes(context_map, norm_gains, conv_biases, conv_weights):
    tile_rows, tile_cols, channels = context_map.shape
    normed = normalize(context_map, norm_gains[0])
    padded = extended(normed, (("row", 0), ("col", 1)), 4)
    current = update(
        context_map, convolve(padded, conv_weights[0], 4, 4, tile_rows, tile_cols), conv_biases[0]
    )
    class_count = lax.axis_size("row") // tile_rows
    sub_cols = tile_cols // class_count
    outgoing = (
        current.reshape(tile_rows, sub_cols, class_count, channels)
        .transpose(0, 2, 1, 3)
        .reshape(tile_rows * class_count, sub_cols, channels)
    )
    grouped = lax.all_to_all(outgoing, "row", split_axis=0, concat_axis=0, tiled=True)
    sub_rows = grouped.shape[0]
    for position, dilation in ((1, 32), (2, 64)):
        normed = normalize(grouped, norm_gains[position])
        row_gap = dilation // tile_rows
        col_gap = dilation // class_count
        with_sides = extended(normed, (("col", 1),), col_gap)
        padded = jnp.pad(with_sides, ((row_gap, row_gap), (0, 0), (0, 0)))
        response = convolve(padded, conv_weights[position], row_gap, col_gap, sub_rows, sub_cols)
        grouped = update(grouped, response, conv_biases[position])
    returned = lax.all_to_all(grouped, "row", split_axis=0, concat_axis=0, tiled=True)
    return (
        returned.reshape(tile_rows, class_count, sub_cols, channels)
        .transpose(0, 2, 1, 3)
        .reshape(tile_rows, tile_cols, channels)
    )


def vmem_spec():
    return pl.BlockSpec(memory_space=pltpu.VMEM)


def smem_spec():
    return pl.BlockSpec(memory_space=pltpu.SMEM)


def any_spec():
    return pl.BlockSpec(memory_space=pl.ANY)


def kernel_call(body, out_shape, in_specs, scratch, out_specs=None):
    return pl.pallas_call(
        body,
        out_shape=out_shape,
        in_specs=in_specs,
        out_specs=out_specs or jax.tree.map(lambda _: vmem_spec(), out_shape),
        scratch_shapes=scratch,
        compiler_params=pltpu.CompilerParams(vmem_limit_bytes=vmem_limit),
        cost_estimate=pl.CostEstimate(flops=1, bytes_accessed=1, transcendentals=0),
    )


def place(core, at_zero, at_one):
    return pl.multiple_of(jnp.where(core == 0, at_zero, at_one), lane_pad)


def row_of(flag_ref, row):
    return row if isinstance(row, int) else jnp.where(flag_ref[2] == 0, *row)


def guarded(flag_ref, condition, action):
    if condition is None:
        action()
    else:
        number, value = condition
        pl.when(flag_ref[number] == value)(action)


def copy_kernel(moves, inputs, flag_ref, *refs):
    sources, targets = refs[:inputs], refs[inputs:]

    def move(which, row, count, column, width, target, target_row):
        src = place(flag_ref[0], *column)
        first = row_of(flag_ref, target_row)
        for r in range(count):
            targets[target][first + r] = sources[which][row + r, pl.ds(src, width), :]

    for parts in moves:
        guarded(flag_ref, parts[0], functools.partial(move, *parts[1:]))


def copies(flags, arrays, moves):
    channels, kind = arrays[0].shape[2], arrays[0].dtype
    shapes = {}
    for _, _, _, count, _, width, target, target_row in moves:
        end = count + (target_row if isinstance(target_row, int) else max(target_row))
        height = max(end, shapes.get(target, (0, 0))[0])
        shapes[target] = (height, width)
    out = tuple(
        jax.ShapeDtypeStruct(shapes[target] + (channels,), kind) for target in range(len(shapes))
    )
    return kernel_call(
        functools.partial(copy_kernel, moves, len(arrays)),
        out,
        [smem_spec()] + [vmem_spec()] * len(arrays),
        [],
    )(flags, *arrays)


def hold_kernel(flag_ref, w_ref, first_ref, second_ref, last_ref):
    first_ref[...] = w_ref[0]
    second_ref[0] = w_ref[1, 1]
    second_ref[1] = w_ref[1, flag_ref[1]]
    last_ref[...] = w_ref[2, 1]


def first_layer_kernel(
    segments, out_at, cuts, rows, width, count, flag_ref, scale_ref, w_ref, *rest
):
    parts, (next_ref, normed_ref), (window, taps) = rest[:count], rest[count : count + 2], rest[-2:]
    cut_refs = rest[count + 2 : -2]
    core = flag_ref[0]
    half = rows // 2
    channels = window.shape[2]
    gain = scale_ref[0:1, :]

    def fill(which, source_row, window_row, count, source, target, columns):
        src, dst = place(core, *source), place(core, *target)
        first = row_of(flag_ref, window_row)
        for r in range(count):
            if which is None:
                values = jnp.zeros((columns, channels), window.dtype)
            else:
                values = normalize(
                    parts[which][source_row + r, pl.ds(src, columns), :], gain
                )
            window[first + r, pl.ds(dst, columns), :] = values

    for segment in segments:
        guarded(flag_ref, segment[0], functools.partial(fill, *segment[1:]))
    step = dilations[0]
    for b in range(3):
        first = lane_pad + (b - 1) * step
        for r in range(2 * rows):
            taps[b, r] = window[r, first : first + width, :]
    stacked = jnp.concatenate(
        [
            taps[b, a * half : a * half + rows].reshape(rows * width, channels)
            for a in range(3)
            for b in range(3)
        ],
        axis=1,
    )
    response = jnp.dot(
        stacked, w_ref[...].reshape(9 * channels, channels), preferred_element_type=jnp.float32
    )
    out_col = place(core, *out_at)
    current = parts[0][:, pl.ds(out_col, width), :].reshape(rows * width, channels)
    result = update(current, response, scale_ref[3:4, :])
    next_ref[...] = result.reshape(rows, width, channels)
    normed_ref[...] = normalize(result, scale_ref[1:2, :]).reshape(rows, width, channels)
    for cut_ref, (at, columns) in zip(cut_refs, cuts):
        cut_ref[...] = normed_ref[:, pl.ds(place(core, *at), columns), :]


def first_layer(flags, params, parts, segments, out_at, width, cuts=()):
    rows, _, channels = parts[0].shape
    kind = parts[0].dtype
    return kernel_call(
        functools.partial(first_layer_kernel, segments, out_at, cuts, rows, width, len(parts)),
        tuple(
            jax.ShapeDtypeStruct((rows, columns, channels), kind)
            for columns in (width, width) + tuple(columns for _, columns in cuts)
        ),
        [smem_spec()] + [vmem_spec()] * (2 + len(parts)),
        [
            pltpu.VMEM((2 * rows, width + 2 * lane_pad, channels), kind),
            pltpu.VMEM((3, 2 * rows, width, channels), kind),
        ],
    )(flags, *params, *parts)


def partial_kernel(
    flag_ref, scale_ref, w_ref, near_ref, mid_ref, far_ref, cfar_ref, side_ref, near1_ref, mid1_ref,
    far1_ref, acc_ref, next_ref, far2_ref, farn_ref, own, other,
):
    core = flag_ref[0]
    step = dilations[1]
    rows, near, channels = near_ref.shape
    mid, far = mid_ref.shape[1], far_ref.shape[1]
    cols = near + mid + far
    other[...] = jnp.zeros(other.shape, other.dtype)
    pieces = (
        (near_ref, near1_ref, (cols - near, 0)),
        (mid_ref, mid1_ref, (far, near)),
        (far_ref, far1_ref, (0, cols - far)),
    )
    for normed, current, at in pieces:
        width = normed.shape[1]
        next_ref[:, pl.ds(place(core, *at), width), :] = current[...]
        inside = pl.ds(place(core, at[0] + step, at[1] + step), width)
        own[:, inside, :] = normed[...]
        if normed is far_ref:
            other[:, inside, :] = cfar_ref[...]
    own[:, pl.ds(place(core, step + cols, 0), step), :] = side_ref[...]
    own[:, pl.ds(place(core, 0, step + cols), step), :] = jnp.zeros(
        (rows, step, channels), own.dtype
    )
    stacked = jnp.concatenate(
        [
            ref[:, b * step : b * step + cols, :].reshape(rows * cols, channels)
            for ref in (own, other)
            for b in range(3)
        ],
        axis=1,
    )
    acc_ref[...] = jnp.dot(
        stacked, w_ref[...].reshape(6 * channels, channels), preferred_element_type=jnp.float32
    ).reshape(rows, cols, channels)
    edge = pl.ds(place(core, 0, cols - far2_ref.shape[1]), far2_ref.shape[1])
    far2_ref[...], farn_ref[...] = after_second(
        scale_ref, acc_ref[:, edge, :], next_ref[:, edge, :]
    )


def second_layer(flag_ref, scale_ref, w_ref, window, acc, current):
    step = dilations[1]
    rows, width, channels = current.shape
    cells = rows * width
    stacked = jnp.concatenate(
        [window[:, b * step : b * step + width, :].reshape(cells, channels) for b in range(3)],
        axis=1,
    )
    response = acc.reshape(cells, channels) + jnp.dot(
        stacked,
        w_ref[1].reshape(3 * channels, channels),
        preferred_element_type=jnp.float32,
    )
    return after_second(scale_ref, response, current)


def after_second(scale_ref, response, current):
    cells, channels = current.shape[0] * current.shape[1], current.shape[2]
    result = update(
        current.reshape(cells, channels), response.reshape(cells, channels), scale_ref[4:5, :]
    )
    normed = normalize(result, scale_ref[2:3, :])
    return result.reshape(current.shape), normed.reshape(current.shape)


def near_kernel(
    flag_ref, scale_ref, w_ref, cnear_ref, rim_ref, side_ref, acc_ref, x1_ref, next_ref, normed_ref,
    window,
):
    core = flag_ref[0]
    step, reach = dilations[1], dilations[2]
    near, cols = cnear_ref.shape[1], x1_ref.shape[1]
    window[:, pl.ds(place(core, 0, 2 * step), near), :] = cnear_ref[...]
    window[:, pl.ds(place(core, near, step), step), :] = rim_ref[...]
    window[:, pl.ds(place(core, near + step, 0), step), :] = side_ref[...]
    at = pl.ds(place(core, cols - reach, 0), reach)
    next_ref[...], normed_ref[...] = second_layer(
        flag_ref, scale_ref, w_ref, window[...], acc_ref[:, at, :], x1_ref[:, at, :]
    )


def mid_kernel(
    flag_ref, scale_ref, w_ref, cmid_ref, cnear_ref, acc_ref, x1_ref, next_ref, normed_ref, window
):
    core = flag_ref[0]
    step, reach = dilations[1], dilations[2]
    rows, mid, channels = cmid_ref.shape
    near, width = cnear_ref.shape[1], next_ref.shape[1]
    blank = width + 2 * step - near - mid
    window[:, pl.ds(place(core, blank + mid, 0), near), :] = cnear_ref[...]
    window[:, pl.ds(place(core, blank, near), mid), :] = cmid_ref[...]
    window[:, pl.ds(place(core, 0, near + mid), blank), :] = jnp.zeros(
        (rows, blank, channels), window.dtype
    )
    at = pl.ds(place(core, x1_ref.shape[1] - reach - width, reach), width)
    next_ref[...], normed_ref[...] = second_layer(
        flag_ref, scale_ref, w_ref, window[...], acc_ref[:, at, :], x1_ref[:, at, :]
    )


def sides_kernel(
    flag_ref, scale_ref, w_ref, near2_ref, far2_ref, near_ref, far_ref, acc_ref, ends_ref, normed
):
    core = flag_ref[0]
    rows, reach, channels = near_ref.shape
    ends_ref[core], ends_ref[1 - core] = far2_ref[...], near2_ref[...]
    normed[core], normed[1 - core] = far_ref[...], near_ref[...]
    for block, (end, tap) in enumerate(((0, 1), (0, 0), (1, 2), (1, 1))):
        acc_ref[:, block * reach : (block + 1) * reach, :] = jnp.dot(
            normed[end].reshape(rows * reach, channels),
            w_ref[tap],
            preferred_element_type=jnp.float32,
        ).reshape(rows, reach, channels)


def last_kernel(
    flag_ref, scale_ref, w_ref, ends_ref, mid2_ref, mid_ref, side_ref, acc_ref, out_ref, result, sems
):
    core = flag_ref[0]
    rows, reach, channels = side_ref.shape
    group = 2
    leaving = []
    for first in range(0, rows, group):
        some = slice(first, first + group)
        cells = group * reach
        side = side_ref[some].reshape(cells, channels)
        nothing = jnp.zeros_like(side)
        inner = [
            mid_ref[some, at * reach : (at + 1) * reach, :].reshape(cells, channels)
            for at in range(2)
        ]
        blocks = (
            (inner[0], 2, jnp.where(core == 1, side, nothing), 0, ends_ref[0, some]),
            (inner[0], 1, inner[1], 2, mid2_ref[some, 0:reach, :]),
            (inner[0], 0, inner[1], 1, mid2_ref[some, reach : 2 * reach, :]),
            (inner[1], 0, jnp.where(core == 0, side, nothing), 2, ends_ref[1, some]),
        )
        for block, (one, tap, two, other_tap, current) in enumerate(blocks):
            at = slice(block * reach, (block + 1) * reach)
            response = acc_ref[some, at, :].reshape(cells, channels) + jnp.dot(
                jnp.concatenate([one, two], axis=1),
                jnp.concatenate([w_ref[tap], w_ref[other_tap]], axis=0),
                preferred_element_type=jnp.float32,
            )
            result[some, at, :] = update(
                current.reshape(cells, channels), response, scale_ref[5:6, :]
            ).reshape(group, reach, channels)
        leaving.append(
            pltpu.make_async_copy(result.at[some], out_ref.at[some], sems.at[first // group])
        )
        leaving[-1].start()
    for copy in leaving:
        copy.wait()


def by_halves(context_map, norm_gains, conv_biases, conv_weights):
    rows, cols, channels = context_map.shape
    kind = context_map.dtype
    size = lax.axis_size("row")
    group = size // 2
    half = rows // 2
    step, reach = dilations[1], dilations[2]
    strip = step + reach
    mid = cols - 2 * strip
    pad = lane_pad
    wide = strip + pad
    core, row = lax.axis_index("col"), lax.axis_index("row")
    upper_half = row < group
    flags = jnp.stack([core, jnp.where(upper_half, 2, 0), row % 2]).astype(jnp.int32)
    even, odd = (2, 0), (2, 1)
    one_at, two_at = (half + rows, 0), (0, half + rows)
    swap = [(0, 1), (1, 0)]
    partner = [(i, (i + group) % size) for i in range(size)]
    first_pairs = [(i, i ^ 1) for i in range(size)]
    second_pairs = [(i, ((i + 1) ^ 1) - 1) for i in range(1, size - 1)]

    far_wide_at, near_wide_at = (0, cols - wide), (cols - wide, 0)
    span, span_at = cols - wide, (wide, 0)
    parts = (
        (None, 0, 0, rows, far_wide_at, wide, 0, 0),
        (None, 0, 0, rows, near_wide_at, wide, 1, 0),
        (None, 0, 0, rows, (strip - pad, strip - pad), mid + 2 * pad, 2, 0),
        (even, 0, half, half, far_wide_at, wide, 3, 0),
        (odd, 0, 0, half, far_wide_at, wide, 3, 0),
        (even, 0, 0, half, far_wide_at, wide, 4, 0),
        (odd, 0, half, half, far_wide_at, wide, 4, 0),
        (even, 0, half, half, span_at, span, 5, 0),
        (odd, 0, 0, half, span_at, span, 5, 0),
        (even, 0, 0, half, span_at, span, 6, 0),
        (odd, 0, half, half, span_at, span, 6, 0),
    )
    (
        far_x, near_x, mid_x, far_one, far_two, one, two
    ) = copies(flags, (context_map,), parts)
    far_one = lax.ppermute(far_one, "row", first_pairs)
    far_two = lax.ppermute(far_two, "row", second_pairs)
    tail = conv_weights.shape[2:]
    scales = jnp.concatenate([norm_gains, conv_biases], axis=0)
    first_w, second_w, last_w = kernel_call(
        hold_kernel,
        (
            jax.ShapeDtypeStruct((3,) + tail, kind),
            jax.ShapeDtypeStruct((2,) + tail, kind),
            jax.ShapeDtypeStruct(tail, kind),
        ),
        [smem_spec(), vmem_spec()],
        [],
    )(flags, conv_weights)
    one, two, first_w = lax.optimization_barrier((one, two, first_w))
    one = lax.ppermute(one, "row", first_pairs)
    two = lax.ppermute(two, "row", second_pairs)

    params = (scales, first_w)
    far_body, far_edge = (pad, 0), (0, wide)
    far_segments = (
        (None, 0, 0, half, rows, (0, 0), far_body, wide),
        (None, 1, 0, one_at, half, (0, 0), far_body, wide),
        (None, 2, 0, two_at, half, (0, 0), far_body, wide),
        (None, None, 0, 0, 2 * rows, (0, 0), far_edge, pad),
    )
    far1, far_n = first_layer(
        flags, params, (far_x, far_one, far_two), far_segments, (0, pad), strip
    )
    cross_far = lax.ppermute(far_n, "row", partner)

    near_end, span_end = (wide - pad, 0), (span - pad, 0)
    (rim,) = copies(
        flags,
        (near_x, one, two),
        (
            (None, 1, 0, half, span_end, pad, 0, one_at),
            (None, 2, 0, half, span_end, pad, 0, two_at),
            (None, 0, 0, rows, near_end, pad, 0, half),
        ),
    )
    rim = lax.ppermute(rim, "col", swap)
    near_body, near_span = (0, pad), (span - wide, 0)
    near_segments = (
        (None, 0, 0, half, rows, (0, 0), near_body, wide),
        (None, 1, 0, one_at, half, near_span, near_body, wide),
        (None, 2, 0, two_at, half, near_span, near_body, wide),
        (None, 3, 0, 0, 2 * rows, (0, 0), (wide, 0), pad),
    )
    near1, near_n, near_rim, near_rest = first_layer(
        flags,
        params,
        (near_x, one, two, rim),
        near_segments,
        (pad, 0),
        strip,
        (((strip - step, 0), step), ((0, step), strip - step)),
    )
    cross_rim = lax.ppermute(near_rim, "row", partner)
    cross_near = lax.ppermute(near_rest, "row", partner)
    side_pads = 2 * pad
    far_side, rest_side = ((wide - side_pads, 0), (0, mid)), ((0, span - mid), (side_pads, 0))
    mid_segments = (
        (None, 0, 0, half, rows, (0, 0), (0, 0), mid + side_pads),
        (None, 1, 0, one_at, half, *far_side, side_pads),
        (None, 2, 0, two_at, half, *far_side, side_pads),
        (None, 3, 0, one_at, half, *rest_side, mid),
        (None, 4, 0, two_at, half, *rest_side, mid),
    )
    mid1, mid_n = first_layer(
        flags,
        params,
        (
            mid_x, far_one, far_two, one, two
        ),
        mid_segments,
        (pad, pad),
        mid,
    )
    cross_mid = lax.ppermute(mid_n, "row", partner)

    near_rim, cross_far = lax.optimization_barrier((near_rim, cross_far))
    near_side = lax.ppermute(near_rim, "col", swap)
    def plain(body, weights, out, operands, scratch, more=()):
        return kernel_call(
            body,
            out,
            [smem_spec()] + [vmem_spec()] * (len(operands) + 2),
            [pltpu.VMEM((rows, width, channels), kind) for width in scratch] + list(more),
        )(flags, scales, weights, *operands)

    def strip_shape(width, kind=kind):
        return jax.ShapeDtypeStruct((rows, width, channels), kind)

    acc, x1, far2, far_n = plain(
        partial_kernel,
        second_w,
        (
            strip_shape(cols, jnp.float32),
            strip_shape(cols),
            strip_shape(strip - step),
            strip_shape(strip - step),
        ),
        (near_n, mid_n, far_n, cross_far, near_side, near1, mid1, far1),
        (cols + 2 * step, cols + 2 * step),
    )
    cross_side = lax.ppermute(cross_rim, "col", swap)
    near2, near_n = plain(
        near_kernel,
        second_w,
        (strip_shape(reach), strip_shape(reach)),
        (cross_near, cross_rim, cross_side, acc, x1),
        (reach + 2 * step,),
    )
    sums, ends = plain(
        sides_kernel,
        last_w,
        (
            strip_shape(cols, jnp.float32),
            jax.ShapeDtypeStruct((2, rows, reach, channels), kind),
        ),
        (near2, far2, near_n, far_n),
        (),
        [pltpu.VMEM((2, rows, reach, channels), kind)],
    )
    near_n, cross_mid, sums = lax.optimization_barrier((near_n, cross_mid, sums))
    last_side = lax.ppermute(near_n, "col", swap)
    mid2, mid_n = plain(
        mid_kernel,
        second_w,
        (strip_shape(2 * reach), strip_shape(2 * reach)),
        (cross_mid, cross_near, acc, x1),
        (2 * reach + 2 * step,),
    )
    return kernel_call(
        last_kernel,
        strip_shape(cols),
        [smem_spec()] + [vmem_spec()] * 7,
        [
            pltpu.VMEM((rows, cols, channels), kind),
            pltpu.SemaphoreType.DMA((rows,)),
        ],
        any_spec(),
    )(flags, scales, last_w, ends, mid2, mid_n, last_side, sums)


def shards(context_map, *params):
    rows, cols, _ = context_map.shape
    map_rows = lax.axis_size("row") * rows
    strip = dilations[1] + dilations[2]
    if (
        map_rows == 2 * dilations[1]
        and map_rows <= dilations[2]
        and rows == 2 * dilations[0]
        and dilations[1] % rows == 0
        and lax.axis_size("col") == 2
        and cols == 4 * dilations[2]
        and dilations[2] == 2 * dilations[1]
    ):
        return by_halves(context_map, *params)
    return by_classes(context_map, *params)


def solution(mesh):
    return jax.shard_map(
        shards,
        mesh=mesh,
        in_specs=(P(("ctx", "row"), "col", None), P(), P(), P()),
        out_specs=P(("ctx", "row"), "col", None),
        check_vma=False,
    )
```
